32 devices in a mesh: ctx: 2 (over y), fsdp: 16 (over z, x, core).
Axes of the slice: x: 2, y: 2, z: 4, core: 2. Of those that a mesh axis runs over, the one named last changes fastest.
Arguments:
- tokens: bfloat16 [2, 16, 1536, 1024], P(None, 'fsdp', 'ctx'), may hold values from -6 to 6
- encoded: bfloat16 [2, 16, 1024, 1024], P(None, 'fsdp', 'ctx'), may hold values from -6 to 6
- cotangent: bfloat16 [2, 16, 1536, 1024], P(None, 'fsdp', 'ctx'), may hold values from -6 to 6
- order: int32 [2, 16, 1536], P(None, 'fsdp'), may hold values from 0 to 1535, as said below
- target_lengths: int32 [2, 16, 4], P(None, 'fsdp'), may hold values from 1 to 1152, as said below
- source_lengths: int32 [2, 16, 4], P(None, 'fsdp'), may hold values from 1 to 512, 1024 in all within a row
- self_project: bfloat16 [1024, 3072], P('fsdp'), may hold values from -0.25 to 0.25
- self_output: bfloat16 [1024, 1024], P('fsdp'), may hold values from -0.75 to 0.75
- cross_query: bfloat16 [1024, 1024], P('fsdp'), may hold values from -0.25 to 0.25
- cross_source: bfloat16 [1024, 2048], P('fsdp'), may hold values from -0.25 to 0.25
- cross_output: bfloat16 [1024, 1024], P('fsdp'), may hold values from -0.75 to 0.75
- feed_in: bfloat16 [1024, 4096], P('fsdp'), may hold values from -0.1875 to 0.1875
- feed_out: bfloat16 [4096, 1024], P('fsdp'), may hold values from -0.09375 to 0.09375
- norm_gain: bfloat16 [3, 1024], P(None, 'fsdp'), may hold values from 0.5 to 1.5
- norm_bias: bfloat16 [3, 1024], P(None, 'fsdp'), may hold values from -2 to 2
Outputs:
- output: bfloat16 [2, 16, 1536, 1024], P(None, 'fsdp', 'ctx')
- grad_tokens: bfloat16 [2, 16, 1536, 1024], P(None, 'fsdp', 'ctx')
- grad_encoded: bfloat16 [2, 16, 1024, 1024], P(None, 'fsdp', 'ctx')
- grad_self_project: float32 [1024, 3072], P('fsdp')
- grad_self_output: float32 [1024, 1024], P('fsdp')
- grad_cross_query: float32 [1024, 1024], P('fsdp')
- grad_cross_source: float32 [1024, 2048], P('fsdp')
- grad_cross_output: float32 [1024, 1024], P('fsdp')
- grad_feed_in: float32 [1024, 4096], P('fsdp')
- grad_feed_out: float32 [4096, 1024], P('fsdp')
- grad_norm_gain: float32 [3, 1024], P(None, 'fsdp')
- grad_norm_bias: float32 [2, 1024], P(None, 'fsdp')
- grad_feed_norm_bias: float32 [1024], P('fsdp')
The draws below stay inside these ranges and needn't reach their ends.
Inputs may be any that keep to these rules, and one draw needn't show every extreme that they name: Within a pack the slots form blocks of 384 in a row; each pair of blocks 2i, 2i + 1 holds, in increasing order, the positions of one of the first 1536 / 768 position blocks and of one of the later ones; each position once. `target_lengths`: A pack's lengths sum to 1536; its first document has exactly 1152 positions. `source_lengths`: A pack's lengths sum to 1024; source document k belongs to target document k.
All inputs are finite; a program needn't handle non-finite values.
Results may differ from the reference program's by a relative error of at most 0.029.
Values may be sent and summed in bfloat16 or wider, within the bound.
No kernel may reach another device: no remote copies, remote signals or barrier semaphores. Data moves between devices by JAX's collectives and lax.ppermute only.
A program may use at most 232 MiB of HBM per device.

```python
import math
import jax
import jax.numpy as jnp
import numpy as np
from jax import lax

D = 1024
HEAD = 64
FF = 4096
MB = 2
DOCS = 4
PACKS = 16
PACK = 1536
SRC_PACK = 1024
BLK = 384


def draw_order(key, part):
    halves = PACK // (2 * BLK)
    slots = jnp.arange(PACK, dtype=jnp.int32)

    def one_pack(pack_key):
        early_key, late_key = jax.random.split(pack_key)
        early = jax.random.permutation(early_key, halves).astype(jnp.int32)
        late = jax.random.permutation(late_key, halves).astype(jnp.int32) + halves
        blocks = jnp.stack([early, late], axis=1).reshape(-1)
        return (blocks[slots // BLK] * BLK + slots % BLK).astype(jnp.int32)
    pack_keys = jax.random.split(jax.random.fold_in(key, 11), MB * PACKS)
    return jax.vmap(one_pack)(pack_keys).reshape(MB, PACKS, PACK)


def draw_target_lengths(key, part):
    spare = PACK // 4 - (DOCS - 1)

    def one_pack(pack_key):
        cuts = jnp.sort(jax.random.randint(pack_key, (DOCS - 2,), 0, spare + 1)).astype(jnp.int32)
        edges = jnp.concatenate([jnp.zeros((1,), jnp.int32), cuts, jnp.full((1,), spare, jnp.int32)])
        others = edges[1:] - edges[:-1] + 1
        return jnp.concatenate([jnp.full((1,), 3 * PACK // 4, jnp.int32), others]).astype(jnp.int32)
    pack_keys = jax.random.split(jax.random.fold_in(key, 23), MB * PACKS)
    return jax.vmap(one_pack)(pack_keys).reshape(MB, PACKS, DOCS)


def raised(values, rng, source, target, blocks, factor):
    owner, partner = [(jnp.arange(values.shape[position]) // (values.shape[position] // blocks)).reshape([-1 if axis == position else 1 for axis in range(values.ndim)]) for position in (source, target)]
    chosen = jax.random.permutation(rng, blocks)[partner]
    strong = (owner == chosen) | (owner == (partner + blocks // 2) % blocks)
    return jnp.where(strong, factor * values, values)


def shard_levels(key, dims, cuts, smallest, top_value):
    loudness, own = 1.0, jax.random.fold_in(key, 6)
    for position, shards_of in cuts:
        heights = jnp.exp(jax.random.uniform(jax.random.fold_in(own, position), (shards_of,), jnp.float32, smallest / len(cuts), top_value / len(cuts)))
        loudness = loudness * jnp.repeat(heights, dims[position] // shards_of).reshape([-1 if axis == position else 1 for axis in range(len(dims))])
    return loudness


def split_up(number_of, total, limit, slope):
    weights = [(1 << 20) // math.isqrt(grade ** slope) + 1 for grade in range(2, number_of + 1)]
    surplus, holding = total - limit - (number_of - 1), [1] * (number_of - 1)
    while surplus > 0:
        candidates = [i for i in range(number_of - 1) if holding[i] < limit]
        whole, remaining = sum([weights[i] for i in candidates]), surplus
        for i in candidates:
            extra = min(limit - holding[i], max(1, remaining * weights[i] // whole), surplus)
            holding[i] = holding[i] + extra
            surplus = surplus - extra
    return np.array([limit] + holding)


def uneven_parts(key, number_of, total, bound, slope):
    if number_of == 2:
        one = jax.random.randint(key, (), max(1, total - bound), min(bound, total - 1) + 1)
        return jnp.stack([one, total - one])
    tallies = jnp.asarray(split_up(number_of, total, bound, slope), jnp.int32)
    pairs = (number_of - 1) // 2
    source_of, taker = tallies[1:1 + 2 * pairs:2], tallies[2:2 + 2 * pairs:2]
    room = jnp.minimum(source_of - 1, bound - taker)
    passed = jax.random.randint(jax.random.fold_in(key, 1), (pairs,), 0, 1 << 20) % (room + 1)
    tallies = tallies.at[1:1 + 2 * pairs:2].set(source_of - passed).at[2:2 + 2 * pairs:2].set(taker + passed)
    return tallies[jax.random.permutation(jax.random.fold_in(key, 2), number_of)]


def normal_values(stream_key, extent, scale, most, shards=(), kind=jnp.bfloat16):
    loudness = shard_levels(stream_key, extent, shards, -0.22, 0.18) if shards else 1.0
    values = jax.random.normal(stream_key, extent, jnp.float32) * scale * loudness
    return jnp.minimum(jnp.maximum(values, -most), most).astype(kind)


def noise_with(rng, dims, scale, limit, cuts, heavy, kind=jnp.bfloat16):
    values = scale * jax.random.normal(rng, dims, jnp.float32)
    if cuts:
        values = values * shard_levels(rng, dims, cuts, -0.22, 0.18)
    return jnp.clip(raised(values, jax.random.fold_in(rng, 3), *heavy), -limit, limit).astype(kind)


def setup_inputs(seed: int = 0) -> dict:
    arg_keys = jax.random.split(jax.random.key(seed), 16)
    tokens = noise_with(arg_keys[0], (MB, PACKS, PACK, D), 1.0, 6.0, ((1, 16), (2, 2)), (1, 3, 16, 2.0))
    encoded = noise_with(arg_keys[1], (MB, PACKS, SRC_PACK, D), 1.0, 6.0, ((1, 16), (2, 2)), (1, 3, 16, 2.0))
    cotangent = normal_values(arg_keys[2], (MB, PACKS, PACK, D), 1.0, 6.0, ((1, 16), (2, 2)))
    order = draw_order(jax.random.fold_in(arg_keys[15], 71), 0)
    target_lengths = draw_target_lengths(jax.random.fold_in(arg_keys[15], 71), 0)
    source_lengths = jax.vmap(lambda own: uneven_parts(own, DOCS, SRC_PACK, SRC_PACK // 2, 2))(jax.random.split(arg_keys[5], MB * PACKS)).reshape((MB, PACKS, DOCS)).astype(jnp.int32)
    self_project = normal_values(arg_keys[6], (D, 3 * D), (D // 2) ** -0.5, 0.25, ((0, 16),))
    self_output = normal_values(arg_keys[7], (D, D), (D // 16) ** -0.5, 0.75, ((0, 16),))
    cross_query = normal_values(arg_keys[8], (D, D), (D // 2) ** -0.5, 0.25, ((0, 16),))
    cross_source = normal_values(arg_keys[9], (D, 2 * D), (D // 2) ** -0.5, 0.25, ((0, 16),))
    cross_output = normal_values(arg_keys[10], (D, D), (D // 16) ** -0.5, 0.75, ((0, 16),))
    feed_in = normal_values(arg_keys[11], (D, FF), D ** -0.5, 0.1875, ((0, 16),))
    feed_out = normal_values(arg_keys[12], (FF, D), FF ** -0.5, 0.09375, ((0, 16),))
    norm_gain = jnp.clip(1.0 + 0.1 * jax.random.normal(arg_keys[13], (3, D), jnp.float32), 0.5, 1.5).astype(jnp.bfloat16)
    norm_bias = normal_values(arg_keys[14], (3, D), 0.3, 2.0, ((1, 16),))
    return {"tokens": tokens, "encoded": encoded, "cotangent": cotangent, "order": order, "target_lengths": target_lengths, "source_lengths": source_lengths, "self_project": self_project, "self_output": self_output, "cross_query": cross_query, "cross_source": cross_source, "cross_output": cross_output, "feed_in": feed_in, "feed_out": feed_out, "norm_gain": norm_gain, "norm_bias": norm_bias}


@jax.custom_vjp
def low(v):
    return lax.optimization_barrier(v.astype(jnp.bfloat16)).astype(jnp.float32)

@jax.custom_vjp
def low_back(v):
    return v

def low_keep(v):
    return (low(v), None)

def low_pass(kept, grad):
    return (grad,)

def back_keep(v):
    return (v, None)

def back_low(kept, grad):
    return (low(grad),)
low.defvjp(low_keep, low_pass)
low_back.defvjp(back_keep, back_low)
HIGHEST = lax.Precision.HIGHEST
MASKED = -1e+30

def both_ways(values):
    return low(low_back(values))

def product(left, right):
    return jnp.dot(left, right, precision=HIGHEST)

def norm_apply(values, gain, bias):
    mean = lax.optimization_barrier(jnp.mean(values, axis=-1, keepdims=True))
    centred = values - mean
    spread = lax.optimization_barrier(jnp.mean(centred * centred, axis=-1, keepdims=True))
    return centred * lax.rsqrt(spread + 1e-05) * gain + bias

def docs_of(places, lengths):
    ends = jnp.cumsum(lengths).astype(jnp.int32)
    return lax.optimization_barrier(jnp.sum((places[:, None] >= ends[None, :]).astype(jnp.int32), axis=1)).astype(jnp.int32)

def attend(query, keys, values, allowed):
    rows = query.shape[0]
    scores = jnp.einsum('qhd,khd->hqk', query.reshape(rows, -1, HEAD), keys.reshape(keys.shape[0], -1, HEAD), precision=HIGHEST) * HEAD ** (-0.5)
    scores = low_back(scores)
    scores = jnp.where(allowed[None], scores, MASKED)
    probs = low(jax.nn.softmax(scores, axis=-1))
    mixed = jnp.einsum('hqk,khd->qhd', probs, values.reshape(values.shape[0], -1, HEAD), precision=HIGHEST)
    return both_ways(mixed.reshape(rows, -1))

def attend_blocks(query, keys, values, query_docs, query_places, key_docs, key_places):
    rows = query.shape[0]
    width = math.gcd(rows, 512)
    count = rows // width

    def one_block(item):
        part_query, part_docs, part_places = item
        allowed = part_docs[:, None] == key_docs[None, :]
        if key_places is not None:
            allowed = allowed & (key_places[None, :] <= part_places[:, None])
        return attend(part_query, keys, values, allowed)
    result = lax.map(jax.checkpoint(one_block), (query.reshape(count, width, -1), query_docs.reshape(count, width), query_places.reshape(count, width)))
    return result.reshape(rows, -1)

def layer(tokens, encoded, weights, places, target_docs, source_docs):
    self_project, self_output, cross_query, cross_source, cross_output, feed_in, feed_out, norm_gain, norm_bias = weights
    model = tokens.shape[1]
    first = low(norm_apply(tokens, norm_gain[0], norm_bias[0]))
    projected = both_ways(product(first, self_project))
    query = projected[:, :model]
    keys = projected[:, model:2 * model]
    values = projected[:, 2 * model:]
    self_mixed = attend_blocks(query, keys, values, target_docs, places, target_docs, places)
    after_self = tokens + low_back(product(self_mixed, self_output))
    second = low(norm_apply(after_self, norm_gain[1], norm_bias[1]))
    cross_queries = both_ways(product(second, cross_query))
    source = both_ways(product(encoded, cross_source))
    cross_mixed = attend_blocks(cross_queries, source[:, :model], source[:, model:], target_docs, places, source_docs, None)
    after_cross = after_self + low_back(product(cross_mixed, cross_output))
    third = low(norm_apply(after_cross, norm_gain[2], norm_bias[2]))
    hidden = low_back(product(third, feed_in))
    active = both_ways(jax.nn.gelu(hidden, approximate=False))
    return after_cross + low_back(product(active, feed_out))

def reference(tokens, encoded, cotangent, order, target_lengths, source_lengths, self_project, self_output, cross_query, cross_source, cross_output, feed_in, feed_out, norm_gain, norm_bias):
    weights = tuple((item.astype(jnp.float32) for item in (self_project, self_output, cross_query, cross_source, cross_output, feed_in, feed_out, norm_gain, norm_bias)))
    packs = tokens.shape[0] * tokens.shape[1]
    source_total = encoded.shape[2]

    def flatten(array):
        return array.reshape((packs,) + array.shape[2:])

    def one_pack(carry, item):
        pack_tokens, pack_encoded, pack_cot, places, target_count, source_count = item
        target_docs = docs_of(places, target_count)
        source_docs = docs_of(jnp.arange(source_total, dtype=jnp.int32), source_count)

        def run(values, source, params):
            return layer(values, source, params, places, target_docs, source_docs)
        result, pull = jax.vjp(run, pack_tokens.astype(jnp.float32), pack_encoded.astype(jnp.float32), weights)
        grad_values, grad_source, grad_params = pull(pack_cot.astype(jnp.float32))
        carry = jax.tree.map(jnp.add, carry, grad_params)
        return (carry, (result.astype(jnp.bfloat16), grad_values.astype(jnp.bfloat16), grad_source.astype(jnp.bfloat16)))
    zeros = tuple((jnp.zeros_like(item) for item in weights))
    totals, (results, grad_values, grad_source) = lax.scan(one_pack, zeros, (flatten(tokens), flatten(encoded), flatten(cotangent), flatten(order), flatten(target_lengths), flatten(source_lengths)))
    return (results.reshape(tokens.shape), grad_values.reshape(tokens.shape), grad_source.reshape(encoded.shape), totals[0], totals[1], totals[2], totals[3], totals[4], totals[5], totals[6], totals[7], totals[8][:2], totals[8][2])
```

```python
import functools
import math

import jax
import jax.numpy as jnp
from jax import lax
from jax.experimental import pallas as pl
from jax.experimental.pallas import tpu as pltpu
from jax.sharding import PartitionSpec as P

HEAD = 64


MASKED = -1e30


def as_sent(x):

    def short(part):
        return part.astype(jnp.bfloat16) if part.dtype == jnp.float32 else part

    return jax.tree.map(short, x)


def norm_apply(values, gain, bias):
    mean = jnp.mean(values, axis=-1, keepdims=True)
    centred = values - mean
    spread = jnp.mean(centred * centred, axis=-1, keepdims=True)
    return centred * lax.rsqrt(spread + 1e-05) * gain + bias


def gelu_exact(values):
    return jax.nn.gelu(values, approximate=False)


def docs_of(places, lengths):
    ends = jnp.cumsum(lengths)
    return jnp.sum((places[:, None] >= ends[None, :]).astype(jnp.int32), axis=1)


def split_heads(values):
    return values.reshape(values.shape[0], -1, HEAD)


def block_scores(query, pairs, allowed, start, count):
    model = query.shape[1]
    block = lax.dynamic_slice_in_dim(pairs, start, count, 0)
    scores = jnp.einsum(
        "qhd,khd->hqk",
        split_heads(query),
        split_heads(block[:, :model]),
        preferred_element_type=jnp.float32,
    )
    scores = jnp.where(allowed(start, count)[None], scores * HEAD ** (-0.5), MASKED)
    return (scores, block)


def log_mass(query, pairs, allowed, width):
    rows, model = query.shape
    heads = model // HEAD

    def step(index, carry):
        peak, total = carry
        scores, _ = block_scores(query, pairs, allowed, index * width, width)
        new_peak = jnp.maximum(peak, jnp.max(scores, axis=2))
        total = total * jnp.exp(peak - new_peak) + jnp.sum(
            jnp.exp(scores - new_peak[:, :, None]), axis=2
        )
        return (new_peak, total)

    begin = (jnp.full((heads, rows), MASKED, jnp.float32), jnp.zeros((heads, rows), jnp.float32))
    peak, total = lax.fori_loop(0, pairs.shape[0] // width, step, begin)
    return peak + jnp.log(total)


def attend_forward(query, pairs, allowed, width, log_total):
    rows, model = query.shape

    def step(index, mixed):
        scores, block = block_scores(query, pairs, allowed, index * width, width)
        probs = jnp.exp(scores - log_total[:, :, None]).astype(jnp.bfloat16)
        return mixed + jnp.einsum(
            "hqk,khd->qhd", probs, split_heads(block[:, model:]), preferred_element_type=jnp.float32
        )

    mixed = lax.fori_loop(
        0, pairs.shape[0] // width, step, jnp.zeros((rows, model // HEAD, HEAD), jnp.float32)
    )
    return mixed.reshape(rows, model).astype(jnp.bfloat16)


def score_grads(query, pairs, allowed, grad_mixed, log_total, start, count):
    model = query.shape[1]
    scores, block = block_scores(query, pairs, allowed, start, count)
    probs = jnp.exp(scores - log_total[:, :, None])
    grad_probs = jnp.einsum(
        "qhd,khd->hqk",
        split_heads(grad_mixed),
        split_heads(block[:, model:]),
        preferred_element_type=jnp.float32,
    )
    return (probs, grad_probs, block)


def attend_delta(query, pairs, allowed, grad_mixed, log_total, width):
    rows, model = query.shape

    def step(index, delta):
        probs, grad_probs, _ = score_grads(
            query, pairs, allowed, grad_mixed, log_total, index * width, width
        )
        return delta + jnp.sum(probs * grad_probs, axis=2)

    return lax.fori_loop(
        0, pairs.shape[0] // width, step, jnp.zeros((model // HEAD, rows), jnp.float32)
    )


def attend_query_grad(query, pairs, allowed, grad_mixed, log_total, delta, width):
    rows, model = query.shape

    def step(index, grad):
        probs, grad_probs, block = score_grads(
            query, pairs, allowed, grad_mixed, log_total, index * width, width
        )
        grad_scores = (probs * (grad_probs - delta[:, :, None])).astype(jnp.bfloat16)
        return grad + jnp.einsum(
            "hqk,khd->qhd",
            grad_scores,
            split_heads(block[:, :model]),
            preferred_element_type=jnp.float32,
        )

    grad = lax.fori_loop(
        0, pairs.shape[0] // width, step, jnp.zeros((rows, model // HEAD, HEAD), jnp.float32)
    )
    return (grad.reshape(rows, model) * HEAD ** (-0.5)).astype(jnp.bfloat16)


def key_terms(query, pairs, allowed, grad_mixed, log_total, delta, width, count):
    model = query.shape[1]
    step_width = math.gcd(count, width)

    def step(index, terms):
        probs, grad_probs, _ = score_grads(
            query, pairs, allowed, grad_mixed, log_total, index * step_width, step_width
        )
        grad_scores = (probs * (grad_probs - delta[:, :, None])).astype(jnp.bfloat16)
        grad_keys = jnp.einsum(
            "hqk,qhd->khd", grad_scores, split_heads(query), preferred_element_type=jnp.float32
        ) * HEAD ** (-0.5)
        grad_values = jnp.einsum(
            "hqk,qhd->khd",
            probs.astype(jnp.bfloat16),
            split_heads(grad_mixed),
            preferred_element_type=jnp.float32,
        )
        piece = jnp.concatenate(
            [grad_keys.reshape(step_width, model), grad_values.reshape(step_width, model)], axis=1
        )
        return lax.dynamic_update_slice_in_dim(terms, piece, index * step_width, 0)

    return lax.fori_loop(0, count // step_width, step, jnp.zeros((count, 2 * model), jnp.float32))


def body(
    tokens,
    encoded,
    cotangent,
    order,
    target_lengths,
    source_lengths,
    self_project,
    self_output,
    cross_query,
    cross_source,
    cross_output,
    feed_in,
    feed_out,
    norm_gain,
    norm_bias,
):
    micro = tokens.shape[0]
    rows = tokens.shape[2]
    model = tokens.shape[3]
    source_rows = encoded.shape[2]
    place = lax.axis_index("ctx")
    group = lax.axis_size("ctx")
    pack_total = rows * group
    source_total = source_rows * group
    self_width = math.gcd(pack_total, 512)
    cross_width = math.gcd(source_total, 512)
    results = []
    grad_values_all = []
    grad_encoded_all = []
    totals = ()
    for index in range(micro):
        attention_part = (
            lax.all_gather(self_project, "fsdp", axis=0, tiled=True),
            lax.all_gather(self_output, "fsdp", axis=0, tiled=True),
            lax.all_gather(cross_query, "fsdp", axis=0, tiled=True),
            lax.all_gather(cross_source, "fsdp", axis=0, tiled=True),
            lax.all_gather(cross_output, "fsdp", axis=0, tiled=True),
            lax.all_gather(norm_gain, "fsdp", axis=1, tiled=True),
            lax.all_gather(norm_bias, "fsdp", axis=1, tiled=True),
        )
        feed_part = (
            lax.all_gather(feed_in, "fsdp", axis=0, tiled=True),
            lax.all_gather(feed_out, "fsdp", axis=0, tiled=True),
        )
        weights = tuple(attention_part) + tuple(feed_part)
        (
            self_in_full,
            self_out_full,
            cross_query_full,
            cross_source_full,
            cross_out_full,
            gain_full,
            bias_full,
            feed_in_full,
            feed_out_full,
        ) = weights
        gains = gain_full.astype(jnp.float32)
        biases = bias_full.astype(jnp.float32)
        values = tokens[index, 0].astype(jnp.float32)
        source = encoded[index, 0]
        grad_out = cotangent[index, 0]
        places = order[index, 0]
        target_docs = docs_of(places, target_lengths[index, 0])
        query_places = lax.dynamic_slice_in_dim(places, place * rows, rows)
        query_docs = lax.dynamic_slice_in_dim(target_docs, place * rows, rows)
        source_docs = docs_of(jnp.arange(source_total, dtype=jnp.int32), source_lengths[index, 0])

        def self_allowed(start, count):
            key_docs = lax.dynamic_slice_in_dim(target_docs, start, count)
            key_places = lax.dynamic_slice_in_dim(places, start, count)
            return (query_docs[:, None] == key_docs[None, :]) & (
                key_places[None, :] <= query_places[:, None]
            )

        def cross_allowed(start, count):
            return (
                query_docs[:, None] == lax.dynamic_slice_in_dim(source_docs, start, count)[None, :]
            )

        first = norm_apply(values, gains[0], biases[0]).astype(jnp.bfloat16)
        query = jnp.dot(first, self_in_full[:, :model], preferred_element_type=jnp.float32).astype(
            jnp.bfloat16
        )
        local_pairs = jnp.dot(
            first, self_in_full[:, model:], preferred_element_type=jnp.float32
        ).astype(jnp.bfloat16)
        self_pairs = lax.all_gather(local_pairs, "ctx", axis=0, tiled=True)
        self_total = log_mass(query, self_pairs, self_allowed, self_width)
        self_mixed = attend_forward(query, self_pairs, self_allowed, self_width, self_total)
        after_self = values + jnp.dot(self_mixed, self_out_full, preferred_element_type=jnp.float32)
        second = norm_apply(after_self, gains[1], biases[1]).astype(jnp.bfloat16)
        cross_queries = jnp.dot(
            second, cross_query_full, preferred_element_type=jnp.float32
        ).astype(jnp.bfloat16)
        cross_local = jnp.dot(source, cross_source_full, preferred_element_type=jnp.float32).astype(
            jnp.bfloat16
        )
        cross_pairs = lax.all_gather(cross_local, "ctx", axis=0, tiled=True)
        cross_total = log_mass(cross_queries, cross_pairs, cross_allowed, cross_width)
        cross_mixed = attend_forward(
            cross_queries, cross_pairs, cross_allowed, cross_width, cross_total
        )
        after_cross = after_self + jnp.dot(
            cross_mixed, cross_out_full, preferred_element_type=jnp.float32
        )
        third = norm_apply(after_cross, gains[2], biases[2]).astype(jnp.bfloat16)
        hidden = jnp.dot(third, feed_in_full, preferred_element_type=jnp.float32)
        active = gelu_exact(hidden).astype(jnp.bfloat16)
        result = (
            after_cross + jnp.dot(active, feed_out_full, preferred_element_type=jnp.float32)
        ).astype(jnp.bfloat16)
        grad_feed_out = jnp.einsum(
            "rf,rd->fd", active, grad_out, preferred_element_type=jnp.float32
        )
        grad_active = jnp.einsum(
            "rd,fd->rf", grad_out, feed_out_full, preferred_element_type=jnp.float32
        ).astype(jnp.bfloat16)
        _, gelu_pull = jax.vjp(gelu_exact, hidden)
        grad_hidden = gelu_pull(grad_active.astype(jnp.float32))[0].astype(jnp.bfloat16)
        grad_feed_in = jnp.einsum(
            "rd,rf->df", third, grad_hidden, preferred_element_type=jnp.float32
        )
        grad_third = jnp.einsum(
            "rf,df->rd", grad_hidden, feed_in_full, preferred_element_type=jnp.float32
        )
        _, norm_pull = jax.vjp(norm_apply, after_cross, gains[2], biases[2])
        norm_part, gain_two, bias_two = norm_pull(grad_third)
        grad_after_cross = grad_out.astype(jnp.float32) + norm_part
        cross_branch = grad_after_cross.astype(jnp.bfloat16)
        grad_cross_output = jnp.einsum(
            "rd,re->de", cross_mixed, cross_branch, preferred_element_type=jnp.float32
        )
        grad_cross_mixed = jnp.einsum(
            "re,de->rd", cross_branch, cross_out_full, preferred_element_type=jnp.float32
        ).astype(jnp.bfloat16)
        cross_delta = attend_delta(
            cross_queries, cross_pairs, cross_allowed, grad_cross_mixed, cross_total, cross_width
        )
        grad_cross_queries = attend_query_grad(
            cross_queries,
            cross_pairs,
            cross_allowed,
            grad_cross_mixed,
            cross_total,
            cross_delta,
            cross_width,
        )
        grad_source = lax.psum_scatter(
            key_terms(
                cross_queries,
                cross_pairs,
                cross_allowed,
                grad_cross_mixed,
                cross_total,
                cross_delta,
                cross_width,
                source_rows * lax.axis_size("ctx"),
            ).astype(jnp.bfloat16),
            "ctx",
            scatter_dimension=0,
            tiled=True,
        )
        grad_cross_source = jnp.einsum(
            "sd,se->de", source, grad_source, preferred_element_type=jnp.float32
        )
        grad_encoded = jnp.einsum(
            "se,de->sd", grad_source, cross_source_full, preferred_element_type=jnp.float32
        ).astype(jnp.bfloat16)
        grad_cross_query = jnp.einsum(
            "rd,re->de", second, grad_cross_queries, preferred_element_type=jnp.float32
        )
        grad_second = jnp.einsum(
            "re,de->rd", grad_cross_queries, cross_query_full, preferred_element_type=jnp.float32
        )
        _, norm_pull = jax.vjp(norm_apply, after_self, gains[1], biases[1])
        norm_part, gain_one, bias_one = norm_pull(grad_second)
        grad_after_self = grad_after_cross + norm_part
        self_branch = grad_after_self.astype(jnp.bfloat16)
        grad_self_output = jnp.einsum(
            "rd,re->de", self_mixed, self_branch, preferred_element_type=jnp.float32
        )
        grad_self_mixed = jnp.einsum(
            "re,de->rd", self_branch, self_out_full, preferred_element_type=jnp.float32
        ).astype(jnp.bfloat16)
        self_delta = attend_delta(
            query, self_pairs, self_allowed, grad_self_mixed, self_total, self_width
        )
        grad_query = attend_query_grad(
            query, self_pairs, self_allowed, grad_self_mixed, self_total, self_delta, self_width
        )
        grad_pairs = lax.psum_scatter(
            key_terms(
                query,
                self_pairs,
                self_allowed,
                grad_self_mixed,
                self_total,
                self_delta,
                self_width,
                rows * lax.axis_size("ctx"),
            ).astype(jnp.bfloat16),
            "ctx",
            scatter_dimension=0,
            tiled=True,
        )
        grad_projected = jnp.concatenate([grad_query, grad_pairs], axis=1)
        grad_self_project = jnp.einsum(
            "rd,re->de", first, grad_projected, preferred_element_type=jnp.float32
        )
        grad_first = jnp.einsum(
            "re,de->rd", grad_projected, self_in_full, preferred_element_type=jnp.float32
        )
        _, norm_pull = jax.vjp(norm_apply, values, gains[0], biases[0])
        norm_part, gain_zero, bias_zero = norm_pull(grad_first)
        grad_values = (grad_after_self + norm_part).astype(jnp.bfloat16)
        grads = (
            grad_self_project,
            grad_self_output,
            grad_cross_query,
            grad_cross_source,
            grad_cross_output,
            grad_feed_in,
            grad_feed_out,
            jnp.stack([gain_zero, gain_one, gain_two]),
            jnp.stack([bias_zero, bias_one, bias_two]),
        )
        result, grad_values, grad_encoded, grads = (result, grad_values, grad_encoded, grads)
        totals = (
            grads
            if index == 0
            else tuple((jnp.add(left, right) for left, right in zip(totals, grads)))
        )
        results.append(result)
        grad_values_all.append(grad_values)
        grad_encoded_all.append(grad_encoded)
    shares = (
        lax.psum_scatter(
            totals[0].astype(jnp.bfloat16), "fsdp", scatter_dimension=0, tiled=True
        ).astype(jnp.float32),
        lax.psum_scatter(
            totals[1].astype(jnp.bfloat16), "fsdp", scatter_dimension=0, tiled=True
        ).astype(jnp.float32),
        lax.psum_scatter(
            totals[2].astype(jnp.bfloat16), "fsdp", scatter_dimension=0, tiled=True
        ).astype(jnp.float32),
        lax.psum_scatter(
            totals[3].astype(jnp.bfloat16), "fsdp", scatter_dimension=0, tiled=True
        ).astype(jnp.float32),
        lax.psum_scatter(
            totals[4].astype(jnp.bfloat16), "fsdp", scatter_dimension=0, tiled=True
        ).astype(jnp.float32),
        lax.psum_scatter(
            totals[5].astype(jnp.bfloat16), "fsdp", scatter_dimension=0, tiled=True
        ).astype(jnp.float32),
        lax.psum_scatter(
            totals[6].astype(jnp.bfloat16), "fsdp", scatter_dimension=0, tiled=True
        ).astype(jnp.float32),
        lax.psum_scatter(
            totals[7].astype(jnp.bfloat16), "fsdp", scatter_dimension=1, tiled=True
        ).astype(jnp.float32),
        lax.psum_scatter(
            totals[8].astype(jnp.bfloat16), "fsdp", scatter_dimension=1, tiled=True
        ).astype(jnp.float32),
    )
    totals = tuple(
        jax.tree.map(lambda part: part.astype(jnp.float32), lax.psum(as_sent(tuple(shares)), "ctx"))
    )
    output = jnp.stack(results)[:, None]
    grad_tokens = jnp.stack(grad_values_all)[:, None]
    grad_source_rows = jnp.stack(grad_encoded_all)[:, None]
    return (
        output,
        grad_tokens,
        grad_source_rows,
        totals[0],
        totals[1],
        totals[2],
        totals[3],
        totals[4],
        totals[5],
        totals[6],
        totals[7],
        totals[8][:2],
        totals[8][2],
    )


BIG = 1e30
SCALE2 = HEAD ** (-0.5) * math.log2(math.e)
NT = (((1,), (1,)), ((), ()))
TN = (((0,), (0,)), ((), ()))
NN = (((1,), (0,)), ((), ()))


def dot(left, right, dims=NN):
    return lax.dot_general(left, right, dims, preferred_element_type=jnp.float32)


def lanes(rows):
    return lax.broadcasted_iota(jnp.int32, (rows, 128), 1)


def parts(x):
    hi = x.astype(jnp.bfloat16)
    rest = x - hi.astype(jnp.float32)
    mid = rest.astype(jnp.bfloat16)
    lo = (rest - mid.astype(jnp.float32)).astype(jnp.bfloat16)
    return (hi, mid, lo)


def spread(x, base):
    hi, mid, lo = parts(x)
    lane = lanes(x.shape[0]) % HEAD
    return jnp.where(lane == 4, hi, jnp.where(lane == 5, mid, jnp.where(lane == 6, lo, base)))


def beyond(size, flip):
    row = lax.broadcasted_iota(jnp.int32, (size, size), 0)
    column = lax.broadcasted_iota(jnp.int32, (size, size), 1)
    return row > column if flip else column > row


def two_heads(ref, own, other):
    left = lanes(own.shape[0]) < HEAD
    ref[0] = jnp.where(left, own, other)
    ref[1] = jnp.where(left, other, own)


def attend_kernel(plan, q_ref, k_ref, v_ref, qd_ref, kd_ref, out_ref, extra_ref, keys, values):
    two_heads(keys, k_ref[...], kd_ref[...])
    two_heads(values, v_ref[...], jnp.ones_like(v_ref))
    for q0, q1, k0, k1, diagonal in plan:
        rows, width = (q1 - q0, k1 - k0)
        left = lanes(rows) < HEAD
        q, qd = (q_ref[q0:q1], qd_ref[q0:q1])
        scores = []
        for h in range(2):
            s = dot(jnp.where(left == (h == 0), q, qd), keys[h, k0:k1], NT)
            if diagonal:
                tail = jnp.where(beyond(rows, False), -BIG, s[:, width - rows :])
                s = tail if width == rows else jnp.concatenate([s[:, : width - rows], tail], axis=1)
            scores.append(s)
        mixed, tops = ([], [])
        for h in range(2):
            top = jnp.max(scores[h], axis=1, keepdims=True)
            probs = jnp.exp2((scores[h] - top) * SCALE2).astype(jnp.bfloat16)
            mixed.append(dot(probs, values[h, k0:k1]))
            tops.append(top)
        mass = jnp.where(left, mixed[1], mixed[0])
        numer = jnp.where(left, mixed[0], mixed[1])
        out_ref[q0:q1] = (numer / pltpu.roll(mass, HEAD, 1)).astype(jnp.bfloat16)
        top = jnp.where(left, tops[1], tops[0])
        extra_ref[q0:q1] = spread(-(top + HEAD**0.5 * jnp.log(mass)), qd)


def attend_back_kernel(
    plan,
    q_ref,
    k_ref,
    v_ref,
    extra_ref,
    kd_ref,
    out_ref,
    g_ref,
    *refs,
):
    *outs, keys, values, queries, grads, total = refs
    if len(outs) == 1:
        dq_ref, dk_ref, dv_ref = (outs[0].at[i] for i in range(3))
    else:
        dq_ref, dk_ref, dv_ref = (outs[0], outs[1].at[0], outs[1].at[1])
    two_heads(keys, k_ref[...], kd_ref[...])
    two_heads(values, v_ref[...], jnp.ones_like(v_ref))
    two_heads(queries, q_ref[...], extra_ref[...])
    square = (128, 128)
    row, column = (lax.broadcasted_iota(jnp.int32, square, axis) < HEAD for axis in (0, 1))
    swap = jnp.where(row != column, 1.0, 0.0).astype(jnp.bfloat16)
    g = g_ref[...]
    terms = parts(g.astype(jnp.float32) * out_ref[...].astype(jnp.float32))
    delta = sum(dot(term, swap) for term in terms)
    two_heads(grads, g, spread(-delta, jnp.zeros_like(g)))
    total[...] = jnp.zeros_like(total)
    for k0, k1, q0, q1, diagonal in plan:
        rows = k1 - k0
        left = lanes(rows) < HEAD
        dks, dvs = ([], [])
        for h in range(2):
            s = dot(keys[h, k0:k1], queries[h, q0:q1], NT)
            if diagonal:
                head = jnp.where(beyond(rows, True), -BIG, s[:, :rows])
                s = head if q1 - q0 == rows else jnp.concatenate([head, s[:, rows:]], axis=1)
            probs = jnp.exp2(s * SCALE2)
            ds = probs * dot(values[h, k0:k1], grads[h, q0:q1], NT)
            ds = ds.astype(jnp.bfloat16)
            dvs.append(dot(probs.astype(jnp.bfloat16), g_ref[q0:q1]))
            dks.append(dot(ds, q_ref[q0:q1]))
            total[h, q0:q1] += dot(ds, k_ref[k0:k1], TN)
        dk_ref[k0:k1] = (jnp.where(left, dks[0], dks[1]) * HEAD ** (-0.5)).astype(jnp.bfloat16)
        dv_ref[k0:k1] = jnp.where(left, dvs[0], dvs[1]).astype(jnp.bfloat16)
    left = lanes(total.shape[1]) < HEAD
    dq_ref[...] = (jnp.where(left, total[0], total[1]) * HEAD ** (-0.5)).astype(jnp.bfloat16)


def pair_of_heads(rows):
    return pl.BlockSpec((rows, 128), lambda i: (0, i))


def all_of(rows):
    return pl.BlockSpec((rows, 128), lambda i: (0, 0))


def plan_cost(plan, model, products):
    area = sum((q1 - q0) * (k1 - k0) for q0, q1, k0, k1, _ in plan) * model
    return pl.CostEstimate(
        flops=8 * area * products, bytes_accessed=1 << 24, transcendentals=area // HEAD
    )


def attend(plan, q, k, v, qd, kd):
    nq, nk, model = (q.shape[0], k.shape[0], q.shape[1])
    shape = jax.ShapeDtypeStruct((nq, model), jnp.bfloat16)
    return pl.pallas_call(
        functools.partial(attend_kernel, plan),
        grid=(model // 128,),
        in_specs=[pair_of_heads(n) for n in (nq, nk, nk)] + [all_of(nq), all_of(nk)],
        out_specs=[pair_of_heads(nq)] * 2,
        out_shape=[shape] * 2,
        scratch_shapes=[pltpu.VMEM((2, nk, 128), jnp.bfloat16)] * 2,
        compiler_params=pltpu.CompilerParams(vmem_limit_bytes=48 * 2**20),
        cost_estimate=plan_cost(plan, model, 2),
    )(q, k, v, qd, kd)


def stacked(count, rows):
    return pl.BlockSpec((count, rows, 128), lambda i: (0, 0, i))


def attend_back(plan, q, k, v, extra, kd, out, g, together):
    nq, nk, model = (q.shape[0], k.shape[0], q.shape[1])
    if together:
        specs, shapes = ([stacked(3, nq)], [(3, nq, model)])
    else:
        specs, shapes = ([pair_of_heads(nq), stacked(2, nk)], [(nq, model), (2, nk, model)])
    outs = pl.pallas_call(
        functools.partial(attend_back_kernel, plan),
        grid=(model // 128,),
        in_specs=[pair_of_heads(n) for n in (nq, nk, nk, nq)]
        + [all_of(nk)]
        + [pair_of_heads(nq)] * 2,
        out_specs=specs,
        out_shape=[jax.ShapeDtypeStruct(shape, jnp.bfloat16) for shape in shapes],
        scratch_shapes=[pltpu.VMEM((2, nk, 128), jnp.bfloat16)] * 2
        + [pltpu.VMEM((2, nq, 128), jnp.bfloat16)] * 2
        + [pltpu.VMEM((2, nq, 128), jnp.float32)],
        compiler_params=pltpu.CompilerParams(vmem_limit_bytes=48 * 2**20),
        cost_estimate=plan_cost(plan, model, 5),
    )(q, k, v, extra, kd, out, g)
    return outs[0] if together else outs


def self_plan(first, total, tile, back):
    plan = []
    for low, high in ((0, first), (first, total)):
        for start in range(low, high, tile):
            end = start + tile
            plan.append((start, end, start, high, True) if back else (start, end, low, end, True))
    return plan


def cross_plan(first, total, reach, source, tile, back):
    if back:
        return [
            (start, start + tile, 0 if start < reach else first, total, False)
            for start in range(0, source, tile)
        ]
    return [
        (start, start + tile, 0, reach if start < first else source, False)
        for start in range(0, total, tile)
    ]


def query_marks(docs):
    lane = jnp.arange(128) % HEAD
    return jnp.where(docs[:, None] == lane[None, :], BIG, 0.0).astype(jnp.bfloat16)


def key_marks(docs, count):
    lane = (jnp.arange(128) % HEAD)[None, :]
    other = jnp.where(docs[:, None] == lane, 0.0, -1.0)
    return jnp.where(lane < count, other, jnp.where(lane < 7, 1.0, 0.0)).astype(jnp.bfloat16)


MODEL = 1024
TILE = 512


def wide(values):
    return values.astype(jnp.float32)


def short(values):
    return values.astype(jnp.bfloat16)


def gathered(ref):
    return ref[...].reshape(-1, ref.shape[-1])


def once(shape, index):
    return pl.BlockSpec(shape, index, pipeline_mode=pl.Buffered(1))


def weight_at(slot):
    return once((16, 64, MODEL), lambda *_: (0, slot, 0))


def norm_rows():
    return once((8, MODEL), lambda *_: (0, 0))


def by_rows(count, width=MODEL):
    return pl.BlockSpec((count, width), lambda i, *_: (i, 0))


def found_rows(count):
    return pl.BlockSpec((count, MODEL), lambda i, held: (held[i], 0))


def sums_out():
    return pl.BlockSpec((8, MODEL), lambda *_: (0, 0))


def struct(shape, kind):
    return jax.ShapeDtypeStruct(shape, kind)


def spread_of(values):
    mean = jnp.mean(values, axis=-1, keepdims=True)
    centred = values - mean
    scale = lax.rsqrt(jnp.mean(centred * centred, axis=-1, keepdims=True) + 1e-05)
    return (centred * scale, scale)


def norm_of(values, norm_ref, k):
    hat, _ = spread_of(values)
    return short(hat * norm_ref[k : k + 1] + norm_ref[3 + k : 4 + k])


def norm_back(values, grad, norm_ref, k, sums_ref):
    hat, scale = spread_of(values)
    each = grad * norm_ref[k : k + 1]
    inner = each - jnp.mean(each, axis=-1, keepdims=True)
    inner = inner - hat * jnp.mean(each * hat, axis=-1, keepdims=True)

    @pl.when(pl.program_id(0) == 0)
    def _():
        sums_ref[...] = jnp.zeros_like(sums_ref)

    sums_ref[0:1] += jnp.sum(grad * hat, axis=0, keepdims=True)
    sums_ref[1:2] += jnp.sum(grad, axis=0, keepdims=True)
    return scale * inner


def call(kernel, grid, in_specs, out_specs, out_shape, flops, scratch=(), prefetch=0, aliases=None):
    return pl.pallas_call(
        kernel,
        grid_spec=pltpu.PrefetchScalarGridSpec(
            num_scalar_prefetch=prefetch,
            grid=grid,
            in_specs=in_specs,
            out_specs=out_specs,
            scratch_shapes=list(scratch),
        ),
        out_shape=out_shape,
        input_output_aliases=aliases or {},
        compiler_params=pltpu.CompilerParams(vmem_limit_bytes=58 * 2**20),
        cost_estimate=pl.CostEstimate(flops=flops, bytes_accessed=1 << 24, transcendentals=0),
    )


def pack_kernel(*refs):
    attention_ref, feed_ref = refs[-2:]
    self_in, self_out, cross_q, cross_s, cross_out, feed_in, feed_out, norms = refs[:-2]
    rows = self_in.shape[0]
    slot = 0
    for ref in (self_in, self_out, cross_q, cross_s, cross_out):
        for start in range(0, ref.shape[1], MODEL):
            attention_ref[slot * rows : (slot + 1) * rows] = ref[:, start : start + MODEL]
            slot += 1
    attention_ref[slot * rows :] = norms[...]
    piece = feed_out.shape[0] // 2
    for lot in range(2):
        for owner in range(16):
            column = (2 * owner + lot) * piece
            slot, spot = (2 * lot + owner // 8, owner % 8 * piece)
            feed_ref[slot * rows : (slot + 1) * rows, spot : spot + piece] = feed_in[
                :, column : column + piece
            ]
    feed_ref[4 * rows : 8 * rows] = feed_out[...]
    feed_ref[8 * rows :] = jnp.zeros_like(norms)


def pack(weights, norms):
    arrays = tuple(weights) + (norms,)
    out = struct((528, MODEL), jnp.bfloat16)
    return call(
        pack_kernel,
        (1,),
        [once(a.shape, lambda i: (0, 0)) for a in arrays],
        [once(out.shape, lambda i: (0, 0))] * 2,
        [out] * 2,
        1 << 20,
    )(*arrays)


def enter_kernel(held, tokens_ref, norm_ref, wq, wk, wv, first_ref, q_ref, k_ref, v_ref):
    first = norm_of(wide(tokens_ref[...]), norm_ref, 0)
    first_ref[...] = first
    for weight, out in ((wq, q_ref), (wk, k_ref), (wv, v_ref)):
        out[...] = short(dot(first, gathered(weight)))


def enter(held, tokens, norms, weights, width):
    shape = struct(tokens.shape, jnp.bfloat16)
    return call(
        enter_kernel,
        (tokens.shape[0] // width,),
        [found_rows(width), norm_rows()] + [weight_at(i) for i in range(3)],
        [by_rows(width)] * 4,
        [shape] * 4,
        6 * tokens.size * MODEL,
        prefetch=1,
    )(held, tokens, norms, weights, weights, weights)


def source_kernel(source_ref, wk, wv, k_ref, v_ref):
    source = source_ref[...]
    k_ref[...] = short(dot(source, gathered(wk)))
    v_ref[...] = short(dot(source, gathered(wv)))


def source_pairs(source, weights, width):
    return call(
        source_kernel,
        (source.shape[0] // width,),
        [by_rows(width), weight_at(5), weight_at(6)],
        [by_rows(width)] * 2,
        [struct(source.shape, jnp.bfloat16)] * 2,
        4 * source.size * MODEL,
    )(source, weights, weights)


def between_kernel(held, mixed_ref, tokens_ref, norm_ref, wo, wq, after_ref, second_ref, q_ref):
    after = wide(tokens_ref[...]) + dot(mixed_ref[...], gathered(wo))
    after_ref[...] = after
    second = norm_of(after, norm_ref, 1)
    second_ref[...] = second
    q_ref[...] = short(dot(second, gathered(wq)))


def between(held, mixed, tokens, norms, weights, width):
    return call(
        between_kernel,
        (mixed.shape[0] // width,),
        [by_rows(width), found_rows(width), norm_rows(), weight_at(3), weight_at(4)],
        [by_rows(width)] * 3,
        [struct(mixed.shape, kind) for kind in (jnp.float32, jnp.bfloat16, jnp.bfloat16)],
        4 * mixed.size * MODEL,
        prefetch=1,
    )(held, mixed, tokens, norms, weights, weights)


def before_feed_kernel(mixed_ref, base_ref, norm_ref, wo, after_ref, third_ref):
    after = base_ref[...] + dot(mixed_ref[...], gathered(wo))
    after_ref[...] = after
    third_ref[...] = norm_of(after, norm_ref, 2)


def before_feed(mixed, base, norms, weights, width):
    return call(
        before_feed_kernel,
        (mixed.shape[0] // width,),
        [by_rows(width), by_rows(width), norm_rows(), weight_at(7)],
        [by_rows(width)] * 2,
        [struct(mixed.shape, kind) for kind in (jnp.float32, jnp.bfloat16)],
        2 * mixed.size * MODEL,
    )(mixed, base, norms, weights)


def gelu_terms(hidden):
    bell = jnp.exp2(hidden * hidden * (-0.5 * math.log2(math.e)))
    t = 1.0 / (1.0 + (0.3275911 / math.sqrt(2.0)) * jnp.abs(hidden))
    series = 1.061405429
    for term in (-1.453152027, 1.421413741, -0.284496736, 0.254829592):
        series = series * t + term
    tail = 0.5 * series * t * bell
    return (jnp.where(hidden < 0, tail, 1.0 - tail), bell * (1.0 / math.sqrt(2.0 * math.pi)))


def deal(place_ref, turned, keep_ref, send_ref, value, core, x, y, index, lead=()):
    rel_x = jnp.bitwise_xor(place_ref[1], x)
    rel_y = jnp.bitwise_xor(place_ref[2], y)
    spot = (rel_y, rel_x) if turned else (rel_x, rel_y)

    @pl.when(place_ref[0] == core)
    def _():
        keep_ref[spot + index] = value

    @pl.when(place_ref[0] != core)
    def _():
        send_ref[spot + index] = value


def feed_kernel(
    turned,
    place_ref,
    third_ref,
    grad_ref,
    win_ref,
    wout_ref,
    out_ref,
    back_ref,
    keep_ref,
    send_ref,
    third_t,
    active_ref,
    hidden_ref,
):
    step = pl.program_id(0)

    @pl.when(step == 0)
    def _():
        third_t[...] = third_ref[...].T
        out_ref[...] = jnp.zeros_like(out_ref)
        back_ref[...] = jnp.zeros_like(back_ref)

    win, wout = (gathered(win_ref), gathered(wout_ref))
    rows = third_ref.shape[0]
    lots = [slice(start, start + TILE) for start in range(0, rows, TILE)]

    def enter(lot):
        return (dot(third_ref[lot], win), dot(grad_ref[lot], wout, NT))

    def leave(lot, hidden, grad):
        mass, bell = gelu_terms(hidden)
        active = short(hidden * mass)
        grad = short((mass + hidden * bell) * wide(short(grad)))
        active_ref[lot] = active
        hidden_ref[lot] = grad
        out_ref[lot] += dot(active, wout)
        back_ref[lot] += dot(grad, win, NT)

    ready = enter(lots[0])
    for index, lot in enumerate(lots):
        following = enter(lots[index + 1]) if index + 1 < len(lots) else None
        leave(lot, *ready)
        ready = following
    grad_out = short(dot(active_ref[...], grad_ref[...], TN))
    grad_in = short(dot(third_t[...], hidden_ref[...]))
    for owner in range(4):
        for y in range(2):
            start = owner * 128 + y * 64
            for half in range(2):
                value = grad_out[start + 32 * half : start + 32 * half + 32]
                deal(
                    place_ref, turned, keep_ref, send_ref, value,
                    owner % 2, owner // 2, y, (step, 2 + half),
                )
    for owner in range(16):
        for y in range(2):
            start = owner * 64 + y * 32
            for side in range(2):

                @pl.when(step % 2 == side)
                def _(start=start, owner=owner, y=y, side=side):
                    deal(
                        place_ref, turned, keep_ref, send_ref, grad_in[start : start + 32],
                        owner % 2, owner // 2 % 2, y,
                        (owner // 4, step // 2, slice(None), slice(side * TILE, side * TILE + TILE)),
                    )


def feed(place, third, grad, weights, lot, turned):
    rows = third.shape[0]
    full = struct((rows, MODEL), jnp.float32)
    buffer = struct((2, 2, 4, 4, 32, MODEL), jnp.bfloat16)
    return call(
        functools.partial(feed_kernel, turned),
        (4,),
        [
            once((rows, MODEL), lambda t, place: (0, 0)),
            once((rows, MODEL), lambda t, place: (0, 0)),
            pl.BlockSpec((16, 64, TILE), lambda t, place: (0, 2 * lot + t // 2, t % 2)),
            pl.BlockSpec((4, 128, MODEL), lambda t, place: (t, 2 + lot, 0)),
        ],
        [once((rows, MODEL), lambda t, place: (0, 0))] * 2
        + [once(buffer.shape, lambda t, place: (0, 0, 0, 0, 0, 0))] * 2,
        [full, full, buffer, buffer],
        12 * rows * MODEL * 2048,
        scratch=[
            pltpu.VMEM((MODEL, rows), jnp.bfloat16),
            pltpu.VMEM((rows, TILE), jnp.bfloat16),
            pltpu.VMEM((rows, TILE), jnp.bfloat16),
        ],
        prefetch=1,
    )(place, third, grad, weights, weights)


def after_feed_kernel(
    held,
    after_ref,
    out_a,
    out_b,
    back_a,
    back_b,
    grad_ref,
    norm_ref,
    wo,
    result_ref,
    total_ref,
    branch_ref,
    mixed_ref,
    sums_ref,
):
    after = after_ref[...]
    result_ref[...] = short(after + out_a[...] + out_b[...])
    part = norm_back(after, back_a[...] + back_b[...], norm_ref, 2, sums_ref)
    total = wide(grad_ref[...]) + part
    total_ref[...] = total
    branch = short(total)
    branch_ref[...] = branch
    mixed_ref[...] = short(dot(branch, gathered(wo), NT))


def after_feed(held, after, outs, backs, grad, norms, weights, width):
    narrow = struct(after.shape, jnp.bfloat16)
    return call(
        after_feed_kernel,
        (after.shape[0] // width,),
        [by_rows(width)] * 6 + [norm_rows(), weight_at(7)],
        [found_rows(width)] + [by_rows(width)] * 3 + [sums_out()],
        [narrow, struct(after.shape, jnp.float32), narrow, narrow, struct((8, MODEL), jnp.float32)],
        2 * after.size * MODEL,
        prefetch=1,
    )(held, after, *outs, *backs, grad, norms, weights)


def middle_kernel(
    grad_ref,
    after_ref,
    base_ref,
    norm_ref,
    wq,
    wo,
    total_ref,
    branch_ref,
    mixed_ref,
    sums_ref,
):
    grad = dot(grad_ref[...], gathered(wq), NT)
    total = base_ref[...] + norm_back(after_ref[...], grad, norm_ref, 1, sums_ref)
    total_ref[...] = total
    branch = short(total)
    branch_ref[...] = branch
    mixed_ref[...] = short(dot(branch, gathered(wo), NT))


def middle(grad, after, base, norms, weights, width):
    narrow = struct(after.shape, jnp.bfloat16)
    return call(
        middle_kernel,
        (after.shape[0] // width,),
        [by_rows(width)] * 3 + [norm_rows(), weight_at(4), weight_at(3)],
        [by_rows(width)] * 3 + [sums_out()],
        [struct(after.shape, jnp.float32), narrow, narrow, struct((8, MODEL), jnp.float32)],
        4 * after.size * MODEL,
    )(grad, after, base, norms, weights, weights)


def finish_kernel(
    held, grads_ref, tokens_ref, base_ref, norm_ref, wq, wk, wv, result_ref, sums_ref
):
    grad = sum(dot(grads_ref[i], gathered(w), NT) for i, w in enumerate((wq, wk, wv)))
    part = norm_back(wide(tokens_ref[...]), grad, norm_ref, 0, sums_ref)
    result_ref[...] = short(base_ref[...] + part)


def finish(held, grads, tokens, base, norms, weights, width):
    return call(
        finish_kernel,
        (base.shape[0] // width,),
        [
            pl.BlockSpec((3, width, MODEL), lambda i, held: (0, i, 0)),
            found_rows(width),
            by_rows(width),
            norm_rows(),
        ]
        + [weight_at(i) for i in range(3)],
        [found_rows(width), sums_out()],
        [struct(base.shape, jnp.bfloat16), struct((8, MODEL), jnp.float32)],
        6 * base.size * MODEL,
        prefetch=1,
    )(held, grads, tokens, base, norms, weights, weights, weights)


def source_back_kernel(grads_ref, wk, wv, out_ref):
    grad = dot(grads_ref[0], gathered(wk), NT) + dot(grads_ref[1], gathered(wv), NT)
    out_ref[...] = short(grad)


def source_back(grads, weights, width):
    rows = grads.shape[1]
    return call(
        source_back_kernel,
        (rows // width,),
        [pl.BlockSpec((2, width, MODEL), lambda i: (0, i, 0)), weight_at(5), weight_at(6)],
        [by_rows(width)],
        [struct((rows, MODEL), jnp.bfloat16)],
        4 * rows * MODEL * MODEL,
    )(grads, weights, weights)[0]


def weight_grad_kernel(turned, place_ref, left_ref, right_ref, *refs):
    keep_ref, send_ref = refs[-2:]
    right = right_ref[0] if len(right_ref.shape) == 3 else right_ref[...]
    product = short(dot(left_ref[...], right, TN))
    for owner in range(TILE // 64):
        for y in range(2):
            start = owner * 64 + y * 32
            deal(
                place_ref, turned, keep_ref, send_ref, product[start : start + 32],
                owner % 2, owner // 2 % 2, y, (owner // 4, 0),
            )


def weight_grad(place, left, right, turned, held=None, slot=0, slots=1):
    rows = left.shape[0]
    several = right.ndim == 3
    count = right.shape[0] if several else 1
    shape = struct((2, 2, 4, slots, 32, MODEL), jnp.bfloat16)
    held = () if held is None else tuple(held)
    return call(
        functools.partial(weight_grad_kernel, turned),
        (count, MODEL // TILE),
        [
            pl.BlockSpec((rows, TILE), lambda n, t, place: (0, t)),
            pl.BlockSpec((1, rows, MODEL), lambda n, t, place: (n, 0, 0))
            if several
            else pl.BlockSpec((rows, MODEL), lambda n, t, place: (0, 0)),
        ]
        + [pl.BlockSpec(memory_space=pl.ANY)] * len(held),
        [pl.BlockSpec((2, 2, 2, 1, 32, MODEL), lambda n, t, place: (0, 0, t, slot + n, 0, 0))] * 2,
        [shape] * 2,
        2 * rows * MODEL * MODEL * count,
        prefetch=1,
        aliases={3 + i: i for i in range(len(held))},
    )(place, left, right, *held)


def pairs(bit):
    return [(i, i ^ bit) for i in range(16)]


def swap(values):
    return lax.ppermute(values, "ctx", [(0, 1), (1, 0)])


def reduce_to_owner(keep, send, turned, z):
    def over_x(values):
        return lax.ppermute(values, "fsdp", pairs(2))

    one, two = (swap, over_x) if turned else (over_x, swap)
    core = lax.ppermute(send, "fsdp", pairs(1))
    first = short(wide(keep[1]) + wide(core[1]))
    first = yield (first,)
    first = one(first[0])
    second = short(wide(keep[0, 1]) + wide(core[0, 1]) + wide(first[1]))
    second = yield (second,)
    second = two(second[0])

    def share(index):
        terms = (keep[0, 0], core[0, 0], first[0], second)
        return sum(wide(lax.dynamic_index_in_dim(term, index, 0, False)) for term in terms)

    away = yield tuple(short(share((z + hop) % 4)) for hop in range(1, 4))
    total = share(z)
    for hop, values in enumerate(away, 1):
        cycle = [(i, (i + 4 * hop) % 16) for i in range(16)]
        total = total + wide(lax.ppermute(values, "fsdp", cycle))
    (total,) = yield (short(total),)
    other = swap(total)
    low = lax.axis_index("ctx") == 0
    yield (
        wide(jnp.stack([jnp.where(low, total, other), jnp.where(low, other, total)], axis=1)),
    )


class Steps:
    def __init__(self, steps):
        self.steps = steps
        self.held = next(steps)

    def advance(self):
        self.held = self.steps.send(self.held)


def before(value, *transfers):
    flat = tuple(item for transfer in transfers for item in transfer.held)
    value, *flat = lax.optimization_barrier((value,) + flat)
    for transfer in transfers:
        count = len(transfer.held)
        transfer.held, flat = (tuple(flat[:count]), flat[count:])
    return value


def columns(shares, start, stop):
    part = shares[start:stop].reshape(stop - start, -1, MODEL)
    return jnp.concatenate(list(part), axis=1)


def feed_shares(lots):
    inner = [lot[:2].reshape(2, 64, 8, 128).transpose(1, 0, 2, 3).reshape(64, 16, 128) for lot in lots]
    inner = jnp.stack(inner, axis=2).reshape(64, 4 * MODEL)
    outer = [lot[2:].transpose(1, 0, 2, 3).reshape(128, MODEL) for lot in lots]
    return inner, jnp.concatenate(outer)


def after_all(value, *others):
    return lax.optimization_barrier((value,) + others)[0]


def whole_packs(mesh):
    return mesh.shape["ctx"] == 2 and mesh.shape["fsdp"] == 16


def whole_pack_body(
    tokens,
    encoded,
    cotangent,
    order,
    target_lengths,
    source_lengths,
    self_project,
    self_output,
    cross_query,
    cross_source,
    cross_output,
    feed_in,
    feed_out,
    norm_gain,
    norm_bias,
):
    rows = tokens.shape[2]
    pack_rows, source_rows = (2 * rows, 2 * encoded.shape[2])
    first_rows = 3 * pack_rows // 4
    width = rows // 2
    mine = lax.axis_index("ctx")
    spot = lax.axis_index("fsdp")
    z = spot // 4
    place = jnp.stack([spot % 2, spot // 2 % 2, mine]).astype(jnp.int32)
    part = self_project.shape[0]

    norms = jnp.pad(jnp.concatenate([norm_gain, norm_bias]), ((0, 10), (0, MODEL - part)))
    attention_shard, feed_shard = pack(
        (self_project, self_output, cross_query, cross_source, cross_output, feed_in, feed_out),
        norms,
    )
    weights = lax.all_gather(attention_shard, "fsdp", axis=0)
    norms = wide(weights[:, 8 * part : 8 * part + 8, :part])
    norms = norms.transpose(1, 0, 2).reshape(8, MODEL)

    def both_halves(array):
        own = lax.dynamic_index_in_dim(array, mine, 0, False)[0]
        return own, swap(lax.dynamic_index_in_dim(array, 1 - mine, 0, False)[0])

    places = lax.dynamic_index_in_dim(order, mine, 0, False)[0]
    holds = places[::width] // width
    found = jnp.argsort(holds).astype(jnp.int32)
    held = jnp.where(found // 2 == mine, found % 2, 2 + found % 2)

    def from_both(own, other):
        low = mine == 0
        return jnp.stack([jnp.where(low, own, other), jnp.where(low, other, own)])[:, None]

    def to_slots(halves):
        return from_both(halves[:rows], swap(halves[rows:]))

    halves = jnp.concatenate(both_halves(tokens))
    own, other = both_halves(encoded)
    source = jnp.concatenate([jnp.where(mine == 0, own, other), jnp.where(mine == 0, other, own)])
    grad_out = jnp.concatenate(both_halves(cotangent))
    feed_shard = after_all(feed_shard, halves, source, grad_out)
    grad_out = jnp.concatenate(
        [lax.dynamic_slice_in_dim(grad_out, held[p] * width, width) for p in range(4)]
    )
    feed_weights = lax.all_gather(feed_shard, "fsdp", axis=0)

    lengths = lax.dynamic_index_in_dim(target_lengths, mine, 0, False)[0]
    target_docs = docs_of(jnp.arange(pack_rows, dtype=jnp.int32), lengths)
    lengths = lax.dynamic_index_in_dim(source_lengths, mine, 0, False)[0]
    source_docs = docs_of(jnp.arange(source_rows, dtype=jnp.int32), lengths)
    docs = lengths.shape[0]
    marks = query_marks(target_docs)
    target_marks = key_marks(target_docs, docs)
    source_marks = key_marks(source_docs, docs)
    reach = source_rows // 2

    first, query, keys, values = enter(held, halves, norms, weights, width)
    plan = self_plan(first_rows, pack_rows, width, False)
    self_mixed, self_extra = attend(plan, query, keys, values, marks, target_marks)
    cross_keys, cross_values = source_pairs(source, weights, source_rows // 2)
    after_self, second, cross_queries = between(held, self_mixed, halves, norms, weights, width)
    plan = cross_plan(first_rows, pack_rows, reach, source_rows, width, False)
    cross_mixed, cross_extra = attend(
        plan, cross_queries, cross_keys, cross_values, marks, source_marks
    )
    after_cross, third = before_feed(cross_mixed, after_self, norms, weights, width)

    out_a, back_a, *sent = feed(place, third, grad_out, feed_weights, 0, False)
    first_lot = Steps(reduce_to_owner(*sent, False, z))
    out_b, back_b, *sent = feed(place, after_all(third, *sent), grad_out, feed_weights, 1, True)
    second_lot = Steps(reduce_to_owner(*sent, True, z))
    after_cross = before(after_cross, first_lot)
    result, grad_after_cross, cross_branch, grad_cross_mixed, sums_two = after_feed(
        held, after_cross, (out_a, out_b), (back_a, back_b), grad_out, norms, weights, width
    )
    result = to_slots(result)

    first_lot.advance()
    others = weight_grad(place, cross_mixed, cross_branch, False, slots=5)
    grad_cross_mixed = before(after_all(grad_cross_mixed, *others), second_lot)
    second_lot.advance()
    plan = cross_plan(first_rows, pack_rows, reach, source_rows, source_rows // 4, True)
    grad_cross_queries, grad_source = attend_back(
        plan,
        cross_queries,
        cross_keys,
        cross_values,
        cross_extra,
        source_marks,
        cross_mixed,
        grad_cross_mixed,
        False,
    )
    grad_source = before(grad_source, first_lot, second_lot)
    first_lot.advance()
    second_lot.advance()
    others = weight_grad(place, source, grad_source, False, others, 1, 5)
    others = weight_grad(
        place, second, after_all(grad_cross_queries, *others), False, others, 3, 5
    )
    grad_after_self, self_branch, grad_self_mixed, sums_one = middle(
        grad_cross_queries, after_self, grad_after_cross, norms, weights, width
    )
    others = weight_grad(place, self_mixed, self_branch, False, others, 4, 5)
    other_weights = Steps(reduce_to_owner(*others, False, z))
    grad_encoded = source_back(after_all(grad_source, *others), weights, source_rows // 2)
    grad_self_mixed = after_all(grad_self_mixed, grad_encoded)
    grad_self_mixed = before(grad_self_mixed, first_lot, second_lot, other_weights)
    low, high = (grad_encoded[:reach], grad_encoded[reach:])
    grad_encoded = from_both(
        jnp.where(mine == 0, low, high), swap(jnp.where(mine == 0, high, low))
    )
    first_lot.advance()
    second_lot.advance()
    other_weights.advance()
    plan = self_plan(first_rows, pack_rows, width, True)
    grads = attend_back(
        plan,
        query,
        keys,
        values,
        self_extra,
        target_marks,
        self_mixed,
        grad_self_mixed,
        True,
    )
    grads = before(grads, first_lot, second_lot, other_weights)
    first_lot.advance()
    second_lot.advance()
    other_weights.advance()
    project = weight_grad(place, first, grads, True, slots=3)
    last = Steps(reduce_to_owner(*project, True, z))
    feed_in_grad, feed_out_grad = feed_shares((first_lot.held[0], second_lot.held[0]))
    grads = before(after_all(grads, feed_in_grad, feed_out_grad), last)
    last.advance()
    grad_tokens, sums_zero = finish(
        held, grads, halves, grad_after_self, norms, weights, width
    )
    grad_tokens = to_slots(grad_tokens)

    sums = jnp.concatenate([sums_zero[:2], sums_one[:2], sums_two[:2]])
    for bit in (1, 2, 4, 8):
        sums = sums + lax.ppermute(sums, "fsdp", pairs(bit))
    sums = sums + swap(sums)
    sums = lax.dynamic_slice_in_dim(sums, spot * part, part, 1)
    for _ in range(2):
        other_weights.advance()
    for _ in range(3):
        last.advance()
    others_share, project_share = (other_weights.held[0], last.held[0])

    return (
        result,
        grad_tokens,
        grad_encoded,
        columns(project_share, 0, 3),
        columns(others_share, 4, 5),
        columns(others_share, 3, 4),
        columns(others_share, 1, 3),
        columns(others_share, 0, 1),
        feed_in_grad,
        feed_out_grad,
        sums[0::2],
        sums[1:4:2],
        sums[5],
    )


def solution(mesh):
    chosen = whole_pack_body if whole_packs(mesh) else body
    return jax.shard_map(
        chosen,
        mesh=mesh,
        in_specs=(
            P(None, "fsdp", "ctx", None),
            P(None, "fsdp", "ctx", None),
            P(None, "fsdp", "ctx", None),
            P(None, "fsdp", None),
            P(None, "fsdp", None),
            P(None, "fsdp", None),
            P("fsdp", None),
            P("fsdp", None),
            P("fsdp", None),
            P("fsdp", None),
            P("fsdp", None),
            P("fsdp", None),
            P("fsdp", None),
            P(None, "fsdp"),
            P(None, "fsdp"),
        ),
        out_specs=(
            P(None, "fsdp", "ctx", None),
            P(None, "fsdp", "ctx", None),
            P(None, "fsdp", "ctx", None),
            P("fsdp", None),
            P("fsdp", None),
            P("fsdp", None),
            P("fsdp", None),
            P("fsdp", None),
            P("fsdp", None),
            P("fsdp", None),
            P(None, "fsdp"),
            P(None, "fsdp"),
            P("fsdp"),
        ),
        check_vma=False,
    )
```

```python
import functools
import math

import jax
import jax.numpy as jnp
from jax import lax
from jax.experimental import pallas as pl
from jax.experimental.pallas import tpu as pltpu
from jax.sharding import PartitionSpec as P

HEAD = 64


MASKED = -1e30


def as_sent(x):

    def short(part):
        return part.astype(jnp.bfloat16) if part.dtype == jnp.float32 else part

    return jax.tree.map(short, x)


def norm_apply(values, gain, bias):
    mean = jnp.mean(values, axis=-1, keepdims=True)
    centred = values - mean
    spread = jnp.mean(centred * centred, axis=-1, keepdims=True)
    return centred * lax.rsqrt(spread + 1e-05) * gain + bias


def gelu_exact(values):
    return jax.nn.gelu(values, approximate=False)


def docs_of(places, lengths):
    ends = jnp.cumsum(lengths)
    return jnp.sum((places[:, None] >= ends[None, :]).astype(jnp.int32), axis=1)


def split_heads(values):
    return values.reshape(values.shape[0], -1, HEAD)


def block_scores(query, pairs, allowed, start, count):
    model = query.shape[1]
    block = lax.dynamic_slice_in_dim(pairs, start, count, 0)
    scores = jnp.einsum(
        "qhd,khd->hqk",
        split_heads(query),
        split_heads(block[:, :model]),
        preferred_element_type=jnp.float32,
    )
    scores = jnp.where(allowed(start, count)[None], scores * HEAD ** (-0.5), MASKED)
    return (scores, block)


def log_mass(query, pairs, allowed, width):
    rows, model = query.shape
    heads = model // HEAD

    def step(index, carry):
        peak, total = carry
        scores, _ = block_scores(query, pairs, allowed, index * width, width)
        new_peak = jnp.maximum(peak, jnp.max(scores, axis=2))
        total = total * jnp.exp(peak - new_peak) + jnp.sum(
            jnp.exp(scores - new_peak[:, :, None]), axis=2
        )
        return (new_peak, total)

    begin = (jnp.full((heads, rows), MASKED, jnp.float32), jnp.zeros((heads, rows), jnp.float32))
    peak, total = lax.fori_loop(0, pairs.shape[0] // width, step, begin)
    return peak + jnp.log(total)


def attend_forward(query, pairs, allowed, width, log_total):
    rows, model = query.shape

    def step(index, mixed):
        scores, block = block_scores(query, pairs, allowed, index * width, width)
        probs = jnp.exp(scores - log_total[:, :, None]).astype(jnp.bfloat16)
        return mixed + jnp.einsum(
            "hqk,khd->qhd", probs, split_heads(block[:, model:]), preferred_element_type=jnp.float32
        )

    mixed = lax.fori_loop(
        0, pairs.shape[0] // width, step, jnp.zeros((rows, model // HEAD, HEAD), jnp.float32)
    )
    return mixed.reshape(rows, model).astype(jnp.bfloat16)


def score_grads(query, pairs, allowed, grad_mixed, log_total, start, count):
    model = query.shape[1]
    scores, block = block_scores(query, pairs, allowed, start, count)
    probs = jnp.exp(scores - log_total[:, :, None])
    grad_probs = jnp.einsum(
        "qhd,khd->hqk",
        split_heads(grad_mixed),
        split_heads(block[:, model:]),
        preferred_element_type=jnp.float32,
    )
    return (probs, grad_probs, block)


def attend_delta(query, pairs, allowed, grad_mixed, log_total, width):
    rows, model = query.shape

    def step(index, delta):
        probs, grad_probs, _ = score_grads(
            query, pairs, allowed, grad_mixed, log_total, index * width, width
        )
        return delta + jnp.sum(probs * grad_probs, axis=2)

    return lax.fori_loop(
        0, pairs.shape[0] // width, step, jnp.zeros((model // HEAD, rows), jnp.float32)
    )


def attend_query_grad(query, pairs, allowed, grad_mixed, log_total, delta, width):
    rows, model = query.shape

    def step(index, grad):
        probs, grad_probs, block = score_grads(
            query, pairs, allowed, grad_mixed, log_total, index * width, width
        )
        grad_scores = (probs * (grad_probs - delta[:, :, None])).astype(jnp.bfloat16)
        return grad + jnp.einsum(
            "hqk,khd->qhd",
            grad_scores,
            split_heads(block[:, :model]),
            preferred_element_type=jnp.float32,
        )

    grad = lax.fori_loop(
        0, pairs.shape[0] // width, step, jnp.zeros((rows, model // HEAD, HEAD), jnp.float32)
    )
    return (grad.reshape(rows, model) * HEAD ** (-0.5)).astype(jnp.bfloat16)


def key_terms(query, pairs, allowed, grad_mixed, log_total, delta, width, count):
    model = query.shape[1]
    step_width = math.gcd(count, width)

    def step(index, terms):
        probs, grad_probs, _ = score_grads(
            query, pairs, allowed, grad_mixed, log_total, index * step_width, step_width
        )
        grad_scores = (probs * (grad_probs - delta[:, :, None])).astype(jnp.bfloat16)
        grad_keys = jnp.einsum(
            "hqk,qhd->khd", grad_scores, split_heads(query), preferred_element_type=jnp.float32
        ) * HEAD ** (-0.5)
        grad_values = jnp.einsum(
            "hqk,qhd->khd",
            probs.astype(jnp.bfloat16),
            split_heads(grad_mixed),
            preferred_element_type=jnp.float32,
        )
        piece = jnp.concatenate(
            [grad_keys.reshape(step_width, model), grad_values.reshape(step_width, model)], axis=1
        )
        return lax.dynamic_update_slice_in_dim(terms, piece, index * step_width, 0)

    return lax.fori_loop(0, count // step_width, step, jnp.zeros((count, 2 * model), jnp.float32))


def body(
    tokens,
    encoded,
    cotangent,
    order,
    target_lengths,
    source_lengths,
    self_project,
    self_output,
    cross_query,
    cross_source,
    cross_output,
    feed_in,
    feed_out,
    norm_gain,
    norm_bias,
):
    micro = tokens.shape[0]
    rows = tokens.shape[2]
    model = tokens.shape[3]
    source_rows = encoded.shape[2]
    place = lax.axis_index("ctx")
    group = lax.axis_size("ctx")
    pack_total = rows * group
    source_total = source_rows * group
    self_width = math.gcd(pack_total, 512)
    cross_width = math.gcd(source_total, 512)
    results = []
    grad_values_all = []
    grad_encoded_all = []
    totals = ()
    for index in range(micro):
        attention_part = (
            lax.all_gather(self_project, "fsdp", axis=0, tiled=True),
            lax.all_gather(self_output, "fsdp", axis=0, tiled=True),
            lax.all_gather(cross_query, "fsdp", axis=0, tiled=True),
            lax.all_gather(cross_source, "fsdp", axis=0, tiled=True),
            lax.all_gather(cross_output, "fsdp", axis=0, tiled=True),
            lax.all_gather(norm_gain, "fsdp", axis=1, tiled=True),
            lax.all_gather(norm_bias, "fsdp", axis=1, tiled=True),
        )
        feed_part = (
            lax.all_gather(feed_in, "fsdp", axis=0, tiled=True),
            lax.all_gather(feed_out, "fsdp", axis=0, tiled=True),
        )
        weights = tuple(attention_part) + tuple(feed_part)
        (
            self_in_full,
            self_out_full,
            cross_query_full,
            cross_source_full,
            cross_out_full,
            gain_full,
            bias_full,
            feed_in_full,
            feed_out_full,
        ) = weights
        gains = gain_full.astype(jnp.float32)
        biases = bias_full.astype(jnp.float32)
        values = tokens[index, 0].astype(jnp.float32)
        source = encoded[index, 0]
        grad_out = cotangent[index, 0]
        places = order[index, 0]
        target_docs = docs_of(places, target_lengths[index, 0])
        query_places = lax.dynamic_slice_in_dim(places, place * rows, rows)
        query_docs = lax.dynamic_slice_in_dim(target_docs, place * rows, rows)
        source_docs = docs_of(jnp.arange(source_total, dtype=jnp.int32), source_lengths[index, 0])

        def self_allowed(start, count):
            key_docs = lax.dynamic_slice_in_dim(target_docs, start, count)
            key_places = lax.dynamic_slice_in_dim(places, start, count)
            return (query_docs[:, None] == key_docs[None, :]) & (
                key_places[None, :] <= query_places[:, None]
            )

        def cross_allowed(start, count):
            return (
                query_docs[:, None] == lax.dynamic_slice_in_dim(source_docs, start, count)[None, :]
            )

        first = norm_apply(values, gains[0], biases[0]).astype(jnp.bfloat16)
        query = jnp.dot(first, self_in_full[:, :model], preferred_element_type=jnp.float32).astype(
            jnp.bfloat16
        )
        local_pairs = jnp.dot(
            first, self_in_full[:, model:], preferred_element_type=jnp.float32
        ).astype(jnp.bfloat16)
        self_pairs = lax.all_gather(local_pairs, "ctx", axis=0, tiled=True)
        self_total = log_mass(query, self_pairs, self_allowed, self_width)
        self_mixed = attend_forward(query, self_pairs, self_allowed, self_width, self_total)
        after_self = values + jnp.dot(self_mixed, self_out_full, preferred_element_type=jnp.float32)
        second = norm_apply(after_self, gains[1], biases[1]).astype(jnp.bfloat16)
        cross_queries = jnp.dot(
            second, cross_query_full, preferred_element_type=jnp.float32
        ).astype(jnp.bfloat16)
        cross_local = jnp.dot(source, cross_source_full, preferred_element_type=jnp.float32).astype(
            jnp.bfloat16
        )
        cross_pairs = lax.all_gather(cross_local, "ctx", axis=0, tiled=True)
        cross_total = log_mass(cross_queries, cross_pairs, cross_allowed, cross_width)
        cross_mixed = attend_forward(
            cross_queries, cross_pairs, cross_allowed, cross_width, cross_total
        )
        after_cross = after_self + jnp.dot(
            cross_mixed, cross_out_full, preferred_element_type=jnp.float32
        )
        third = norm_apply(after_cross, gains[2], biases[2]).astype(jnp.bfloat16)
        hidden = jnp.dot(third, feed_in_full, preferred_element_type=jnp.float32)
        active = gelu_exact(hidden).astype(jnp.bfloat16)
        result = (
            after_cross + jnp.dot(active, feed_out_full, preferred_element_type=jnp.float32)
        ).astype(jnp.bfloat16)
        grad_feed_out = jnp.einsum(
            "rf,rd->fd", active, grad_out, preferred_element_type=jnp.float32
        )
        grad_active = jnp.einsum(
            "rd,fd->rf", grad_out, feed_out_full, preferred_element_type=jnp.float32
        ).astype(jnp.bfloat16)
        _, gelu_pull = jax.vjp(gelu_exact, hidden)
        grad_hidden = gelu_pull(grad_active.astype(jnp.float32))[0].astype(jnp.bfloat16)
        grad_feed_in = jnp.einsum(
            "rd,rf->df", third, grad_hidden, preferred_element_type=jnp.float32
        )
        grad_third = jnp.einsum(
            "rf,df->rd", grad_hidden, feed_in_full, preferred_element_type=jnp.float32
        )
        _, norm_pull = jax.vjp(norm_apply, after_cross, gains[2], biases[2])
        norm_part, gain_two, bias_two = norm_pull(grad_third)
        grad_after_cross = grad_out.astype(jnp.float32) + norm_part
        cross_branch = grad_after_cross.astype(jnp.bfloat16)
        grad_cross_output = jnp.einsum(
            "rd,re->de", cross_mixed, cross_branch, preferred_element_type=jnp.float32
        )
        grad_cross_mixed = jnp.einsum(
            "re,de->rd", cross_branch, cross_out_full, preferred_element_type=jnp.float32
        ).astype(jnp.bfloat16)
        cross_delta = attend_delta(
            cross_queries, cross_pairs, cross_allowed, grad_cross_mixed, cross_total, cross_width
        )
        grad_cross_queries = attend_query_grad(
            cross_queries,
            cross_pairs,
            cross_allowed,
            grad_cross_mixed,
            cross_total,
            cross_delta,
            cross_width,
        )
        grad_source = lax.psum_scatter(
            key_terms(
                cross_queries,
                cross_pairs,
                cross_allowed,
                grad_cross_mixed,
                cross_total,
                cross_delta,
                cross_width,
                source_rows * lax.axis_size("ctx"),
            ).astype(jnp.bfloat16),
            "ctx",
            scatter_dimension=0,
            tiled=True,
        )
        grad_cross_source = jnp.einsum(
            "sd,se->de", source, grad_source, preferred_element_type=jnp.float32
        )
        grad_encoded = jnp.einsum(
            "se,de->sd", grad_source, cross_source_full, preferred_element_type=jnp.float32
        ).astype(jnp.bfloat16)
        grad_cross_query = jnp.einsum(
            "rd,re->de", second, grad_cross_queries, preferred_element_type=jnp.float32
        )
        grad_second = jnp.einsum(
            "re,de->rd", grad_cross_queries, cross_query_full, preferred_element_type=jnp.float32
        )
        _, norm_pull = jax.vjp(norm_apply, after_self, gains[1], biases[1])
        norm_part, gain_one, bias_one = norm_pull(grad_second)
        grad_after_self = grad_after_cross + norm_part
        self_branch = grad_after_self.astype(jnp.bfloat16)
        grad_self_output = jnp.einsum(
            "rd,re->de", self_mixed, self_branch, preferred_element_type=jnp.float32
        )
        grad_self_mixed = jnp.einsum(
            "re,de->rd", self_branch, self_out_full, preferred_element_type=jnp.float32
        ).astype(jnp.bfloat16)
        self_delta = attend_delta(
            query, self_pairs, self_allowed, grad_self_mixed, self_total, self_width
        )
        grad_query = attend_query_grad(
            query, self_pairs, self_allowed, grad_self_mixed, self_total, self_delta, self_width
        )
        grad_pairs = lax.psum_scatter(
            key_terms(
                query,
                self_pairs,
                self_allowed,
                grad_self_mixed,
                self_total,
                self_delta,
                self_width,
                rows * lax.axis_size("ctx"),
            ).astype(jnp.bfloat16),
            "ctx",
            scatter_dimension=0,
            tiled=True,
        )
        grad_projected = jnp.concatenate([grad_query, grad_pairs], axis=1)
        grad_self_project = jnp.einsum(
            "rd,re->de", first, grad_projected, preferred_element_type=jnp.float32
        )
        grad_first = jnp.einsum(
            "re,de->rd", grad_projected, self_in_full, preferred_element_type=jnp.float32
        )
        _, norm_pull = jax.vjp(norm_apply, values, gains[0], biases[0])
        norm_part, gain_zero, bias_zero = norm_pull(grad_first)
        grad_values = (grad_after_self + norm_part).astype(jnp.bfloat16)
        grads = (
            grad_self_project,
            grad_self_output,
            grad_cross_query,
            grad_cross_source,
            grad_cross_output,
            grad_feed_in,
            grad_feed_out,
            jnp.stack([gain_zero, gain_one, gain_two]),
            jnp.stack([bias_zero, bias_one, bias_two]),
        )
        result, grad_values, grad_encoded, grads = (result, grad_values, grad_encoded, grads)
        totals = (
            grads
            if index == 0
            else tuple((jnp.add(left, right) for left, right in zip(totals, grads)))
        )
        results.append(result)
        grad_values_all.append(grad_values)
        grad_encoded_all.append(grad_encoded)
    shares = (
        lax.psum_scatter(
            totals[0].astype(jnp.bfloat16), "fsdp", scatter_dimension=0, tiled=True
        ).astype(jnp.float32),
        lax.psum_scatter(
            totals[1].astype(jnp.bfloat16), "fsdp", scatter_dimension=0, tiled=True
        ).astype(jnp.float32),
        lax.psum_scatter(
            totals[2].astype(jnp.bfloat16), "fsdp", scatter_dimension=0, tiled=True
        ).astype(jnp.float32),
        lax.psum_scatter(
            totals[3].astype(jnp.bfloat16), "fsdp", scatter_dimension=0, tiled=True
        ).astype(jnp.float32),
        lax.psum_scatter(
            totals[4].astype(jnp.bfloat16), "fsdp", scatter_dimension=0, tiled=True
        ).astype(jnp.float32),
        lax.psum_scatter(
            totals[5].astype(jnp.bfloat16), "fsdp", scatter_dimension=0, tiled=True
        ).astype(jnp.float32),
        lax.psum_scatter(
            totals[6].astype(jnp.bfloat16), "fsdp", scatter_dimension=0, tiled=True
        ).astype(jnp.float32),
        lax.psum_scatter(
            totals[7].astype(jnp.bfloat16), "fsdp", scatter_dimension=1, tiled=True
        ).astype(jnp.float32),
        lax.psum_scatter(
            totals[8].astype(jnp.bfloat16), "fsdp", scatter_dimension=1, tiled=True
        ).astype(jnp.float32),
    )
    totals = tuple(
        jax.tree.map(lambda part: part.astype(jnp.float32), lax.psum(as_sent(tuple(shares)), "ctx"))
    )
    output = jnp.stack(results)[:, None]
    grad_tokens = jnp.stack(grad_values_all)[:, None]
    grad_source_rows = jnp.stack(grad_encoded_all)[:, None]
    return (
        output,
        grad_tokens,
        grad_source_rows,
        totals[0],
        totals[1],
        totals[2],
        totals[3],
        totals[4],
        totals[5],
        totals[6],
        totals[7],
        totals[8][:2],
        totals[8][2],
    )


BIG = 1e30
SCALE2 = HEAD ** (-0.5) * math.log2(math.e)
NT = (((1,), (1,)), ((), ()))
TN = (((0,), (0,)), ((), ()))
NN = (((1,), (0,)), ((), ()))


def dot(left, right, dims=NN):
    return lax.dot_general(left, right, dims, preferred_element_type=jnp.float32)


def lanes(rows):
    return lax.broadcasted_iota(jnp.int32, (rows, 128), 1)


def parts(x):
    hi = x.astype(jnp.bfloat16)
    rest = x - hi.astype(jnp.float32)
    mid = rest.astype(jnp.bfloat16)
    lo = (rest - mid.astype(jnp.float32)).astype(jnp.bfloat16)
    return (hi, mid, lo)


def spread(x, base):
    hi, mid, lo = parts(x)
    lane = lanes(x.shape[0]) % HEAD
    return jnp.where(lane == 4, hi, jnp.where(lane == 5, mid, jnp.where(lane == 6, lo, base)))


def two_heads(ref, own, other):
    left = lanes(own.shape[0]) < HEAD
    ref[0] = jnp.where(left, own, other)
    ref[1] = jnp.where(left, other, own)


def tail_masked(scores, rows):
    width = scores.shape[1] - rows
    row = lax.broadcasted_iota(jnp.int32, (rows, rows), 0)
    column = lax.broadcasted_iota(jnp.int32, (rows, rows), 1)
    tail = jnp.where(column > row, -BIG, scores[:, width:])
    return tail if width == 0 else jnp.concatenate([scores[:, :width], tail], axis=1)


def attend_kernel(plan, q_ref, k_ref, v_ref, qd_ref, kd_ref, out_ref, extra_ref, keys, values):
    two_heads(keys, k_ref[...], kd_ref[...])
    two_heads(values, v_ref[...], jnp.ones_like(v_ref))

    def scores_of(item):
        q0, q1, k0, k1, diagonal = item
        left = lanes(q1 - q0) < HEAD
        q, qd = (q_ref[q0:q1], qd_ref[q0:q1])
        pair = [dot(jnp.where(left == (h == 0), q, qd), keys[h, k0:k1], NT) for h in range(2)]
        return [tail_masked(s, q1 - q0) for s in pair] if diagonal else pair

    following = scores_of(plan[0])
    for index, (q0, q1, k0, k1, _) in enumerate(plan):
        scores = following
        following = scores_of(plan[index + 1]) if index + 1 < len(plan) else None
        left = lanes(q1 - q0) < HEAD
        mixed, tops = ([], [])
        for h in range(2):
            top = jnp.max(scores[h], axis=1, keepdims=True)
            probs = jnp.exp2((scores[h] - top) * SCALE2).astype(jnp.bfloat16)
            mixed.append(dot(probs, values[h, k0:k1]))
            tops.append(top)
        mass = jnp.where(left, mixed[1], mixed[0])
        numer = jnp.where(left, mixed[0], mixed[1])
        out_ref[q0:q1] = (numer / pltpu.roll(mass, HEAD, 1)).astype(jnp.bfloat16)
        top = jnp.where(left, tops[1], tops[0])
        extra_ref[q0:q1] = spread(-(top + HEAD**0.5 * jnp.log(mass)), qd_ref[q0:q1])


def attend_back_kernel(
    plan,
    q_ref,
    k_ref,
    v_ref,
    extra_ref,
    kd_ref,
    out_ref,
    g_ref,
    *refs,
):
    *outs, keys, values, queries, grads, g_t, q_t, dk_t, dv_t = refs
    if len(outs) == 1:
        dq_ref, dk_ref, dv_ref = (outs[0].at[i] for i in range(3))
    else:
        dq_ref, dk_ref, dv_ref = (outs[0], outs[1].at[0], outs[1].at[1])
    two_heads(keys, k_ref[...], kd_ref[...])
    two_heads(values, v_ref[...], jnp.ones_like(v_ref))
    two_heads(queries, q_ref[...], extra_ref[...])
    square = (128, 128)
    row, column = (lax.broadcasted_iota(jnp.int32, square, axis) < HEAD for axis in (0, 1))
    across = jnp.where(row != column, 1.0, 0.0).astype(jnp.bfloat16)
    g = g_ref[...]
    terms = parts(g.astype(jnp.float32) * out_ref[...].astype(jnp.float32))
    delta = sum(dot(term, across) for term in terms)
    two_heads(grads, g, spread(-delta, jnp.zeros_like(g)))
    g_t[...] = g.T
    q_t[...] = q_ref[...].T
    dk_t[...] = jnp.zeros_like(dk_t)
    dv_t[...] = jnp.zeros_like(dv_t)
    for q0, q1, k0, k1, diagonal in plan:
        left = lanes(q1 - q0) < HEAD
        pair = []
        for h in range(2):
            s = dot(queries[h, q0:q1], keys[h, k0:k1], NT)
            s = tail_masked(s, q1 - q0) if diagonal else s
            pair.append((s, dot(grads[h, q0:q1], values[h, k0:k1], NT)))
        dqs = []
        for h, (s, grad_probs) in enumerate(pair):
            probs = jnp.exp2(s * SCALE2)
            ds = (probs * grad_probs).astype(jnp.bfloat16)
            head = slice(h * HEAD, h * HEAD + HEAD)
            dv_t[head, k0:k1] += dot(g_t[head, q0:q1], probs.astype(jnp.bfloat16))
            dk_t[head, k0:k1] += dot(q_t[head, q0:q1], ds)
            dqs.append(dot(ds, k_ref[k0:k1]))
        dq_ref[q0:q1] = (jnp.where(left, dqs[0], dqs[1]) * HEAD ** (-0.5)).astype(jnp.bfloat16)
    dk_ref[...] = (dk_t[...].T * HEAD ** (-0.5)).astype(jnp.bfloat16)
    dv_ref[...] = dv_t[...].T.astype(jnp.bfloat16)


def pair_of_heads(rows):
    return pl.BlockSpec((rows, 128), lambda i: (0, i))


def all_of(rows):
    return pl.BlockSpec((rows, 128), lambda i: (0, 0))


def small_cost():
    return pl.CostEstimate(flops=1 << 10, bytes_accessed=1 << 10, transcendentals=0)


def attend(plan, q, k, v, qd, kd):
    nq, nk, model = (q.shape[0], k.shape[0], q.shape[1])
    shape = jax.ShapeDtypeStruct((nq, model), jnp.bfloat16)
    return pl.pallas_call(
        functools.partial(attend_kernel, plan),
        grid=(model // 128,),
        in_specs=[pair_of_heads(n) for n in (nq, nk, nk)] + [all_of(nq), all_of(nk)],
        out_specs=[pair_of_heads(nq)] * 2,
        out_shape=[shape] * 2,
        scratch_shapes=[pltpu.VMEM((2, nk, 128), jnp.bfloat16)] * 2,
        compiler_params=pltpu.CompilerParams(vmem_limit_bytes=58 * 2**20),
        cost_estimate=small_cost(),
    )(q, k, v, qd, kd)


def stacked(count, rows):
    return pl.BlockSpec((count, rows, 128), lambda i: (0, 0, i))


def attend_back(plan, q, k, v, extra, kd, out, g, together):
    nq, nk, model = (q.shape[0], k.shape[0], q.shape[1])
    if together:
        specs, shapes = ([stacked(3, nq)], [(3, nq, model)])
    else:
        specs, shapes = ([pair_of_heads(nq), stacked(2, nk)], [(nq, model), (2, nk, model)])
    outs = pl.pallas_call(
        functools.partial(attend_back_kernel, plan),
        grid=(model // 128,),
        in_specs=[pair_of_heads(n) for n in (nq, nk, nk, nq)]
        + [all_of(nk)]
        + [pair_of_heads(nq)] * 2,
        out_specs=specs,
        out_shape=[jax.ShapeDtypeStruct(shape, jnp.bfloat16) for shape in shapes],
        scratch_shapes=[pltpu.VMEM((2, nk, 128), jnp.bfloat16)] * 2
        + [pltpu.VMEM((2, nq, 128), jnp.bfloat16)] * 2
        + [pltpu.VMEM((128, nq), jnp.bfloat16)] * 2
        + [pltpu.VMEM((128, nk), jnp.float32)] * 2,
        compiler_params=pltpu.CompilerParams(vmem_limit_bytes=58 * 2**20),
        cost_estimate=small_cost(),
    )(q, k, v, extra, kd, out, g)
    return outs[0] if together else outs


def self_plan(first, total, tile):
    return [
        (start, start + tile, low, start + tile, True)
        for low, high in ((0, first), (first, total))
        for start in range(low, high, tile)
    ]


def cross_plan(first, total, reach, source, tile):
    return [
        (start, start + tile, 0, reach if start < first else source, False)
        for start in range(0, total, tile)
    ]


def query_marks(docs):
    lane = jnp.arange(128) % HEAD
    return jnp.where(docs[:, None] == lane[None, :], BIG, 0.0).astype(jnp.bfloat16)


def key_marks(docs, count):
    lane = (jnp.arange(128) % HEAD)[None, :]
    other = jnp.where(docs[:, None] == lane, 0.0, -1.0)
    return jnp.where(lane < count, other, jnp.where(lane < 7, 1.0, 0.0)).astype(jnp.bfloat16)


MODEL = 1024
TILE = 512


def wide(values):
    return values.astype(jnp.float32)


def short(values):
    return values.astype(jnp.bfloat16)


def gathered(ref):
    return ref[...].reshape(-1, ref.shape[-1])


def once(shape, index):
    return pl.BlockSpec(shape, index, pipeline_mode=pl.Buffered(1))


def weight_at(slot):
    return once((16, 64, MODEL), lambda *_: (0, slot, 0))


def norm_rows():
    return once((8, MODEL), lambda *_: (0, 0))


def by_rows(count, width=MODEL):
    return pl.BlockSpec((count, width), lambda i, *_: (i, 0))


def found_rows(count):
    return pl.BlockSpec((count, MODEL), lambda i, held, *_: (held[i], 0))


def sums_out():
    return pl.BlockSpec((8, MODEL), lambda *_: (0, 0))


def struct(shape, kind):
    return jax.ShapeDtypeStruct(shape, kind)


def spread_of(values):
    mean = jnp.mean(values, axis=-1, keepdims=True)
    centred = values - mean
    scale = lax.rsqrt(jnp.mean(centred * centred, axis=-1, keepdims=True) + 1e-05)
    return (centred * scale, scale)


def norm_of(values, norm_ref, k):
    hat, _ = spread_of(values)
    return short(hat * norm_ref[k : k + 1] + norm_ref[3 + k : 4 + k])


def norm_back(values, grad, norm_ref, k, sums_ref):
    hat, scale = spread_of(values)
    each = grad * norm_ref[k : k + 1]
    inner = each - jnp.mean(each, axis=-1, keepdims=True)
    inner = inner - hat * jnp.mean(each * hat, axis=-1, keepdims=True)
    sums_ref[0:1] += jnp.sum(grad * hat, axis=0, keepdims=True)
    sums_ref[1:2] += jnp.sum(grad, axis=0, keepdims=True)
    return scale * inner


def call(kernel, grid, in_specs, out_specs, out_shape, flops, scratch=(), prefetch=0, aliases=None):
    return pl.pallas_call(
        kernel,
        grid_spec=pltpu.PrefetchScalarGridSpec(
            num_scalar_prefetch=prefetch,
            grid=grid,
            in_specs=in_specs,
            out_specs=out_specs,
            scratch_shapes=list(scratch),
        ),
        out_shape=out_shape,
        input_output_aliases=aliases or {},
        compiler_params=pltpu.CompilerParams(vmem_limit_bytes=58 * 2**20),
        cost_estimate=small_cost(),
    )


def pack_kernel(*refs):
    attention_ref, feed_ref = refs[-2:]
    self_in, self_out, cross_q, cross_s, cross_out, feed_in, feed_out, norms = refs[:-2]
    rows = self_in.shape[0]
    slot = 0
    for ref in (self_in, self_out, cross_q, cross_s, cross_out):
        for start in range(0, ref.shape[1], MODEL):
            attention_ref[slot * rows : (slot + 1) * rows] = ref[:, start : start + MODEL]
            slot += 1
    attention_ref[slot * rows :] = norms[...]
    piece = feed_out.shape[0] // 2
    for lot in range(2):
        for owner in range(16):
            column = (2 * owner + lot) * piece
            slot, spot = (2 * lot + owner // 8, owner % 8 * piece)
            feed_ref[slot * rows : (slot + 1) * rows, spot : spot + piece] = feed_in[
                :, column : column + piece
            ]
    feed_ref[4 * rows : 8 * rows] = feed_out[...]
    feed_ref[8 * rows :] = jnp.zeros_like(norms)


def pack(weights, norms):
    arrays = tuple(weights) + (norms,)
    out = struct((528, MODEL), jnp.bfloat16)
    return call(
        pack_kernel,
        (1,),
        [once(a.shape, lambda i: (0, 0)) for a in arrays],
        [once(out.shape, lambda i: (0, 0))] * 2,
        [out] * 2,
        1 << 20,
    )(*arrays)


def enter_kernel(held, tokens_ref, norm_ref, wq, wk, wv, first_ref, q_ref, k_ref, v_ref):
    first = norm_of(wide(tokens_ref[...]), norm_ref, 0)
    first_ref[...] = first
    for weight, out in ((wq, q_ref), (wk, k_ref), (wv, v_ref)):
        out[...] = short(dot(first, gathered(weight)))


def enter(held, tokens, norms, weights, width):
    shape = struct(tokens.shape, jnp.bfloat16)
    return call(
        enter_kernel,
        (tokens.shape[0] // width,),
        [found_rows(width), norm_rows()] + [weight_at(i) for i in range(3)],
        [by_rows(width)] * 4,
        [shape] * 4,
        6 * tokens.size * MODEL,
        prefetch=1,
    )(held, tokens, norms, weights, weights, weights)


def source_kernel(source_ref, wk, wv, k_ref, v_ref):
    source = source_ref[...]
    k_ref[...] = short(dot(source, gathered(wk)))
    v_ref[...] = short(dot(source, gathered(wv)))


def source_pairs(source, weights, width):
    return call(
        source_kernel,
        (source.shape[0] // width,),
        [by_rows(width), weight_at(5), weight_at(6)],
        [by_rows(width)] * 2,
        [struct(source.shape, jnp.bfloat16)] * 2,
        4 * source.size * MODEL,
    )(source, weights, weights)


def between_kernel(held, mixed_ref, tokens_ref, norm_ref, wo, wq, after_ref, second_ref, q_ref):
    after = wide(tokens_ref[...]) + dot(mixed_ref[...], gathered(wo))
    after_ref[...] = after
    second = norm_of(after, norm_ref, 1)
    second_ref[...] = second
    q_ref[...] = short(dot(second, gathered(wq)))


def between(held, mixed, tokens, norms, weights, width):
    return call(
        between_kernel,
        (mixed.shape[0] // width,),
        [by_rows(width), found_rows(width), norm_rows(), weight_at(3), weight_at(4)],
        [by_rows(width)] * 3,
        [struct(mixed.shape, kind) for kind in (jnp.float32, jnp.bfloat16, jnp.bfloat16)],
        4 * mixed.size * MODEL,
        prefetch=1,
    )(held, mixed, tokens, norms, weights, weights)


def before_feed_kernel(
    held, mixed_ref, base_ref, own_ref, other_ref, norm_ref, wo, after_ref, third_ref, grad_ref
):
    after = base_ref[...] + dot(mixed_ref[...], gathered(wo))
    after_ref[...] = after
    third_ref[...] = norm_of(after, norm_ref, 2)
    own = held[pl.program_id(0)] < 2

    @pl.when(own)
    def _():
        grad_ref[...] = own_ref[...]

    @pl.when(jnp.logical_not(own))
    def _():
        grad_ref[...] = other_ref[...]


def before_feed(held, mixed, base, own, other, norms, weights, width):
    return call(
        before_feed_kernel,
        (mixed.shape[0] // width,),
        [
            by_rows(width),
            by_rows(width),
            pl.BlockSpec((width, MODEL), lambda i, held: (jnp.minimum(held[i], 1), 0)),
            pl.BlockSpec((width, MODEL), lambda i, held: (jnp.maximum(held[i] - 2, 0), 0)),
            norm_rows(),
            weight_at(7),
        ],
        [by_rows(width)] * 3,
        [struct(mixed.shape, kind) for kind in (jnp.float32, jnp.bfloat16, jnp.bfloat16)],
        2 * mixed.size * MODEL,
        prefetch=1,
    )(held, mixed, base, own, other, norms, weights)


def gelu_terms(hidden):
    bell = jnp.exp2(hidden * hidden * (-0.5 * math.log2(math.e)))
    t = 1.0 / (1.0 + (0.3275911 / math.sqrt(2.0)) * jnp.abs(hidden))
    series = 1.061405429
    for term in (-1.453152027, 1.421413741, -0.284496736, 0.254829592):
        series = series * t + term
    tail = 0.5 * series * t * bell
    return (jnp.where(hidden < 0, tail, 1.0 - tail), bell * (1.0 / math.sqrt(2.0 * math.pi)))


def deal(place_ref, turned, keep_ref, send_ref, pieces):
    for own in range(2):

        @pl.when(place_ref[0] == own)
        def _(own=own):
            for core, x, y, index, value in pieces:
                rel_x = jnp.bitwise_xor(place_ref[1], x)
                rel_y = jnp.bitwise_xor(place_ref[2], y)
                spot = (rel_y, rel_x) if turned else (rel_x, rel_y)
                ref = keep_ref if core == own else send_ref
                ref[spot + index] = value


def shard_pieces(product, slot, *rest):
    pieces = []
    for owner in range(16):
        for y in range(2):
            start = owner * 64 + y * 32
            index = (owner // 4, slot) + rest
            value = short(product[start : start + 32])
            pieces.append((owner % 2, owner // 2 % 2, y, index, value))
    return pieces


def feed_kernel(
    place_ref,
    third_ref,
    grad_ref,
    win_ref,
    wout_ref,
    out_ref,
    back_ref,
    keep_a,
    send_a,
    keep_b,
    send_b,
    third_t,
    active_ref,
    hidden_ref,
):
    step = pl.program_id(0)

    @pl.when(step == 0)
    def _():
        third_t[...] = third_ref[...].T
        out_ref[...] = jnp.zeros_like(out_ref)
        back_ref[...] = jnp.zeros_like(back_ref)

    win, wout = (gathered(win_ref), gathered(wout_ref))
    rows = third_ref.shape[0]
    lots = [slice(start, start + TILE) for start in range(0, rows, TILE)]

    def enter(lot):
        return (dot(third_ref[lot], win), dot(grad_ref[lot], wout, NT))

    def leave(lot, hidden, grad):
        mass, bell = gelu_terms(hidden)
        active = short(hidden * mass)
        grad = short((mass + hidden * bell) * wide(short(grad)))
        active_ref[lot] = active
        hidden_ref[lot] = grad
        out_ref[lot] += dot(active, wout)
        back_ref[lot] += dot(grad, win, NT)

    ready = enter(lots[0])
    for index, lot in enumerate(lots):
        following = enter(lots[index + 1]) if index + 1 < len(lots) else None
        leave(lot, *ready)
        ready = following
    grad_out = short(dot(active_ref[...], grad_ref[...], TN))
    grad_in = short(dot(third_t[...], hidden_ref[...]))
    turn = lax.rem(step, 4)
    side = pl.ds(pl.multiple_of(lax.rem(turn, 2) * TILE, TILE), TILE)
    pieces = shard_pieces(grad_in, turn // 2, slice(None), side)
    for owner in range(4):
        for y in range(2):
            for half in range(2):
                start = owner * 128 + y * 64 + 32 * half
                value = grad_out[start : start + 32]
                pieces.append((owner % 2, owner // 2, y, (turn, 2 + half), value))

    @pl.when(step < 4)
    def _():
        deal(place_ref, False, keep_a, send_a, pieces)

    @pl.when(step >= 4)
    def _():
        deal(place_ref, True, keep_b, send_b, pieces)


def feed(place, third, grad, weights):
    rows = third.shape[0]
    full = struct((rows, MODEL), jnp.float32)
    buffer = struct((2, 2, 4, 4, 32, MODEL), jnp.bfloat16)
    out, back, *lots = call(
        feed_kernel,
        (8,),
        [
            once((rows, MODEL), lambda t, place: (0, 0)),
            once((rows, MODEL), lambda t, place: (0, 0)),
            pl.BlockSpec((16, 64, TILE), lambda t, place: (0, t // 2, t % 2)),
            pl.BlockSpec((4, 128, MODEL), lambda t, place: (t % 4, 2 + t // 4, 0)),
        ],
        [once((rows, MODEL), lambda t, place: (0, 0))] * 2
        + [once(buffer.shape, lambda t, place: (0, 0, 0, 0, 0, 0))] * 4,
        [full, full] + [buffer] * 4,
        24 * rows * MODEL * 2048,
        scratch=[
            pltpu.VMEM((MODEL, rows), jnp.bfloat16),
            pltpu.VMEM((rows, TILE), jnp.bfloat16),
            pltpu.VMEM((rows, TILE), jnp.bfloat16),
        ],
        prefetch=1,
    )(place, third, grad, weights, weights)
    return out, back, lots[:2], lots[2:]


def clear(*refs):
    @pl.when(pl.program_id(0) == 0)
    def _():
        for ref in refs:
            ref[...] = jnp.zeros_like(ref)


def add_product(total_ref, left, right):
    total_ref[...] += dot(left, right, TN)


def at_end(store):
    pl.when(pl.program_id(0) == pl.num_programs(0) - 1)(store)


def buffer_of(slots):
    return struct((2, 2, 4, slots, 32, MODEL), jnp.bfloat16)


def slots_at(slots):
    return once((2, 2, 4, slots, 32, MODEL), lambda *_: (0,) * 6)


def after_feed_kernel(
    held,
    place,
    after_ref,
    out_ref,
    back_ref,
    grad_ref,
    cross_ref,
    norm_ref,
    wo,
    result_ref,
    total_ref,
    mixed_ref,
    sums_ref,
    keep_ref,
    send_ref,
    weight_ref,
):
    clear(sums_ref, weight_ref)
    after = after_ref[...]
    result_ref[...] = short(after + out_ref[...])
    part = norm_back(after, back_ref[...], norm_ref, 2, sums_ref)
    total = wide(grad_ref[...]) + part
    total_ref[...] = total
    branch = short(total)
    mixed_ref[...] = short(dot(branch, gathered(wo), NT))
    add_product(weight_ref, cross_ref[...], branch)
    at_end(lambda: deal(place, False, keep_ref, send_ref, shard_pieces(weight_ref, 0)))


def after_feed(held, place, after, out, back, grad, mixed, norms, weights, width):
    narrow = struct(after.shape, jnp.bfloat16)
    full = struct(after.shape, jnp.float32)
    return call(
        after_feed_kernel,
        (after.shape[0] // width,),
        [by_rows(width)] * 5 + [norm_rows(), weight_at(7)],
        [found_rows(width)] + [by_rows(width)] * 2 + [sums_out()] + [slots_at(1)] * 2,
        [narrow, full, narrow, struct((8, MODEL), jnp.float32)] + [buffer_of(1)] * 2,
        4 * after.size * MODEL,
        scratch=[pltpu.VMEM((MODEL, MODEL), jnp.float32)],
        prefetch=2,
    )(held, place, after, out, back, grad, mixed, norms, weights)


def middle_kernel(
    place,
    grad_ref,
    second_ref,
    after_ref,
    base_ref,
    self_ref,
    norm_ref,
    wq,
    wo,
    *refs,
):
    total_ref, mixed_ref, sums_ref, keep_ref, send_ref, weight_q, weight_o = refs
    clear(sums_ref, weight_q, weight_o)
    grad_q = grad_ref[...]
    grad = dot(grad_q, gathered(wq), NT)
    add_product(weight_q, second_ref[...], grad_q)
    total = base_ref[...] + norm_back(after_ref[...], grad, norm_ref, 1, sums_ref)
    total_ref[...] = total
    branch = short(total)
    mixed_ref[...] = short(dot(branch, gathered(wo), NT))
    add_product(weight_o, self_ref[...], branch)

    @at_end
    def _():
        deal(place, False, keep_ref, send_ref, shard_pieces(weight_q, 0))
        deal(place, False, keep_ref, send_ref, shard_pieces(weight_o, 1))


def middle(place, grad, second, after, base, mixed, norms, weights, width):
    narrow = struct(after.shape, jnp.bfloat16)
    return call(
        middle_kernel,
        (after.shape[0] // width,),
        [by_rows(width)] * 5 + [norm_rows(), weight_at(4), weight_at(3)],
        [by_rows(width)] * 2 + [sums_out()] + [slots_at(2)] * 2,
        [struct(after.shape, jnp.float32), narrow, struct((8, MODEL), jnp.float32)]
        + [buffer_of(2)] * 2,
        8 * after.size * MODEL,
        scratch=[pltpu.VMEM((MODEL, MODEL), jnp.float32)] * 2,
        prefetch=1,
    )(place, grad, second, after, base, mixed, norms, weights, weights)


def finish_kernel(
    held,
    place,
    grads_ref,
    first_ref,
    tokens_ref,
    base_ref,
    norm_ref,
    wq,
    wk,
    wv,
    result_ref,
    sums_ref,
    keep_ref,
    send_ref,
    weight_ref,
):
    clear(sums_ref, weight_ref)
    grad = sum(dot(grads_ref[i], gathered(w), NT) for i, w in enumerate((wq, wk, wv)))
    part = norm_back(wide(tokens_ref[...]), grad, norm_ref, 0, sums_ref)
    result_ref[...] = short(base_ref[...] + part)
    first = first_ref[...].T
    for i in range(3):
        weight_ref[i] += dot(first, grads_ref[i])

    @at_end
    def _():
        for i in range(3):
            deal(place, False, keep_ref, send_ref, shard_pieces(weight_ref.at[i], i))


def finish(held, place, grads, first, tokens, base, norms, weights, width):
    return call(
        finish_kernel,
        (base.shape[0] // width,),
        [
            pl.BlockSpec((3, width, MODEL), lambda i, *_: (0, i, 0)),
            by_rows(width),
            found_rows(width),
            by_rows(width),
            norm_rows(),
        ]
        + [weight_at(i) for i in range(3)],
        [found_rows(width), sums_out()] + [slots_at(3)] * 2,
        [struct(base.shape, jnp.bfloat16), struct((8, MODEL), jnp.float32)]
        + [buffer_of(3)] * 2,
        12 * base.size * MODEL,
        scratch=[pltpu.VMEM((3, MODEL, MODEL), jnp.float32)],
        prefetch=2,
    )(held, place, grads, first, tokens, base, norms, weights, weights, weights)


def source_back_kernel(
    place, grads_ref, source_ref, wk, wv, out_ref, keep_ref, send_ref, weight_ref
):
    clear(weight_ref)
    source = source_ref[...].T
    for i in range(2):
        weight_ref[i] += dot(source, grads_ref[i])
    grad = dot(grads_ref[0], gathered(wk), NT) + dot(grads_ref[1], gathered(wv), NT)
    out_ref[...] = short(grad)

    @at_end
    def _():
        for i in range(2):
            deal(place, False, keep_ref, send_ref, shard_pieces(weight_ref.at[i], i))


def source_back(place, grads, source, weights, width):
    rows = grads.shape[1]
    return call(
        source_back_kernel,
        (rows // width,),
        [
            pl.BlockSpec((2, width, MODEL), lambda i, *_: (0, i, 0)),
            by_rows(width),
            weight_at(5),
            weight_at(6),
        ],
        [
            pl.BlockSpec(
                (width, MODEL), lambda i, place: (jnp.bitwise_xor(i, place[2]), 0)
            )
        ]
        + [slots_at(2)] * 2,
        [struct((rows, MODEL), jnp.bfloat16)] + [buffer_of(2)] * 2,
        8 * rows * MODEL * MODEL,
        scratch=[pltpu.VMEM((2, MODEL, MODEL), jnp.float32)],
        prefetch=1,
    )(place, grads, source, weights, weights)


def pairs(bit):
    return [(i, i ^ bit) for i in range(16)]


def swap(values):
    return lax.ppermute(values, "ctx", [(0, 1), (1, 0)])


def over_x(values):
    return lax.ppermute(values, "fsdp", pairs(2))


def over_core(values):
    return lax.ppermute(values, "fsdp", pairs(1))


def tie(*values):
    return lax.optimization_barrier(values)


def lot_specs(lot, first, second, spread, z_of, depth=1):
    specs = []
    for keep, _ in lot:
        slots, rows = keep.shape[3:5]
        block = (1, spread, depth, slots, rows, MODEL)
        specs += [
            pl.BlockSpec(block, lambda i, place: (first, second, z_of(i, place), 0, 0, 0))
        ] * 2
    return specs


def slots_of(lot):
    return sum(keep.shape[3] for keep, _ in lot)


def in_order(i, place):
    return i


def from_own(i, place):
    return lax.rem(place[3] + i, 4)


def pair_sums(refs, count):
    return [wide(refs[2 * i][...]) + wide(refs[2 * i + 1][...]) for i in range(count)]


def depth_of(lots):
    return 4 if sum(slots_of(lot) for lot in lots) < 4 else 1


def first_sums(place, lots):
    def kernel(place_ref, *refs):
        refs = list(refs)
        outs = refs[-len(lots) :]
        for lot, out in zip(lots, outs):
            start = 0
            for value in pair_sums([refs.pop(0) for _ in range(2 * len(lot))], len(lot)):
                end = start + value.shape[3]
                out[:, :, start:end] = short(value[0])
                start = end

    depth = depth_of(lots)
    specs = [spec for lot in lots for spec in lot_specs(lot, 1, 0, 2, in_order, depth)]
    shapes = [(2, 4, slots_of(lot), 32, MODEL) for lot in lots]
    return call(
        kernel,
        (4 // depth,),
        specs,
        [
            pl.BlockSpec((2, depth) + shape[2:], lambda i, place: (0, i, 0, 0, 0))
            for shape in shapes
        ],
        [struct(shape, jnp.bfloat16) for shape in shapes],
        1 << 20,
        prefetch=1,
    )(place, *[array for lot in lots for pair in lot for array in pair])


def second_sums(place, lots, firsts):
    def kernel(place_ref, *refs):
        refs = list(refs)
        outs = refs[-len(lots) :]
        for lot, out in zip(lots, outs):
            sources = [refs.pop(0) for _ in range(2 * len(lot))]
            received = refs.pop(0)
            start = 0
            for value in pair_sums(sources, len(lot)):
                end = start + value.shape[3]
                out[:, start:end] = short(value[0, 0] + wide(received[0, :, start:end]))
                start = end

    depth = depth_of(lots)
    specs, shapes, arrays = ([], [], [])
    for lot, first in zip(lots, firsts):
        specs += lot_specs(lot, 0, 1, 1, in_order, depth)
        specs.append(
            pl.BlockSpec((1, depth) + first.shape[2:], lambda i, place: (1, i, 0, 0, 0))
        )
        shapes.append(first.shape[1:])
        arrays += [array for pair in lot for array in pair] + [first]
    return call(
        kernel,
        (4 // depth,),
        specs,
        [pl.BlockSpec((depth,) + shape[1:], lambda i, place: (i, 0, 0, 0)) for shape in shapes],
        [struct(shape, jnp.bfloat16) for shape in shapes],
        1 << 20,
        prefetch=1,
    )(place, *arrays)


def third_sums(place, lots, firsts, seconds):
    def kernel(place_ref, *refs):
        refs = list(refs)
        outs = refs[-4:]
        start = 0
        for lot in lots:
            sources = [refs.pop(0) for _ in range(2 * len(lot))]
            received = wide(refs.pop(0)[0, 0]) + wide(refs.pop(0)[0])
            spot = 0
            for value in pair_sums(sources, len(lot)):
                count = value.shape[3]
                total = value[0, 0, 0] + received[spot : spot + count]
                for hop in range(4):

                    @pl.when(pl.program_id(0) == hop)
                    def _(out=outs[hop], total=total, start=start, end=start + count):
                        out[start:end] = total.astype(out.dtype)

                start, spot = (start + count, spot + count)

    specs, arrays = ([], [])
    for lot, first, second in zip(lots, firsts, seconds):
        specs += lot_specs(lot, 0, 0, 1, from_own)
        specs.append(
            pl.BlockSpec(
                (1, 1) + first.shape[2:], lambda i, place: (0, from_own(i, place), 0, 0, 0)
            )
        )
        specs.append(
            pl.BlockSpec(
                (1,) + second.shape[1:], lambda i, place: (from_own(i, place), 0, 0, 0)
            )
        )
        arrays += [array for pair in lot for array in pair] + [first, second]
    shape = (sum(slots_of(lot) for lot in lots), 32, MODEL)
    return call(
        kernel,
        (4,),
        specs,
        [once(shape, lambda i, place: (0, 0, 0)) for _ in range(4)],
        [struct(shape, jnp.bfloat16 if hop else jnp.float32) for hop in range(4)],
        1 << 20,
        prefetch=1,
    )(place, *arrays)


def cycled(hop, values):
    return lax.ppermute(values, "fsdp", [(i, (i + 4 * hop) % 16) for i in range(16)])


def over_z(shares):
    return [shares[0]] + [cycled(hop, shares[hop]) for hop in range(1, 4)]


def whole(shares):
    return short(shares[0] + sum(wide(share) for share in shares[1:]))


def both_parts(total, other):
    low = lax.axis_index("ctx") == 0
    return wide(jnp.stack([jnp.where(low, total, other), jnp.where(low, other, total)], axis=1))


def columns(shares, start, stop):
    part = shares[start:stop].reshape(stop - start, -1, MODEL)
    return jnp.concatenate(list(part), axis=1)


def feed_shares(lots):
    inner = [lot[:2].reshape(2, 64, 8, 128).transpose(1, 0, 2, 3).reshape(64, 16, 128) for lot in lots]
    inner = jnp.stack(inner, axis=2).reshape(64, 4 * MODEL)
    outer = [lot[2:].transpose(1, 0, 2, 3).reshape(128, MODEL) for lot in lots]
    return inner, jnp.concatenate(outer)


def whole_packs(mesh):
    return mesh.shape["ctx"] == 2 and mesh.shape["fsdp"] == 16


def whole_pack_body(
    tokens,
    encoded,
    cotangent,
    order,
    target_lengths,
    source_lengths,
    self_project,
    self_output,
    cross_query,
    cross_source,
    cross_output,
    feed_in,
    feed_out,
    norm_gain,
    norm_bias,
):
    rows = tokens.shape[2]
    pack_rows, source_rows = (2 * rows, 2 * encoded.shape[2])
    first_rows = 3 * pack_rows // 4
    width = rows // 2
    mine = lax.axis_index("ctx")
    spot = lax.axis_index("fsdp")
    z = spot // 4
    place = jnp.stack([spot % 2, spot // 2 % 2, mine, z]).astype(jnp.int32)
    part = self_project.shape[0]

    norms = jnp.pad(jnp.concatenate([norm_gain, norm_bias]), ((0, 10), (0, MODEL - part)))
    attention_shard, feed_shard = pack(
        (self_project, self_output, cross_query, cross_source, cross_output, feed_in, feed_out),
        norms,
    )
    weights = lax.all_gather(attention_shard, "fsdp", axis=0)
    norms = wide(weights[:, 8 * part : 8 * part + 8, :part])
    norms = norms.transpose(1, 0, 2).reshape(8, MODEL)

    def both_halves(array):
        own = lax.dynamic_index_in_dim(array, mine, 0, False)[0]
        return own, swap(lax.dynamic_index_in_dim(array, 1 - mine, 0, False)[0])

    places = lax.dynamic_index_in_dim(order, mine, 0, False)[0]
    holds = places[::width] // width
    found = jnp.argsort(holds).astype(jnp.int32)
    held = jnp.where(found // 2 == mine, found % 2, 2 + found % 2)

    def from_both(own, other):
        low = mine == 0
        return jnp.stack([jnp.where(low, own, other), jnp.where(low, other, own)])[:, None]

    halves = jnp.concatenate(both_halves(tokens))
    own, other = both_halves(encoded)
    source = jnp.concatenate([jnp.where(mine == 0, own, other), jnp.where(mine == 0, other, own)])
    feed_shard, halves, source = tie(feed_shard, halves, source)
    feed_weights = lax.all_gather(feed_shard, "fsdp", axis=0)

    lengths = lax.dynamic_index_in_dim(target_lengths, mine, 0, False)[0]
    target_docs = docs_of(jnp.arange(pack_rows, dtype=jnp.int32), lengths)
    lengths = lax.dynamic_index_in_dim(source_lengths, mine, 0, False)[0]
    source_docs = docs_of(jnp.arange(source_rows, dtype=jnp.int32), lengths)
    docs = lengths.shape[0]
    marks = query_marks(target_docs)
    target_marks = key_marks(target_docs, docs)
    source_marks = key_marks(source_docs, docs)
    reach = source_rows // 2

    first, query, keys, values = enter(held, halves, norms, weights, width)
    query, cotangent = tie(query, cotangent)
    cotangents = both_halves(cotangent)
    plan = self_plan(first_rows, pack_rows, width)
    self_mixed, self_extra = attend(plan, query, keys, values, marks, target_marks)
    self_mixed, source = tie(self_mixed, source)
    cross_keys, cross_values = source_pairs(source, weights, source_rows // 2)
    after_self, second, cross_queries = between(held, self_mixed, halves, norms, weights, width)
    plan = cross_plan(first_rows, pack_rows, reach, source_rows, width // 2)
    cross_mixed, cross_extra = attend(
        plan, cross_queries, cross_keys, cross_values, marks, source_marks
    )
    after_cross, third, grad_out = before_feed(
        held, cross_mixed, after_self, *cotangents, norms, weights, width
    )

    out, back, lot_a, lot_b = feed(place, third, grad_out, feed_weights)
    lot_a, lot_b = ([(lot[0], over_core(lot[1]))] for lot in (lot_a, lot_b))
    result, grad_after_cross, grad_cross_mixed, sums_two, *part_out = after_feed(
        held, place, after_cross, out, back, grad_out, cross_mixed, norms, weights, width
    )
    first_ab = first_sums(place, [lot_a, lot_b])
    grad_cross_mixed, part_out[1], *first_ab = tie(grad_cross_mixed, part_out[1], *first_ab)
    first_ab = (over_x(first_ab[0]), swap(first_ab[1]))
    part_out[1] = over_core(part_out[1])
    plan = cross_plan(first_rows, pack_rows, reach, source_rows, width)
    grad_cross_queries, grad_source = attend_back(
        plan,
        cross_queries,
        cross_keys,
        cross_values,
        cross_extra,
        source_marks,
        cross_mixed,
        grad_cross_mixed,
        False,
    )
    grad_source, part_out[1], *first_ab = tie(grad_source, part_out[1], *first_ab)
    grad_encoded, *part_source = source_back(place, grad_source, source, weights, source_rows // 2)
    encoded_own = grad_encoded[: source_rows // 2]
    away = jnp.concatenate([result[rows:], grad_encoded[source_rows // 2 :]])
    second_ab = second_sums(place, [lot_a, lot_b], first_ab)
    grad_cross_queries, encoded_own, away, *second_ab = tie(
        grad_cross_queries, encoded_own, away, *second_ab
    )
    second_ab = (swap(second_ab[0]), over_x(second_ab[1]))
    grad_after_self, grad_self_mixed, sums_one, *part_middle = middle(
        place,
        grad_cross_queries,
        second,
        after_self,
        grad_after_cross,
        self_mixed,
        norms,
        weights,
        width,
    )
    grad_self_mixed, part_source[1], part_middle[1], *second_ab = tie(
        grad_self_mixed, part_source[1], part_middle[1], *second_ab
    )
    part_source[1], part_middle[1] = (over_core(part_source[1]), over_core(part_middle[1]))
    third_ab = third_sums(place, [lot_a, lot_b], first_ab, second_ab)
    lot_c = [part_out, part_source, part_middle]
    (first_c,) = first_sums(place, [lot_c])
    grad_self_mixed, first_c, away, *third_ab = tie(grad_self_mixed, first_c, away, *third_ab)
    first_c = over_x(first_c)
    away = swap(away)
    third_ab = over_z(third_ab)
    plan = self_plan(first_rows, pack_rows, width)
    grads = attend_back(
        plan,
        query,
        keys,
        values,
        self_extra,
        target_marks,
        self_mixed,
        grad_self_mixed,
        True,
    )
    grads, first_c, away, *third_ab = tie(grads, first_c, away, *third_ab)
    (second_c,) = second_sums(place, [lot_c], [first_c])
    total_ab = whole(third_ab)
    grads, second_c, total_ab = tie(grads, second_c, total_ab)
    second_c, other_ab = (swap(second_c), swap(total_ab))
    grad_tokens, sums_zero, *lot_d = finish(
        held, place, grads, first, halves, grad_after_self, norms, weights, width
    )
    grad_tokens, sums_zero, second_c, other_ab, *lot_d = tie(
        grad_tokens, sums_zero, second_c, other_ab, *lot_d
    )
    sums = jnp.concatenate([sums_zero[:2], sums_one[:2], sums_two[:2]])
    lot_d = [(lot_d[0], over_core(lot_d[1]))]
    third_c = third_sums(place, [lot_c], [first_c], [second_c])
    (first_d,) = first_sums(place, [lot_d])
    first_d, grad_tokens, result, encoded_own, away, sums, *third_c = tie(
        first_d, grad_tokens, result, encoded_own, away, sums, *third_c
    )
    first_d = over_x(first_d)
    tokens_other = swap(grad_tokens[rows:])
    third_c = over_z(third_c)
    share_ab = both_parts(total_ab, other_ab)
    feed_in_grad, feed_out_grad = feed_shares((share_ab[:4], share_ab[4:]))
    result = from_both(result[:rows], away[:rows])
    grad_encoded = from_both(encoded_own, away[rows:])
    sums = sums + over_core(sums)
    total_c = whole(third_c)
    (second_d,) = second_sums(place, [lot_d], [first_d])
    second_d, total_c, sums, result, grad_encoded, feed_in_grad, feed_out_grad = tie(
        second_d, total_c, sums, result, grad_encoded, feed_in_grad, feed_out_grad
    )
    second_d = swap(second_d)
    for bit in (4, 8):
        sums = sums + lax.ppermute(sums, "fsdp", pairs(bit))
    third_d = third_sums(place, [lot_d], [first_d], [second_d])
    sums, tokens_other, *third_d = tie(sums, tokens_other, *third_d)
    sums = sums + over_x(sums)
    total_d = whole(over_z(third_d))
    total = jnp.concatenate([total_c, total_d])
    sums = sums + swap(sums)
    share_cd = both_parts(total, swap(total))
    share_c, share_d = (share_cd[:5], share_cd[5:])

    sums = lax.dynamic_slice_in_dim(sums, spot * part, part, 1)
    grad_tokens = from_both(grad_tokens[:rows], tokens_other)

    return (
        result,
        grad_tokens,
        grad_encoded,
        columns(share_d, 0, 3),
        columns(share_c, 4, 5),
        columns(share_c, 3, 4),
        columns(share_c, 1, 3),
        columns(share_c, 0, 1),
        feed_in_grad,
        feed_out_grad,
        sums[0::2],
        sums[1:4:2],
        sums[5],
    )


def solution(mesh):
    chosen = whole_pack_body if whole_packs(mesh) else body
    return jax.shard_map(
        chosen,
        mesh=mesh,
        in_specs=(
            P(None, "fsdp", "ctx", None),
            P(None, "fsdp", "ctx", None),
            P(None, "fsdp", "ctx", None),
            P(None, "fsdp", None),
            P(None, "fsdp", None),
            P(None, "fsdp", None),
            P("fsdp", None),
            P("fsdp", None),
            P("fsdp", None),
            P("fsdp", None),
            P("fsdp", None),
            P("fsdp", None),
            P("fsdp", None),
            P(None, "fsdp"),
            P(None, "fsdp"),
        ),
        out_specs=(
            P(None, "fsdp", "ctx", None),
            P(None, "fsdp", "ctx", None),
            P(None, "fsdp", "ctx", None),
            P("fsdp", None),
            P("fsdp", None),
            P("fsdp", None),
            P("fsdp", None),
            P("fsdp", None),
            P("fsdp", None),
            P("fsdp", None),
            P(None, "fsdp"),
            P(None, "fsdp"),
            P("fsdp"),
        ),
        check_vma=False,
    )
```

```python
import functools
import math

import jax
import jax.numpy as jnp
from jax import lax
from jax.experimental import pallas as pl
from jax.experimental.pallas import tpu as pltpu
from jax.sharding import PartitionSpec as P

HEAD = 64


MASKED = -1e30


def as_sent(x):

    def short(part):
        return part.astype(jnp.bfloat16) if part.dtype == jnp.float32 else part

    return jax.tree.map(short, x)


def norm_apply(values, gain, bias):
    mean = jnp.mean(values, axis=-1, keepdims=True)
    centred = values - mean
    spread = jnp.mean(centred * centred, axis=-1, keepdims=True)
    return centred * lax.rsqrt(spread + 1e-05) * gain + bias


def gelu_exact(values):
    return jax.nn.gelu(values, approximate=False)


def docs_of(places, lengths):
    ends = jnp.cumsum(lengths)
    return jnp.sum((places[:, None] >= ends[None, :]).astype(jnp.int32), axis=1)


def split_heads(values):
    return values.reshape(values.shape[0], -1, HEAD)


def block_scores(query, pairs, allowed, start, count):
    model = query.shape[1]
    block = lax.dynamic_slice_in_dim(pairs, start, count, 0)
    scores = jnp.einsum(
        "qhd,khd->hqk",
        split_heads(query),
        split_heads(block[:, :model]),
        preferred_element_type=jnp.float32,
    )
    scores = jnp.where(allowed(start, count)[None], scores * HEAD ** (-0.5), MASKED)
    return (scores, block)


def log_mass(query, pairs, allowed, width):
    rows, model = query.shape
    heads = model // HEAD

    def step(index, carry):
        peak, total = carry
        scores, _ = block_scores(query, pairs, allowed, index * width, width)
        new_peak = jnp.maximum(peak, jnp.max(scores, axis=2))
        total = total * jnp.exp(peak - new_peak) + jnp.sum(
            jnp.exp(scores - new_peak[:, :, None]), axis=2
        )
        return (new_peak, total)

    begin = (jnp.full((heads, rows), MASKED, jnp.float32), jnp.zeros((heads, rows), jnp.float32))
    peak, total = lax.fori_loop(0, pairs.shape[0] // width, step, begin)
    return peak + jnp.log(total)


def attend_forward(query, pairs, allowed, width, log_total):
    rows, model = query.shape

    def step(index, mixed):
        scores, block = block_scores(query, pairs, allowed, index * width, width)
        probs = jnp.exp(scores - log_total[:, :, None]).astype(jnp.bfloat16)
        return mixed + jnp.einsum(
            "hqk,khd->qhd", probs, split_heads(block[:, model:]), preferred_element_type=jnp.float32
        )

    mixed = lax.fori_loop(
        0, pairs.shape[0] // width, step, jnp.zeros((rows, model // HEAD, HEAD), jnp.float32)
    )
    return mixed.reshape(rows, model).astype(jnp.bfloat16)


def score_grads(query, pairs, allowed, grad_mixed, log_total, start, count):
    model = query.shape[1]
    scores, block = block_scores(query, pairs, allowed, start, count)
    probs = jnp.exp(scores - log_total[:, :, None])
    grad_probs = jnp.einsum(
        "qhd,khd->hqk",
        split_heads(grad_mixed),
        split_heads(block[:, model:]),
        preferred_element_type=jnp.float32,
    )
    return (probs, grad_probs, block)


def attend_delta(query, pairs, allowed, grad_mixed, log_total, width):
    rows, model = query.shape

    def step(index, delta):
        probs, grad_probs, _ = score_grads(
            query, pairs, allowed, grad_mixed, log_total, index * width, width
        )
        return delta + jnp.sum(probs * grad_probs, axis=2)

    return lax.fori_loop(
        0, pairs.shape[0] // width, step, jnp.zeros((model // HEAD, rows), jnp.float32)
    )


def attend_query_grad(query, pairs, allowed, grad_mixed, log_total, delta, width):
    rows, model = query.shape

    def step(index, grad):
        probs, grad_probs, block = score_grads(
            query, pairs, allowed, grad_mixed, log_total, index * width, width
        )
        grad_scores = (probs * (grad_probs - delta[:, :, None])).astype(jnp.bfloat16)
        return grad + jnp.einsum(
            "hqk,khd->qhd",
            grad_scores,
            split_heads(block[:, :model]),
            preferred_element_type=jnp.float32,
        )

    grad = lax.fori_loop(
        0, pairs.shape[0] // width, step, jnp.zeros((rows, model // HEAD, HEAD), jnp.float32)
    )
    return (grad.reshape(rows, model) * HEAD ** (-0.5)).astype(jnp.bfloat16)


def key_terms(query, pairs, allowed, grad_mixed, log_total, delta, width, count):
    model = query.shape[1]
    step_width = math.gcd(count, width)

    def step(index, terms):
        probs, grad_probs, _ = score_grads(
            query, pairs, allowed, grad_mixed, log_total, index * step_width, step_width
        )
        grad_scores = (probs * (grad_probs - delta[:, :, None])).astype(jnp.bfloat16)
        grad_keys = jnp.einsum(
            "hqk,qhd->khd", grad_scores, split_heads(query), preferred_element_type=jnp.float32
        ) * HEAD ** (-0.5)
        grad_values = jnp.einsum(
            "hqk,qhd->khd",
            probs.astype(jnp.bfloat16),
            split_heads(grad_mixed),
            preferred_element_type=jnp.float32,
        )
        piece = jnp.concatenate(
            [grad_keys.reshape(step_width, model), grad_values.reshape(step_width, model)], axis=1
        )
        return lax.dynamic_update_slice_in_dim(terms, piece, index * step_width, 0)

    return lax.fori_loop(0, count // step_width, step, jnp.zeros((count, 2 * model), jnp.float32))


def body(
    tokens,
    encoded,
    cotangent,
    order,
    target_lengths,
    source_lengths,
    self_project,
    self_output,
    cross_query,
    cross_source,
    cross_output,
    feed_in,
    feed_out,
    norm_gain,
    norm_bias,
):
    micro = tokens.shape[0]
    rows = tokens.shape[2]
    model = tokens.shape[3]
    source_rows = encoded.shape[2]
    place = lax.axis_index("ctx")
    group = lax.axis_size("ctx")
    pack_total = rows * group
    source_total = source_rows * group
    self_width = math.gcd(pack_total, 512)
    cross_width = math.gcd(source_total, 512)
    results = []
    grad_values_all = []
    grad_encoded_all = []
    totals = ()
    for index in range(micro):
        attention_part = (
            lax.all_gather(self_project, "fsdp", axis=0, tiled=True),
            lax.all_gather(self_output, "fsdp", axis=0, tiled=True),
            lax.all_gather(cross_query, "fsdp", axis=0, tiled=True),
            lax.all_gather(cross_source, "fsdp", axis=0, tiled=True),
            lax.all_gather(cross_output, "fsdp", axis=0, tiled=True),
            lax.all_gather(norm_gain, "fsdp", axis=1, tiled=True),
            lax.all_gather(norm_bias, "fsdp", axis=1, tiled=True),
        )
        feed_part = (
            lax.all_gather(feed_in, "fsdp", axis=0, tiled=True),
            lax.all_gather(feed_out, "fsdp", axis=0, tiled=True),
        )
        weights = tuple(attention_part) + tuple(feed_part)
        (
            self_in_full,
            self_out_full,
            cross_query_full,
            cross_source_full,
            cross_out_full,
            gain_full,
            bias_full,
            feed_in_full,
            feed_out_full,
        ) = weights
        gains = gain_full.astype(jnp.float32)
        biases = bias_full.astype(jnp.float32)
        values = tokens[index, 0].astype(jnp.float32)
        source = encoded[index, 0]
        grad_out = cotangent[index, 0]
        places = order[index, 0]
        target_docs = docs_of(places, target_lengths[index, 0])
        query_places = lax.dynamic_slice_in_dim(places, place * rows, rows)
        query_docs = lax.dynamic_slice_in_dim(target_docs, place * rows, rows)
        source_docs = docs_of(jnp.arange(source_total, dtype=jnp.int32), source_lengths[index, 0])

        def self_allowed(start, count):
            key_docs = lax.dynamic_slice_in_dim(target_docs, start, count)
            key_places = lax.dynamic_slice_in_dim(places, start, count)
            return (query_docs[:, None] == key_docs[None, :]) & (
                key_places[None, :] <= query_places[:, None]
            )

        def cross_allowed(start, count):
            return (
                query_docs[:, None] == lax.dynamic_slice_in_dim(source_docs, start, count)[None, :]
            )

        first = norm_apply(values, gains[0], biases[0]).astype(jnp.bfloat16)
        query = jnp.dot(first, self_in_full[:, :model], preferred_element_type=jnp.float32).astype(
            jnp.bfloat16
        )
        local_pairs = jnp.dot(
            first, self_in_full[:, model:], preferred_element_type=jnp.float32
        ).astype(jnp.bfloat16)
        self_pairs = lax.all_gather(local_pairs, "ctx", axis=0, tiled=True)
        self_total = log_mass(query, self_pairs, self_allowed, self_width)
        self_mixed = attend_forward(query, self_pairs, self_allowed, self_width, self_total)
        after_self = values + jnp.dot(self_mixed, self_out_full, preferred_element_type=jnp.float32)
        second = norm_apply(after_self, gains[1], biases[1]).astype(jnp.bfloat16)
        cross_queries = jnp.dot(
            second, cross_query_full, preferred_element_type=jnp.float32
        ).astype(jnp.bfloat16)
        cross_local = jnp.dot(source, cross_source_full, preferred_element_type=jnp.float32).astype(
            jnp.bfloat16
        )
        cross_pairs = lax.all_gather(cross_local, "ctx", axis=0, tiled=True)
        cross_total = log_mass(cross_queries, cross_pairs, cross_allowed, cross_width)
        cross_mixed = attend_forward(
            cross_queries, cross_pairs, cross_allowed, cross_width, cross_total
        )
        after_cross = after_self + jnp.dot(
            cross_mixed, cross_out_full, preferred_element_type=jnp.float32
        )
        third = norm_apply(after_cross, gains[2], biases[2]).astype(jnp.bfloat16)
        hidden = jnp.dot(third, feed_in_full, preferred_element_type=jnp.float32)
        active = gelu_exact(hidden).astype(jnp.bfloat16)
        result = (
            after_cross + jnp.dot(active, feed_out_full, preferred_element_type=jnp.float32)
        ).astype(jnp.bfloat16)
        grad_feed_out = jnp.einsum(
            "rf,rd->fd", active, grad_out, preferred_element_type=jnp.float32
        )
        grad_active = jnp.einsum(
            "rd,fd->rf", grad_out, feed_out_full, preferred_element_type=jnp.float32
        ).astype(jnp.bfloat16)
        _, gelu_pull = jax.vjp(gelu_exact, hidden)
        grad_hidden = gelu_pull(grad_active.astype(jnp.float32))[0].astype(jnp.bfloat16)
        grad_feed_in = jnp.einsum(
            "rd,rf->df", third, grad_hidden, preferred_element_type=jnp.float32
        )
        grad_third = jnp.einsum(
            "rf,df->rd", grad_hidden, feed_in_full, preferred_element_type=jnp.float32
        )
        _, norm_pull = jax.vjp(norm_apply, after_cross, gains[2], biases[2])
        norm_part, gain_two, bias_two = norm_pull(grad_third)
        grad_after_cross = grad_out.astype(jnp.float32) + norm_part
        cross_branch = grad_after_cross.astype(jnp.bfloat16)
        grad_cross_output = jnp.einsum(
            "rd,re->de", cross_mixed, cross_branch, preferred_element_type=jnp.float32
        )
        grad_cross_mixed = jnp.einsum(
            "re,de->rd", cross_branch, cross_out_full, preferred_element_type=jnp.float32
        ).astype(jnp.bfloat16)
        cross_delta = attend_delta(
            cross_queries, cross_pairs, cross_allowed, grad_cross_mixed, cross_total, cross_width
        )
        grad_cross_queries = attend_query_grad(
            cross_queries,
            cross_pairs,
            cross_allowed,
            grad_cross_mixed,
            cross_total,
            cross_delta,
            cross_width,
        )
        grad_source = lax.psum_scatter(
            key_terms(
                cross_queries,
                cross_pairs,
                cross_allowed,
                grad_cross_mixed,
                cross_total,
                cross_delta,
                cross_width,
                source_rows * lax.axis_size("ctx"),
            ).astype(jnp.bfloat16),
            "ctx",
            scatter_dimension=0,
            tiled=True,
        )
        grad_cross_source = jnp.einsum(
            "sd,se->de", source, grad_source, preferred_element_type=jnp.float32
        )
        grad_encoded = jnp.einsum(
            "se,de->sd", grad_source, cross_source_full, preferred_element_type=jnp.float32
        ).astype(jnp.bfloat16)
        grad_cross_query = jnp.einsum(
            "rd,re->de", second, grad_cross_queries, preferred_element_type=jnp.float32
        )
        grad_second = jnp.einsum(
            "re,de->rd", grad_cross_queries, cross_query_full, preferred_element_type=jnp.float32
        )
        _, norm_pull = jax.vjp(norm_apply, after_self, gains[1], biases[1])
        norm_part, gain_one, bias_one = norm_pull(grad_second)
        grad_after_self = grad_after_cross + norm_part
        self_branch = grad_after_self.astype(jnp.bfloat16)
        grad_self_output = jnp.einsum(
            "rd,re->de", self_mixed, self_branch, preferred_element_type=jnp.float32
        )
        grad_self_mixed = jnp.einsum(
            "re,de->rd", self_branch, self_out_full, preferred_element_type=jnp.float32
        ).astype(jnp.bfloat16)
        self_delta = attend_delta(
            query, self_pairs, self_allowed, grad_self_mixed, self_total, self_width
        )
        grad_query = attend_query_grad(
            query, self_pairs, self_allowed, grad_self_mixed, self_total, self_delta, self_width
        )
        grad_pairs = lax.psum_scatter(
            key_terms(
                query,
                self_pairs,
                self_allowed,
                grad_self_mixed,
                self_total,
                self_delta,
                self_width,
                rows * lax.axis_size("ctx"),
            ).astype(jnp.bfloat16),
            "ctx",
            scatter_dimension=0,
            tiled=True,
        )
        grad_projected = jnp.concatenate([grad_query, grad_pairs], axis=1)
        grad_self_project = jnp.einsum(
            "rd,re->de", first, grad_projected, preferred_element_type=jnp.float32
        )
        grad_first = jnp.einsum(
            "re,de->rd", grad_projected, self_in_full, preferred_element_type=jnp.float32
        )
        _, norm_pull = jax.vjp(norm_apply, values, gains[0], biases[0])
        norm_part, gain_zero, bias_zero = norm_pull(grad_first)
        grad_values = (grad_after_self + norm_part).astype(jnp.bfloat16)
        grads = (
            grad_self_project,
            grad_self_output,
            grad_cross_query,
            grad_cross_source,
            grad_cross_output,
            grad_feed_in,
            grad_feed_out,
            jnp.stack([gain_zero, gain_one, gain_two]),
            jnp.stack([bias_zero, bias_one, bias_two]),
        )
        result, grad_values, grad_encoded, grads = (result, grad_values, grad_encoded, grads)
        totals = (
            grads
            if index == 0
            else tuple((jnp.add(left, right) for left, right in zip(totals, grads)))
        )
        results.append(result)
        grad_values_all.append(grad_values)
        grad_encoded_all.append(grad_encoded)
    shares = (
        lax.psum_scatter(
            totals[0].astype(jnp.bfloat16), "fsdp", scatter_dimension=0, tiled=True
        ).astype(jnp.float32),
        lax.psum_scatter(
            totals[1].astype(jnp.bfloat16), "fsdp", scatter_dimension=0, tiled=True
        ).astype(jnp.float32),
        lax.psum_scatter(
            totals[2].astype(jnp.bfloat16), "fsdp", scatter_dimension=0, tiled=True
        ).astype(jnp.float32),
        lax.psum_scatter(
            totals[3].astype(jnp.bfloat16), "fsdp", scatter_dimension=0, tiled=True
        ).astype(jnp.float32),
        lax.psum_scatter(
            totals[4].astype(jnp.bfloat16), "fsdp", scatter_dimension=0, tiled=True
        ).astype(jnp.float32),
        lax.psum_scatter(
            totals[5].astype(jnp.bfloat16), "fsdp", scatter_dimension=0, tiled=True
        ).astype(jnp.float32),
        lax.psum_scatter(
            totals[6].astype(jnp.bfloat16), "fsdp", scatter_dimension=0, tiled=True
        ).astype(jnp.float32),
        lax.psum_scatter(
            totals[7].astype(jnp.bfloat16), "fsdp", scatter_dimension=1, tiled=True
        ).astype(jnp.float32),
        lax.psum_scatter(
            totals[8].astype(jnp.bfloat16), "fsdp", scatter_dimension=1, tiled=True
        ).astype(jnp.float32),
    )
    totals = tuple(
        jax.tree.map(lambda part: part.astype(jnp.float32), lax.psum(as_sent(tuple(shares)), "ctx"))
    )
    output = jnp.stack(results)[:, None]
    grad_tokens = jnp.stack(grad_values_all)[:, None]
    grad_source_rows = jnp.stack(grad_encoded_all)[:, None]
    return (
        output,
        grad_tokens,
        grad_source_rows,
        totals[0],
        totals[1],
        totals[2],
        totals[3],
        totals[4],
        totals[5],
        totals[6],
        totals[7],
        totals[8][:2],
        totals[8][2],
    )


BIG = 1e30
SCALE2 = HEAD ** (-0.5) * math.log2(math.e)
NT = (((1,), (1,)), ((), ()))
TN = (((0,), (0,)), ((), ()))
NN = (((1,), (0,)), ((), ()))


def dot(left, right, dims=NN):
    return lax.dot_general(left, right, dims, preferred_element_type=jnp.float32)


def lanes(rows):
    return lax.broadcasted_iota(jnp.int32, (rows, 128), 1)


def parts(x):
    hi = x.astype(jnp.bfloat16)
    rest = x - hi.astype(jnp.float32)
    mid = rest.astype(jnp.bfloat16)
    lo = (rest - mid.astype(jnp.float32)).astype(jnp.bfloat16)
    return (hi, mid, lo)


def spread(x, base):
    hi, mid, lo = parts(x)
    lane = lanes(x.shape[0]) % HEAD
    return jnp.where(lane == 4, hi, jnp.where(lane == 5, mid, jnp.where(lane == 6, lo, base)))


def two_heads(ref, own, other):
    left = lanes(own.shape[0]) < HEAD
    ref[0] = jnp.where(left, own, other)
    ref[1] = jnp.where(left, other, own)


def tail_masked(scores, rows):
    width = scores.shape[1] - rows
    row = lax.broadcasted_iota(jnp.int32, (rows, rows), 0)
    column = lax.broadcasted_iota(jnp.int32, (rows, rows), 1)
    tail = jnp.where(column > row, -BIG, scores[:, width:])
    return tail if width == 0 else jnp.concatenate([scores[:, :width], tail], axis=1)


def attend_kernel(plan, q_ref, k_ref, v_ref, qd_ref, kd_ref, out_ref, extra_ref, keys, values):
    two_heads(keys, k_ref[...], kd_ref[...])
    two_heads(values, v_ref[...], jnp.ones_like(v_ref))

    def scores_of(item):
        q0, q1, k0, k1, diagonal = item
        left = lanes(q1 - q0) < HEAD
        q, qd = (q_ref[q0:q1], qd_ref[q0:q1])
        pair = [dot(jnp.where(left == (h == 0), q, qd), keys[h, k0:k1], NT) for h in range(2)]
        return [tail_masked(s, q1 - q0) for s in pair] if diagonal else pair

    following = scores_of(plan[0])
    for index, (q0, q1, k0, k1, _) in enumerate(plan):
        scores = following
        following = scores_of(plan[index + 1]) if index + 1 < len(plan) else None
        left = lanes(q1 - q0) < HEAD
        mixed, tops = ([], [])
        for h in range(2):
            top = jnp.max(scores[h], axis=1, keepdims=True)
            probs = jnp.exp2((scores[h] - top) * SCALE2).astype(jnp.bfloat16)
            mixed.append(dot(probs, values[h, k0:k1]))
            tops.append(top)
        mass = jnp.where(left, mixed[1], mixed[0])
        numer = jnp.where(left, mixed[0], mixed[1])
        out_ref[q0:q1] = (numer / pltpu.roll(mass, HEAD, 1)).astype(jnp.bfloat16)
        top = jnp.where(left, tops[1], tops[0])
        extra_ref[q0:q1] = spread(-(top + HEAD**0.5 * jnp.log(mass)), qd_ref[q0:q1])


def attend_back_kernel(
    plan,
    q_ref,
    k_ref,
    v_ref,
    extra_ref,
    kd_ref,
    out_ref,
    g_ref,
    *refs,
):
    *outs, keys, values, queries, grads, g_t, q_t, dk_t, dv_t = refs
    if len(outs) == 1:
        dq_ref, dk_ref, dv_ref = (outs[0].at[i] for i in range(3))
    else:
        dq_ref, dk_ref, dv_ref = (outs[0], outs[1].at[0], outs[1].at[1])
    two_heads(keys, k_ref[...], kd_ref[...])
    two_heads(values, v_ref[...], jnp.ones_like(v_ref))
    two_heads(queries, q_ref[...], extra_ref[...])
    square = (128, 128)
    row, column = (lax.broadcasted_iota(jnp.int32, square, axis) < HEAD for axis in (0, 1))
    across = jnp.where(row != column, 1.0, 0.0).astype(jnp.bfloat16)
    g = g_ref[...]
    terms = parts(g.astype(jnp.float32) * out_ref[...].astype(jnp.float32))
    delta = sum(dot(term, across) for term in terms)
    two_heads(grads, g, spread(-delta, jnp.zeros_like(g)))
    g_t[...] = g.T
    q_t[...] = q_ref[...].T
    dk_t[...] = jnp.zeros_like(dk_t)
    dv_t[...] = jnp.zeros_like(dv_t)
    for q0, q1, k0, k1, diagonal in plan:
        left = lanes(q1 - q0) < HEAD
        pair = []
        for h in range(2):
            s = dot(queries[h, q0:q1], keys[h, k0:k1], NT)
            s = tail_masked(s, q1 - q0) if diagonal else s
            pair.append((s, dot(grads[h, q0:q1], values[h, k0:k1], NT)))
        dqs = []
        for h, (s, grad_probs) in enumerate(pair):
            probs = jnp.exp2(s * SCALE2)
            ds = (probs * grad_probs).astype(jnp.bfloat16)
            head = slice(h * HEAD, h * HEAD + HEAD)
            dv_t[head, k0:k1] += dot(g_t[head, q0:q1], probs.astype(jnp.bfloat16))
            dk_t[head, k0:k1] += dot(q_t[head, q0:q1], ds)
            dqs.append(dot(ds, k_ref[k0:k1]))
        dq_ref[q0:q1] = (jnp.where(left, dqs[0], dqs[1]) * HEAD ** (-0.5)).astype(jnp.bfloat16)
    dk_ref[...] = (dk_t[...].T * HEAD ** (-0.5)).astype(jnp.bfloat16)
    dv_ref[...] = dv_t[...].T.astype(jnp.bfloat16)


def pair_of_heads(rows):
    return pl.BlockSpec((rows, 128), lambda i: (0, i))


def all_of(rows):
    return pl.BlockSpec((rows, 128), lambda i: (0, 0))


def small_cost():
    return pl.CostEstimate(flops=1 << 10, bytes_accessed=1 << 10, transcendentals=0)


def attend(plan, q, k, v, qd, kd):
    nq, nk, model = (q.shape[0], k.shape[0], q.shape[1])
    shape = jax.ShapeDtypeStruct((nq, model), jnp.bfloat16)
    return pl.pallas_call(
        functools.partial(attend_kernel, plan),
        grid=(model // 128,),
        in_specs=[pair_of_heads(n) for n in (nq, nk, nk)] + [all_of(nq), all_of(nk)],
        out_specs=[pair_of_heads(nq)] * 2,
        out_shape=[shape] * 2,
        scratch_shapes=[pltpu.VMEM((2, nk, 128), jnp.bfloat16)] * 2,
        compiler_params=pltpu.CompilerParams(vmem_limit_bytes=58 * 2**20),
        cost_estimate=small_cost(),
    )(q, k, v, qd, kd)


def stacked(count, rows):
    return pl.BlockSpec((count, rows, 128), lambda i: (0, 0, i))


def attend_back(plan, q, k, v, extra, kd, out, g, together):
    nq, nk, model = (q.shape[0], k.shape[0], q.shape[1])
    if together:
        specs, shapes = ([stacked(3, nq)], [(3, nq, model)])
    else:
        specs, shapes = ([pair_of_heads(nq), stacked(2, nk)], [(nq, model), (2, nk, model)])
    outs = pl.pallas_call(
        functools.partial(attend_back_kernel, plan),
        grid=(model // 128,),
        in_specs=[pair_of_heads(n) for n in (nq, nk, nk, nq)]
        + [all_of(nk)]
        + [pair_of_heads(nq)] * 2,
        out_specs=specs,
        out_shape=[jax.ShapeDtypeStruct(shape, jnp.bfloat16) for shape in shapes],
        scratch_shapes=[pltpu.VMEM((2, nk, 128), jnp.bfloat16)] * 2
        + [pltpu.VMEM((2, nq, 128), jnp.bfloat16)] * 2
        + [pltpu.VMEM((128, nq), jnp.bfloat16)] * 2
        + [pltpu.VMEM((128, nk), jnp.float32)] * 2,
        compiler_params=pltpu.CompilerParams(vmem_limit_bytes=58 * 2**20),
        cost_estimate=small_cost(),
    )(q, k, v, extra, kd, out, g)
    return outs[0] if together else outs


def self_plan(first, total, tile):
    return [
        (start, start + tile, low, start + tile, True)
        for low, high in ((0, first), (first, total))
        for start in range(low, high, tile)
    ]


def cross_plan(first, total, reach, source, tile):
    return [
        (start, start + tile, 0, reach if start < first else source, False)
        for start in range(0, total, tile)
    ]


def query_marks(docs):
    lane = jnp.arange(128) % HEAD
    return jnp.where(docs[:, None] == lane[None, :], BIG, 0.0).astype(jnp.bfloat16)


def key_marks(docs, count):
    lane = (jnp.arange(128) % HEAD)[None, :]
    other = jnp.where(docs[:, None] == lane, 0.0, -1.0)
    return jnp.where(lane < count, other, jnp.where(lane < 7, 1.0, 0.0)).astype(jnp.bfloat16)


MODEL = 1024
TILE = 512


def wide(values):
    return values.astype(jnp.float32)


def short(values):
    return values.astype(jnp.bfloat16)


def gathered(ref):
    return ref[...].reshape(-1, ref.shape[-1])


def once(shape, index):
    return pl.BlockSpec(shape, index, pipeline_mode=pl.Buffered(1))


def weight_at(slot):
    return once((16, 64, MODEL), lambda *_: (0, slot, 0))


def norm_rows():
    return once((8, MODEL), lambda *_: (0, 0))


def by_rows(count, width=MODEL):
    return pl.BlockSpec((count, width), lambda i, *_: (i, 0))


def found_rows(count):
    return pl.BlockSpec((count, MODEL), lambda i, held, *_: (held[i], 0))


def sums_out():
    return pl.BlockSpec((8, MODEL), lambda *_: (0, 0))


def struct(shape, kind):
    return jax.ShapeDtypeStruct(shape, kind)


def spread_of(values):
    mean = jnp.mean(values, axis=-1, keepdims=True)
    centred = values - mean
    scale = lax.rsqrt(jnp.mean(centred * centred, axis=-1, keepdims=True) + 1e-05)
    return (centred * scale, scale)


def norm_of(values, norm_ref, k):
    hat, _ = spread_of(values)
    return short(hat * norm_ref[k : k + 1] + norm_ref[3 + k : 4 + k])


def norm_back(values, grad, norm_ref, k, sums_ref):
    hat, scale = spread_of(values)
    each = grad * norm_ref[k : k + 1]
    inner = each - jnp.mean(each, axis=-1, keepdims=True)
    inner = inner - hat * jnp.mean(each * hat, axis=-1, keepdims=True)
    sums_ref[0:1] += jnp.sum(grad * hat, axis=0, keepdims=True)
    sums_ref[1:2] += jnp.sum(grad, axis=0, keepdims=True)
    return scale * inner


def call(kernel, grid, in_specs, out_specs, out_shape, scratch=(), prefetch=0):
    return pl.pallas_call(
        kernel,
        grid_spec=pltpu.PrefetchScalarGridSpec(
            num_scalar_prefetch=prefetch,
            grid=grid,
            in_specs=in_specs,
            out_specs=out_specs,
            scratch_shapes=list(scratch),
        ),
        out_shape=out_shape,
        compiler_params=pltpu.CompilerParams(vmem_limit_bytes=58 * 2**20),
        cost_estimate=small_cost(),
    )


def pack_kernel(*refs):
    attention_ref, feed_ref = refs[-2:]
    self_in, self_out, cross_q, cross_s, cross_out, feed_in, feed_out, norms = refs[:-2]
    rows = self_in.shape[0]
    slot = 0
    for ref in (self_in, self_out, cross_q, cross_s, cross_out):
        for start in range(0, ref.shape[1], MODEL):
            attention_ref[slot * rows : (slot + 1) * rows] = ref[:, start : start + MODEL]
            slot += 1
    attention_ref[slot * rows :] = norms[...]
    piece = feed_out.shape[0] // 2
    for lot in range(2):
        for owner in range(16):
            column = (2 * owner + lot) * piece
            slot, spot = (2 * lot + owner // 8, owner % 8 * piece)
            feed_ref[slot * rows : (slot + 1) * rows, spot : spot + piece] = feed_in[
                :, column : column + piece
            ]
    feed_ref[4 * rows : 8 * rows] = feed_out[...]
    feed_ref[8 * rows :] = jnp.zeros_like(norms)


def pack(weights, norms):
    arrays = tuple(weights) + (norms,)
    out = struct((528, MODEL), jnp.bfloat16)
    return call(
        pack_kernel,
        (1,),
        [once(a.shape, lambda i: (0, 0)) for a in arrays],
        [once(out.shape, lambda i: (0, 0))] * 2,
        [out] * 2,
    )(*arrays)


def enter_kernel(held, tokens_ref, norm_ref, wq, wk, wv, first_ref, q_ref, k_ref, v_ref):
    first = norm_of(wide(tokens_ref[...]), norm_ref, 0)
    first_ref[...] = first
    for weight, out in ((wq, q_ref), (wk, k_ref), (wv, v_ref)):
        out[...] = short(dot(first, gathered(weight)))


def enter(held, tokens, norms, weights, width):
    shape = struct(tokens.shape, jnp.bfloat16)
    return call(
        enter_kernel,
        (tokens.shape[0] // width,),
        [found_rows(width), norm_rows()] + [weight_at(i) for i in range(3)],
        [by_rows(width)] * 4,
        [shape] * 4,
        prefetch=1,
    )(held, tokens, norms, weights, weights, weights)


def source_kernel(source_ref, wk, wv, k_ref, v_ref):
    source = source_ref[...]
    k_ref[...] = short(dot(source, gathered(wk)))
    v_ref[...] = short(dot(source, gathered(wv)))


def source_pairs(source, weights, width):
    return call(
        source_kernel,
        (source.shape[0] // width,),
        [by_rows(width), weight_at(5), weight_at(6)],
        [by_rows(width)] * 2,
        [struct(source.shape, jnp.bfloat16)] * 2,
    )(source, weights, weights)


def between_kernel(held, mixed_ref, tokens_ref, norm_ref, wo, wq, after_ref, second_ref, q_ref):
    after = wide(tokens_ref[...]) + dot(mixed_ref[...], gathered(wo))
    after_ref[...] = after
    second = norm_of(after, norm_ref, 1)
    second_ref[...] = second
    q_ref[...] = short(dot(second, gathered(wq)))


def between(held, mixed, tokens, norms, weights, width):
    return call(
        between_kernel,
        (mixed.shape[0] // width,),
        [by_rows(width), found_rows(width), norm_rows(), weight_at(3), weight_at(4)],
        [by_rows(width)] * 3,
        [struct(mixed.shape, kind) for kind in (jnp.float32, jnp.bfloat16, jnp.bfloat16)],
        prefetch=1,
    )(held, mixed, tokens, norms, weights, weights)


def before_feed_kernel(
    held, mixed_ref, base_ref, own_ref, other_ref, norm_ref, wo, after_ref, third_ref, grad_ref
):
    after = base_ref[...] + dot(mixed_ref[...], gathered(wo))
    after_ref[...] = after
    third_ref[...] = norm_of(after, norm_ref, 2)
    own = held[pl.program_id(0)] < 2

    @pl.when(own)
    def _():
        grad_ref[...] = own_ref[...]

    @pl.when(jnp.logical_not(own))
    def _():
        grad_ref[...] = other_ref[...]


def before_feed(held, mixed, base, own, other, norms, weights, width):
    return call(
        before_feed_kernel,
        (mixed.shape[0] // width,),
        [
            by_rows(width),
            by_rows(width),
            pl.BlockSpec((width, MODEL), lambda i, held: (jnp.minimum(held[i], 1), 0)),
            pl.BlockSpec((width, MODEL), lambda i, held: (jnp.maximum(held[i] - 2, 0), 0)),
            norm_rows(),
            weight_at(7),
        ],
        [by_rows(width)] * 3,
        [struct(mixed.shape, kind) for kind in (jnp.float32, jnp.bfloat16, jnp.bfloat16)],
        prefetch=1,
    )(held, mixed, base, own, other, norms, weights)


def gelu_terms(hidden):
    bell = jnp.exp2(hidden * hidden * (-0.5 * math.log2(math.e)))
    t = 1.0 / (1.0 + (0.3275911 / math.sqrt(2.0)) * jnp.abs(hidden))
    series = 1.061405429
    for term in (-1.453152027, 1.421413741, -0.284496736, 0.254829592):
        series = series * t + term
    tail = 0.5 * series * t * bell
    return (jnp.where(hidden < 0, tail, 1.0 - tail), bell * (1.0 / math.sqrt(2.0 * math.pi)))


def deal(place_ref, turned, keep_ref, send_ref, pieces, own_y=True):
    for own in range(2):

        @pl.when(place_ref[0] == own)
        def _(own=own):
            for core, x, y, index, value in pieces:
                rel_x = jnp.bitwise_xor(place_ref[1], x)
                rel_y = jnp.bitwise_xor(place_ref[2], y) if own_y else y
                spot = (rel_y, rel_x) if turned else (rel_x, rel_y)
                ref = keep_ref if core == own else send_ref
                ref[spot + index] = value


def shard_pieces(product, slot, *rest):
    pieces = []
    for owner in range(product.shape[0] // 64):
        for y in range(2):
            start = owner * 64 + y * 32
            index = (owner // 4, slot) + rest
            value = short(product[start : start + 32])
            pieces.append((owner % 2, owner // 2 % 2, y, index, value))
    return pieces


def feed_kernel(
    place_ref,
    third_ref,
    grad_ref,
    win_ref,
    wout_ref,
    out_ref,
    back_ref,
    keep_a,
    send_a,
    keep_b,
    send_b,
    third_t,
    active_ref,
    hidden_ref,
):
    step = pl.program_id(0)

    @pl.when(step == 0)
    def _():
        third_t[...] = third_ref[...].T
        out_ref[...] = jnp.zeros_like(out_ref)
        back_ref[...] = jnp.zeros_like(back_ref)

    win, wout = (gathered(win_ref), gathered(wout_ref))
    rows = third_ref.shape[0]
    lots = [slice(start, start + TILE) for start in range(0, rows, TILE)]

    def enter(lot):
        return (dot(third_ref[lot], win), dot(grad_ref[lot], wout, NT))

    def leave(lot, hidden, grad):
        mass, bell = gelu_terms(hidden)
        active = short(hidden * mass)
        grad = short((mass + hidden * bell) * wide(short(grad)))
        active_ref[lot] = active
        hidden_ref[lot] = grad
        out_ref[lot] += dot(active, wout)
        back_ref[lot] += dot(grad, win, NT)

    ready = enter(lots[0])
    for index, lot in enumerate(lots):
        following = enter(lots[index + 1]) if index + 1 < len(lots) else None
        leave(lot, *ready)
        ready = following
    grad_out = short(dot(active_ref[...], grad_ref[...], TN))
    grad_in = short(dot(third_t[...], hidden_ref[...]))
    turn = lax.rem(step, 4)
    side = pl.ds(pl.multiple_of(lax.rem(turn, 2) * TILE, TILE), TILE)
    pieces = shard_pieces(grad_in, turn // 2, slice(None), side)
    for owner in range(4):
        for y in range(2):
            for half in range(2):
                start = owner * 128 + y * 64 + 32 * half
                value = grad_out[start : start + 32]
                pieces.append((owner % 2, owner // 2, y, (turn, 2 + half), value))

    @pl.when(step < 4)
    def _():
        deal(place_ref, False, keep_a, send_a, pieces)

    @pl.when(step >= 4)
    def _():
        deal(place_ref, True, keep_b, send_b, pieces)


def feed(place, third, grad, weights):
    rows = third.shape[0]
    full = struct((rows, MODEL), jnp.float32)
    buffer = struct((2, 2, 4, 4, 32, MODEL), jnp.bfloat16)
    out, back, *lots = call(
        feed_kernel,
        (8,),
        [
            once((rows, MODEL), lambda t, place: (0, 0)),
            once((rows, MODEL), lambda t, place: (0, 0)),
            pl.BlockSpec((16, 64, TILE), lambda t, place: (0, t // 2, t % 2)),
            pl.BlockSpec((4, 128, MODEL), lambda t, place: (t % 4, 2 + t // 4, 0)),
        ],
        [once((rows, MODEL), lambda t, place: (0, 0))] * 2
        + [once(buffer.shape, lambda t, place: (0, 0, 0, 0, 0, 0))] * 4,
        [full, full] + [buffer] * 4,
        scratch=[
            pltpu.VMEM((MODEL, rows), jnp.bfloat16),
            pltpu.VMEM((rows, TILE), jnp.bfloat16),
            pltpu.VMEM((rows, TILE), jnp.bfloat16),
        ],
        prefetch=1,
    )(place, third, grad, weights, weights)
    return out, back, lots[:2], lots[2:]


def clear(*refs):
    @pl.when(pl.program_id(0) == 0)
    def _():
        for ref in refs:
            ref[...] = jnp.zeros_like(ref)


def add_product(total_ref, left, right):
    total_ref[...] += dot(left, right, TN)


def at_end(store):
    pl.when(pl.program_id(0) == pl.num_programs(0) - 1)(store)


def buffer_of(slots):
    return struct((2, 2, 4, slots, 32, MODEL), jnp.bfloat16)


def slots_at(slots):
    return once((2, 2, 4, slots, 32, MODEL), lambda *_: (0,) * 6)


def after_feed_kernel(
    held,
    place,
    after_ref,
    out_ref,
    back_ref,
    grad_ref,
    cross_ref,
    norm_ref,
    wo,
    result_ref,
    total_ref,
    mixed_ref,
    sums_ref,
    keep_ref,
    send_ref,
    weight_ref,
):
    clear(sums_ref, weight_ref)
    after = after_ref[...]
    result_ref[...] = short(after + out_ref[...])
    part = norm_back(after, back_ref[...], norm_ref, 2, sums_ref)
    total = wide(grad_ref[...]) + part
    total_ref[...] = total
    branch = short(total)
    mixed_ref[...] = short(dot(branch, gathered(wo), NT))
    add_product(weight_ref, cross_ref[...], branch)
    at_end(lambda: deal(place, False, keep_ref, send_ref, shard_pieces(weight_ref, 0)))


def after_feed(held, place, after, out, back, grad, mixed, norms, weights, width):
    narrow = struct(after.shape, jnp.bfloat16)
    full = struct(after.shape, jnp.float32)
    return call(
        after_feed_kernel,
        (after.shape[0] // width,),
        [by_rows(width)] * 5 + [norm_rows(), weight_at(7)],
        [found_rows(width)] + [by_rows(width)] * 2 + [sums_out()] + [slots_at(1)] * 2,
        [narrow, full, narrow, struct((8, MODEL), jnp.float32)] + [buffer_of(1)] * 2,
        scratch=[pltpu.VMEM((MODEL, MODEL), jnp.float32)],
        prefetch=2,
    )(held, place, after, out, back, grad, mixed, norms, weights)


def middle_kernel(
    place,
    grad_ref,
    second_ref,
    after_ref,
    base_ref,
    self_ref,
    norm_ref,
    wq,
    wo,
    *refs,
):
    total_ref, mixed_ref, sums_ref, keep_ref, send_ref, weight_q, weight_o = refs
    clear(sums_ref, weight_q, weight_o)
    grad_q = grad_ref[...]
    grad = dot(grad_q, gathered(wq), NT)
    add_product(weight_q, second_ref[...], grad_q)
    total = base_ref[...] + norm_back(after_ref[...], grad, norm_ref, 1, sums_ref)
    total_ref[...] = total
    branch = short(total)
    mixed_ref[...] = short(dot(branch, gathered(wo), NT))
    add_product(weight_o, self_ref[...], branch)

    @at_end
    def _():
        deal(place, False, keep_ref, send_ref, shard_pieces(weight_q, 0))
        deal(place, False, keep_ref, send_ref, shard_pieces(weight_o, 1))


def middle(place, grad, second, after, base, mixed, norms, weights, width):
    narrow = struct(after.shape, jnp.bfloat16)
    return call(
        middle_kernel,
        (after.shape[0] // width,),
        [by_rows(width)] * 5 + [norm_rows(), weight_at(4), weight_at(3)],
        [by_rows(width)] * 2 + [sums_out()] + [slots_at(2)] * 2,
        [struct(after.shape, jnp.float32), narrow, struct((8, MODEL), jnp.float32)]
        + [buffer_of(2)] * 2,
        scratch=[pltpu.VMEM((MODEL, MODEL), jnp.float32)] * 2,
        prefetch=1,
    )(place, grad, second, after, base, mixed, norms, weights, weights)


def project_grad_kernel(place, left_ref, right_ref, keep_ref, send_ref, left_t):
    @pl.when(pl.program_id(1) == 0)
    def _():
        left_t[...] = left_ref[...].T

    product = dot(left_t[...], right_ref[0])
    deal(place, False, keep_ref, send_ref, shard_pieces(product, 0), own_y=False)


def project_grad(place, left, right):
    rows = left.shape[0]
    block = (2, 2, TILE // 256, 1, 32, MODEL)
    return call(
        project_grad_kernel,
        (MODEL // TILE, 3),
        [
            pl.BlockSpec((rows, TILE), lambda t, n, place: (0, t)),
            pl.BlockSpec((1, rows, MODEL), lambda t, n, place: (n, 0, 0)),
        ],
        [pl.BlockSpec(block, lambda t, n, place: (0, 0, t, n, 0, 0))] * 2,
        [buffer_of(3)] * 2,
        scratch=[pltpu.VMEM((TILE, rows), jnp.bfloat16)],
        prefetch=1,
    )(place, left, right)


def finish_kernel(
    held, grads_ref, tokens_ref, base_ref, norm_ref, wq, wk, wv, result_ref, sums_ref
):
    clear(sums_ref)
    grad = sum(dot(grads_ref[i], gathered(w), NT) for i, w in enumerate((wq, wk, wv)))
    part = norm_back(wide(tokens_ref[...]), grad, norm_ref, 0, sums_ref)
    result_ref[...] = short(base_ref[...] + part)


def finish(held, grads, tokens, base, norms, weights, width):
    return call(
        finish_kernel,
        (base.shape[0] // width,),
        [
            pl.BlockSpec((3, width, MODEL), lambda i, *_: (0, i, 0)),
            found_rows(width),
            by_rows(width),
            norm_rows(),
        ]
        + [weight_at(i) for i in range(3)],
        [found_rows(width), sums_out()],
        [struct(base.shape, jnp.bfloat16), struct((8, MODEL), jnp.float32)],
        prefetch=1,
    )(held, grads, tokens, base, norms, weights, weights, weights)


def source_back_kernel(
    place, grads_ref, source_ref, wk, wv, out_ref, keep_ref, send_ref, weight_ref
):
    clear(weight_ref)
    source = source_ref[...].T
    for i in range(2):
        weight_ref[i] += dot(source, grads_ref[i])
    grad = dot(grads_ref[0], gathered(wk), NT) + dot(grads_ref[1], gathered(wv), NT)
    out_ref[...] = short(grad)

    @at_end
    def _():
        for i in range(2):
            deal(place, False, keep_ref, send_ref, shard_pieces(weight_ref.at[i], i))


def source_back(place, grads, source, weights, width):
    rows = grads.shape[1]
    return call(
        source_back_kernel,
        (rows // width,),
        [
            pl.BlockSpec((2, width, MODEL), lambda i, *_: (0, i, 0)),
            by_rows(width),
            weight_at(5),
            weight_at(6),
        ],
        [
            pl.BlockSpec(
                (width, MODEL), lambda i, place: (jnp.bitwise_xor(i, place[2]), 0)
            )
        ]
        + [slots_at(2)] * 2,
        [struct((rows, MODEL), jnp.bfloat16)] + [buffer_of(2)] * 2,
        scratch=[pltpu.VMEM((2, MODEL, MODEL), jnp.float32)],
        prefetch=1,
    )(place, grads, source, weights, weights)


def pairs(bit):
    return [(i, i ^ bit) for i in range(16)]


def swap(values):
    return lax.ppermute(values, "ctx", [(0, 1), (1, 0)])


def over_x(values):
    return lax.ppermute(values, "fsdp", pairs(2))


def over_core(values):
    return lax.ppermute(values, "fsdp", pairs(1))


def tie(*values):
    return lax.optimization_barrier(values)


def lot_specs(lot, first, second, spread, z_of, depth=1):
    specs = []
    for keep, _ in lot:
        slots, rows = keep.shape[3:5]
        block = (1, spread, depth, slots, rows, MODEL)
        specs += [
            pl.BlockSpec(block, lambda i, place: (first, second, z_of(i, place), 0, 0, 0))
        ] * 2
    return specs


def slots_of(lot):
    return sum(keep.shape[3] for keep, _ in lot)


def in_order(i, place):
    return i


def from_own(i, place):
    return lax.rem(place[3] + i, 4)


def pair_sums(refs, count):
    return [wide(refs[2 * i][...]) + wide(refs[2 * i + 1][...]) for i in range(count)]


def depth_of(lots):
    return 4 if sum(slots_of(lot) for lot in lots) < 4 else 1


def ranges(sizes):
    starts = [sum(sizes[:i]) for i in range(len(sizes))]
    return [(start, start + size) for start, size in zip(starts, sizes)]


def overlaps(sources, pieces):
    for i, (s0, s1) in enumerate(ranges(sources)):
        for j, (p0, p1) in enumerate(ranges(pieces)):
            low, high = (max(s0, p0), min(s1, p1))
            if low < high:
                yield i, j, slice(low - s0, high - s0), slice(low - p0, high - p0)


def sizes_of(lot):
    return [keep.shape[3] for keep, _ in lot]


def first_sums(place, lots, cuts=None):
    cuts = cuts or [[slots_of(lot)] for lot in lots]

    def kernel(place_ref, *refs):
        refs = list(refs)
        outs = refs[-sum(len(cut) for cut in cuts) :]
        for lot, cut in zip(lots, cuts):
            values = pair_sums([refs.pop(0) for _ in range(2 * len(lot))], len(lot))
            pieces, outs = (outs[: len(cut)], outs[len(cut) :])
            for i, j, taken, put in overlaps(sizes_of(lot), cut):
                pieces[j][:, :, put] = short(values[i][0, :, :, taken])

    depth = depth_of(lots)
    shapes = [(2, 4, size, 32, MODEL) for cut in cuts for size in cut]
    outs = call(
        kernel,
        (4 // depth,),
        [spec for lot in lots for spec in lot_specs(lot, 1, 0, 2, in_order, depth)],
        [
            pl.BlockSpec((2, depth) + shape[2:], lambda i, place: (0, i, 0, 0, 0))
            for shape in shapes
        ],
        [struct(shape, jnp.bfloat16) for shape in shapes],
        prefetch=1,
    )(place, *[array for lot in lots for pair in lot for array in pair])
    return [outs[start:end] for start, end in ranges([len(cut) for cut in cuts])]


def second_sums(place, lots, firsts, cuts=None):
    cuts = cuts or [[slots_of(lot)] for lot in lots]

    def kernel(place_ref, *refs):
        refs = list(refs)
        outs = refs[-sum(len(cut) for cut in cuts) :]
        for lot, first, cut in zip(lots, firsts, cuts):
            values = pair_sums([refs.pop(0) for _ in range(2 * len(lot))], len(lot))
            received = [wide(refs.pop(0)[0]) for _ in first]
            received = received[0] if len(first) == 1 else jnp.concatenate(received, axis=1)
            pieces, outs = (outs[: len(cut)], outs[len(cut) :])
            spots = ranges(sizes_of(lot))
            for i, j, taken, put in overlaps(sizes_of(lot), cut):
                there = received[:, spots[i][0] + taken.start : spots[i][0] + taken.stop]
                pieces[j][:, put] = short(values[i][0, 0, :, taken] + there)

    depth = depth_of(lots)
    specs, arrays = ([], [])
    for lot, first in zip(lots, firsts):
        specs += lot_specs(lot, 0, 1, 1, in_order, depth)
        specs += [
            pl.BlockSpec((1, depth) + piece.shape[2:], lambda i, place: (1, i, 0, 0, 0))
            for piece in first
        ]
        arrays += [array for pair in lot for array in pair] + list(first)
    shapes = [(4, size, 32, MODEL) for cut in cuts for size in cut]
    outs = call(
        kernel,
        (4 // depth,),
        specs,
        [pl.BlockSpec((depth,) + shape[1:], lambda i, place: (i, 0, 0, 0)) for shape in shapes],
        [struct(shape, jnp.bfloat16) for shape in shapes],
        prefetch=1,
    )(place, *arrays)
    return [outs[start:end] for start, end in ranges([len(cut) for cut in cuts])]


def third_sums(place, lots, firsts, seconds):
    def kernel(place_ref, *refs):
        refs = list(refs)
        out = refs[-1]
        start = 0
        for lot, first, second in zip(lots, firsts, seconds):
            values = pair_sums([refs.pop(0) for _ in range(2 * len(lot))], len(lot))
            parts_of = (
                [wide(refs.pop(0)[0, 0]) for _ in first],
                [wide(refs.pop(0)[0]) for _ in second],
            )
            received = sum(p[0] if len(p) == 1 else jnp.concatenate(p, axis=0) for p in parts_of)
            for value, (s0, s1) in zip(values, ranges(sizes_of(lot))):
                out[0, start + s0 : start + s1] = short(value[0, 0, 0] + received[s0:s1])
            start += slots_of(lot)

    specs, arrays = ([], [])
    for lot, first, second in zip(lots, firsts, seconds):
        specs += lot_specs(lot, 0, 0, 1, in_order)
        specs += [
            pl.BlockSpec((1, 1) + piece.shape[2:], lambda i, place: (0, i, 0, 0, 0))
            for piece in first
        ]
        specs += [
            pl.BlockSpec((1,) + piece.shape[1:], lambda i, place: (i, 0, 0, 0))
            for piece in second
        ]
        arrays += [array for pair in lot for array in pair] + list(first) + list(second)
    shape = (4, sum(slots_of(lot) for lot in lots), 32, MODEL)
    return call(
        kernel,
        (4,),
        specs,
        [pl.BlockSpec((1,) + shape[1:], lambda i, place: (i, 0, 0, 0))],
        [struct(shape, jnp.bfloat16)],
        prefetch=1,
    )(place, *arrays)[0]


def direct_sums(place, lot, first):
    (keep, core) = lot
    slots = keep.shape[3]

    def kernel(place_ref, keep_ref, core_ref, *refs):
        received = [wide(ref[...]) for ref in refs[:-1]]
        received = received[0] if len(first) == 1 else jnp.concatenate(received, axis=2)
        total = wide(keep_ref[0]) + wide(core_ref[0]) + received
        refs[-1][0] = short(total[:, 0])

    block = (1, 2, 1, slots, 32, MODEL)
    shape = (4, 2, slots, 32, MODEL)
    return call(
        kernel,
        (4,),
        [pl.BlockSpec(block, lambda i, place: (0, 0, i, 0, 0, 0))] * 2
        + [
            pl.BlockSpec((2, 1) + piece.shape[2:], lambda i, place: (0, i, 0, 0, 0))
            for piece in first
        ],
        [pl.BlockSpec((1,) + shape[1:], lambda i, place: (i, 0, 0, 0, 0))],
        [struct(shape, jnp.bfloat16)],
        prefetch=1,
    )(place, keep, core, *first)[0]


def over_z(values):
    groups = [[first + 4 * z for z in range(4)] for first in range(4)]
    return lax.psum_scatter(values, "fsdp", scatter_dimension=0, axis_index_groups=groups)


def both_parts(total, other):
    low = lax.axis_index("ctx") == 0
    return wide(jnp.stack([jnp.where(low, total, other), jnp.where(low, other, total)], axis=1))


def columns(shares, start, stop):
    part = shares[start:stop].reshape(stop - start, -1, MODEL)
    return jnp.concatenate(list(part), axis=1)


def feed_shares(lots):
    inner = [lot[:2].reshape(2, 64, 8, 128).transpose(1, 0, 2, 3).reshape(64, 16, 128) for lot in lots]
    inner = jnp.stack(inner, axis=2).reshape(64, 4 * MODEL)
    outer = [lot[2:].transpose(1, 0, 2, 3).reshape(128, MODEL) for lot in lots]
    return inner, jnp.concatenate(outer)


def whole_packs(mesh):
    return mesh.shape["ctx"] == 2 and mesh.shape["fsdp"] == 16


def whole_pack_body(
    tokens,
    encoded,
    cotangent,
    order,
    target_lengths,
    source_lengths,
    self_project,
    self_output,
    cross_query,
    cross_source,
    cross_output,
    feed_in,
    feed_out,
    norm_gain,
    norm_bias,
):
    rows = tokens.shape[2]
    pack_rows, source_rows = (2 * rows, 2 * encoded.shape[2])
    first_rows = 3 * pack_rows // 4
    width = rows // 2
    mine = lax.axis_index("ctx")
    spot = lax.axis_index("fsdp")
    z = spot // 4
    place = jnp.stack([spot % 2, spot // 2 % 2, mine, z]).astype(jnp.int32)
    part = self_project.shape[0]

    norms = jnp.pad(jnp.concatenate([norm_gain, norm_bias]), ((0, 10), (0, MODEL - part)))
    attention_shard, feed_shard = pack(
        (self_project, self_output, cross_query, cross_source, cross_output, feed_in, feed_out),
        norms,
    )
    weights = lax.all_gather(attention_shard, "fsdp", axis=0)
    norms = wide(weights[:, 8 * part : 8 * part + 8, :part])
    norms = norms.transpose(1, 0, 2).reshape(8, MODEL)

    def both_halves(array):
        own = lax.dynamic_index_in_dim(array, mine, 0, False)[0]
        return own, swap(lax.dynamic_index_in_dim(array, 1 - mine, 0, False)[0])

    places = lax.dynamic_index_in_dim(order, mine, 0, False)[0]
    holds = places[::width] // width
    found = jnp.argsort(holds).astype(jnp.int32)
    held = jnp.where(found // 2 == mine, found % 2, 2 + found % 2)

    def from_both(own, other):
        low = mine == 0
        return jnp.stack([jnp.where(low, own, other), jnp.where(low, other, own)])[:, None]

    halves = jnp.concatenate(both_halves(tokens))
    own, other = both_halves(encoded)
    source = jnp.concatenate([jnp.where(mine == 0, own, other), jnp.where(mine == 0, other, own)])
    feed_shard, halves, source = tie(feed_shard, halves, source)
    feed_weights = lax.all_gather(feed_shard, "fsdp", axis=0)

    lengths = lax.dynamic_index_in_dim(target_lengths, mine, 0, False)[0]
    target_docs = docs_of(jnp.arange(pack_rows, dtype=jnp.int32), lengths)
    lengths = lax.dynamic_index_in_dim(source_lengths, mine, 0, False)[0]
    source_docs = docs_of(jnp.arange(source_rows, dtype=jnp.int32), lengths)
    docs = lengths.shape[0]
    marks = query_marks(target_docs)
    target_marks = key_marks(target_docs, docs)
    source_marks = key_marks(source_docs, docs)
    reach = source_rows // 2

    first, query, keys, values = enter(held, halves, norms, weights, width)
    query, cotangent = tie(query, cotangent)
    cotangents = both_halves(cotangent)
    plan = self_plan(first_rows, pack_rows, width)
    self_mixed, self_extra = attend(plan, query, keys, values, marks, target_marks)
    self_mixed, source = tie(self_mixed, source)
    cross_keys, cross_values = source_pairs(source, weights, source_rows // 2)
    after_self, second, cross_queries = between(held, self_mixed, halves, norms, weights, width)
    plan = cross_plan(first_rows, pack_rows, reach, source_rows, width // 2)
    cross_mixed, cross_extra = attend(
        plan, cross_queries, cross_keys, cross_values, marks, source_marks
    )
    after_cross, third, grad_out = before_feed(
        held, cross_mixed, after_self, *cotangents, norms, weights, width
    )

    out, back, lot_a, lot_b = feed(place, third, grad_out, feed_weights)
    lot_a, lot_b = ([(lot[0], over_core(lot[1]))] for lot in (lot_a, lot_b))
    result, grad_after_cross, grad_cross_mixed, sums_two, *part_out = after_feed(
        held, place, after_cross, out, back, grad_out, cross_mixed, norms, weights, width
    )
    (first_a,), (first_b,) = first_sums(place, [lot_a, lot_b])
    first_ab = (first_a, first_b)
    grad_cross_mixed, part_out[1], *first_ab = tie(grad_cross_mixed, part_out[1], *first_ab)
    first_ab = (over_x(first_ab[0]), swap(first_ab[1]))
    part_out[1] = over_core(part_out[1])
    plan = cross_plan(first_rows, pack_rows, reach, source_rows, width)
    grad_cross_queries, grad_source = attend_back(
        plan,
        cross_queries,
        cross_keys,
        cross_values,
        cross_extra,
        source_marks,
        cross_mixed,
        grad_cross_mixed,
        False,
    )
    grad_source, part_out[1], *first_ab = tie(grad_source, part_out[1], *first_ab)
    grad_encoded, *part_source = source_back(place, grad_source, source, weights, source_rows // 2)
    encoded_own = grad_encoded[: source_rows // 2]
    away = jnp.concatenate([result[rows:], grad_encoded[source_rows // 2 :]])
    first_ab = [[first] for first in first_ab]
    second_ab = [second for (second,) in second_sums(place, [lot_a, lot_b], first_ab)]
    grad_cross_queries, encoded_own, away, *second_ab = tie(
        grad_cross_queries, encoded_own, away, *second_ab
    )
    second_ab = (swap(second_ab[0]), over_x(second_ab[1]))
    grad_after_self, grad_self_mixed, sums_one, *part_middle = middle(
        place,
        grad_cross_queries,
        second,
        after_self,
        grad_after_cross,
        self_mixed,
        norms,
        weights,
        width,
    )
    grad_self_mixed, part_source[1], part_middle[1], *second_ab = tie(
        grad_self_mixed, part_source[1], part_middle[1], *second_ab
    )
    part_source[1], part_middle[1] = (over_core(part_source[1]), over_core(part_middle[1]))
    third_ab = third_sums(place, [lot_a, lot_b], first_ab, [[second] for second in second_ab])
    lot_c = [part_out, part_source, part_middle]
    ((first_c,),) = first_sums(place, [lot_c])
    grad_self_mixed, first_c, away, third_ab = tie(grad_self_mixed, first_c, away, third_ab)
    first_c = over_x(first_c)
    away = swap(away)
    total_ab = over_z(third_ab)
    plan = self_plan(first_rows, pack_rows, width)
    grads = attend_back(
        plan,
        query,
        keys,
        values,
        self_extra,
        target_marks,
        self_mixed,
        grad_self_mixed,
        True,
    )
    grads, first_c, away, total_ab = tie(grads, first_c, away, total_ab)
    (second_c,) = second_sums(place, [lot_c], [[first_c]], [[3, 2]])
    grads, total_ab, *second_c = tie(grads, total_ab, *second_c)
    second_c[0] = swap(second_c[0])
    lot_d = list(project_grad(place, first, grads))
    lot_d[1], total_ab, *second_c = tie(lot_d[1], total_ab, *second_c)
    second_c[1] = swap(second_c[1])
    lot_d = [(lot_d[0], over_core(lot_d[1]))]
    (first_d,) = first_sums(place, [lot_d], [[2, 1]])
    second_c[1], *first_d = tie(second_c[1], *first_d)
    third_c = third_sums(place, [lot_c], [[first_c]], [second_c])
    grads, third_c, total_ab, *first_d = tie(grads, third_c, total_ab, *first_d)
    total_c, other_ab = (over_z(third_c), swap(total_ab))
    first_d[0] = over_x(first_d[0])
    grad_tokens, sums_zero = finish(held, grads, halves, grad_after_self, norms, weights, width)
    grad_tokens, sums_zero, other_ab, *first_d = tie(grad_tokens, sums_zero, other_ab, *first_d)
    first_d[1] = over_x(first_d[1])
    tokens_other = swap(grad_tokens[rows:])
    third_d = direct_sums(place, lot_d[0], first_d)
    sums_zero, other_ab, third_d, result, encoded_own, away = tie(
        sums_zero, other_ab, third_d, result, encoded_own, away
    )
    total_d = over_z(third_d)
    result = from_both(result[:rows], away[:rows])
    grad_encoded = from_both(encoded_own, away[rows:])
    sums = jnp.concatenate([sums_zero[:2], sums_one[:2], sums_two[:2]])
    for bit in (1, 2, 4, 8):
        sums = sums + lax.ppermute(sums, "fsdp", pairs(bit))
    sums = sums + swap(sums)
    share_ab = both_parts(total_ab, other_ab)
    feed_in_grad, feed_out_grad = feed_shares((share_ab[:4], share_ab[4:]))
    share_c = both_parts(total_c, swap(total_c))
    grad_tokens = from_both(grad_tokens[:rows], tokens_other)
    tied = (sums, result, grad_encoded, grad_tokens, feed_in_grad, feed_out_grad, share_c, total_d)
    sums, result, grad_encoded, grad_tokens, feed_in_grad, feed_out_grad, share_c, total_d = tie(
        *tied
    )
    share_d = (wide(total_d) + wide(swap(total_d))).transpose(1, 0, 2, 3)

    sums = lax.dynamic_slice_in_dim(sums, spot * part, part, 1)

    return (
        result,
        grad_tokens,
        grad_encoded,
        columns(share_d, 0, 3),
        columns(share_c, 4, 5),
        columns(share_c, 3, 4),
        columns(share_c, 1, 3),
        columns(share_c, 0, 1),
        feed_in_grad,
        feed_out_grad,
        sums[0::2],
        sums[1:4:2],
        sums[5],
    )


def solution(mesh):
    chosen = whole_pack_body if whole_packs(mesh) else body
    return jax.shard_map(
        chosen,
        mesh=mesh,
        in_specs=(
            P(None, "fsdp", "ctx", None),
            P(None, "fsdp", "ctx", None),
            P(None, "fsdp", "ctx", None),
            P(None, "fsdp", None),
            P(None, "fsdp", None),
            P(None, "fsdp", None),
            P("fsdp", None),
            P("fsdp", None),
            P("fsdp", None),
            P("fsdp", None),
            P("fsdp", None),
            P("fsdp", None),
            P("fsdp", None),
            P(None, "fsdp"),
            P(None, "fsdp"),
        ),
        out_specs=(
            P(None, "fsdp", "ctx", None),
            P(None, "fsdp", "ctx", None),
            P(None, "fsdp", "ctx", None),
            P("fsdp", None),
            P("fsdp", None),
            P("fsdp", None),
            P("fsdp", None),
            P("fsdp", None),
            P("fsdp", None),
            P("fsdp", None),
            P(None, "fsdp"),
            P(None, "fsdp"),
            P("fsdp"),
        ),
        check_vma=False,
    )
```

```python
import functools
import math

import jax
import jax.numpy as jnp
from jax import lax
from jax.experimental import pallas as pl
from jax.experimental.pallas import tpu as pltpu
from jax.sharding import PartitionSpec as P

HEAD = 64


MASKED = -1e30


def as_sent(x):

    def short(part):
        return part.astype(jnp.bfloat16) if part.dtype == jnp.float32 else part

    return jax.tree.map(short, x)


def norm_apply(values, gain, bias):
    mean = jnp.mean(values, axis=-1, keepdims=True)
    centred = values - mean
    spread = jnp.mean(centred * centred, axis=-1, keepdims=True)
    return centred * lax.rsqrt(spread + 1e-05) * gain + bias


def gelu_exact(values):
    return jax.nn.gelu(values, approximate=False)


def docs_of(places, lengths):
    ends = jnp.cumsum(lengths)
    return jnp.sum((places[:, None] >= ends[None, :]).astype(jnp.int32), axis=1)


def split_heads(values):
    return values.reshape(values.shape[0], -1, HEAD)


def block_scores(query, pairs, allowed, start, count):
    model = query.shape[1]
    block = lax.dynamic_slice_in_dim(pairs, start, count, 0)
    scores = jnp.einsum(
        "qhd,khd->hqk",
        split_heads(query),
        split_heads(block[:, :model]),
        preferred_element_type=jnp.float32,
    )
    scores = jnp.where(allowed(start, count)[None], scores * HEAD ** (-0.5), MASKED)
    return (scores, block)


def log_mass(query, pairs, allowed, width):
    rows, model = query.shape
    heads = model // HEAD

    def step(index, carry):
        peak, total = carry
        scores, _ = block_scores(query, pairs, allowed, index * width, width)
        new_peak = jnp.maximum(peak, jnp.max(scores, axis=2))
        total = total * jnp.exp(peak - new_peak) + jnp.sum(
            jnp.exp(scores - new_peak[:, :, None]), axis=2
        )
        return (new_peak, total)

    begin = (jnp.full((heads, rows), MASKED, jnp.float32), jnp.zeros((heads, rows), jnp.float32))
    peak, total = lax.fori_loop(0, pairs.shape[0] // width, step, begin)
    return peak + jnp.log(total)


def attend_forward(query, pairs, allowed, width, log_total):
    rows, model = query.shape

    def step(index, mixed):
        scores, block = block_scores(query, pairs, allowed, index * width, width)
        probs = jnp.exp(scores - log_total[:, :, None]).astype(jnp.bfloat16)
        return mixed + jnp.einsum(
            "hqk,khd->qhd", probs, split_heads(block[:, model:]), preferred_element_type=jnp.float32
        )

    mixed = lax.fori_loop(
        0, pairs.shape[0] // width, step, jnp.zeros((rows, model // HEAD, HEAD), jnp.float32)
    )
    return mixed.reshape(rows, model).astype(jnp.bfloat16)


def score_grads(query, pairs, allowed, grad_mixed, log_total, start, count):
    model = query.shape[1]
    scores, block = block_scores(query, pairs, allowed, start, count)
    probs = jnp.exp(scores - log_total[:, :, None])
    grad_probs = jnp.einsum(
        "qhd,khd->hqk",
        split_heads(grad_mixed),
        split_heads(block[:, model:]),
        preferred_element_type=jnp.float32,
    )
    return (probs, grad_probs, block)


def attend_delta(query, pairs, allowed, grad_mixed, log_total, width):
    rows, model = query.shape

    def step(index, delta):
        probs, grad_probs, _ = score_grads(
            query, pairs, allowed, grad_mixed, log_total, index * width, width
        )
        return delta + jnp.sum(probs * grad_probs, axis=2)

    return lax.fori_loop(
        0, pairs.shape[0] // width, step, jnp.zeros((model // HEAD, rows), jnp.float32)
    )


def attend_query_grad(query, pairs, allowed, grad_mixed, log_total, delta, width):
    rows, model = query.shape

    def step(index, grad):
        probs, grad_probs, block = score_grads(
            query, pairs, allowed, grad_mixed, log_total, index * width, width
        )
        grad_scores = (probs * (grad_probs - delta[:, :, None])).astype(jnp.bfloat16)
        return grad + jnp.einsum(
            "hqk,khd->qhd",
            grad_scores,
            split_heads(block[:, :model]),
            preferred_element_type=jnp.float32,
        )

    grad = lax.fori_loop(
        0, pairs.shape[0] // width, step, jnp.zeros((rows, model // HEAD, HEAD), jnp.float32)
    )
    return (grad.reshape(rows, model) * HEAD ** (-0.5)).astype(jnp.bfloat16)


def key_terms(query, pairs, allowed, grad_mixed, log_total, delta, width, count):
    model = query.shape[1]
    step_width = math.gcd(count, width)

    def step(index, terms):
        probs, grad_probs, _ = score_grads(
            query, pairs, allowed, grad_mixed, log_total, index * step_width, step_width
        )
        grad_scores = (probs * (grad_probs - delta[:, :, None])).astype(jnp.bfloat16)
        grad_keys = jnp.einsum(
            "hqk,qhd->khd", grad_scores, split_heads(query), preferred_element_type=jnp.float32
        ) * HEAD ** (-0.5)
        grad_values = jnp.einsum(
            "hqk,qhd->khd",
            probs.astype(jnp.bfloat16),
            split_heads(grad_mixed),
            preferred_element_type=jnp.float32,
        )
        piece = jnp.concatenate(
            [grad_keys.reshape(step_width, model), grad_values.reshape(step_width, model)], axis=1
        )
        return lax.dynamic_update_slice_in_dim(terms, piece, index * step_width, 0)

    return lax.fori_loop(0, count // step_width, step, jnp.zeros((count, 2 * model), jnp.float32))


def body(
    tokens,
    encoded,
    cotangent,
    order,
    target_lengths,
    source_lengths,
    self_project,
    self_output,
    cross_query,
    cross_source,
    cross_output,
    feed_in,
    feed_out,
    norm_gain,
    norm_bias,
):
    micro = tokens.shape[0]
    rows = tokens.shape[2]
    model = tokens.shape[3]
    source_rows = encoded.shape[2]
    place = lax.axis_index("ctx")
    group = lax.axis_size("ctx")
    pack_total = rows * group
    source_total = source_rows * group
    self_width = math.gcd(pack_total, 512)
    cross_width = math.gcd(source_total, 512)
    results = []
    grad_values_all = []
    grad_encoded_all = []
    totals = ()
    for index in range(micro):
        attention_part = (
            lax.all_gather(self_project, "fsdp", axis=0, tiled=True),
            lax.all_gather(self_output, "fsdp", axis=0, tiled=True),
            lax.all_gather(cross_query, "fsdp", axis=0, tiled=True),
            lax.all_gather(cross_source, "fsdp", axis=0, tiled=True),
            lax.all_gather(cross_output, "fsdp", axis=0, tiled=True),
            lax.all_gather(norm_gain, "fsdp", axis=1, tiled=True),
            lax.all_gather(norm_bias, "fsdp", axis=1, tiled=True),
        )
        feed_part = (
            lax.all_gather(feed_in, "fsdp", axis=0, tiled=True),
            lax.all_gather(feed_out, "fsdp", axis=0, tiled=True),
        )
        weights = tuple(attention_part) + tuple(feed_part)
        (
            self_in_full,
            self_out_full,
            cross_query_full,
            cross_source_full,
            cross_out_full,
            gain_full,
            bias_full,
            feed_in_full,
            feed_out_full,
        ) = weights
        gains = gain_full.astype(jnp.float32)
        biases = bias_full.astype(jnp.float32)
        values = tokens[index, 0].astype(jnp.float32)
        source = encoded[index, 0]
        grad_out = cotangent[index, 0]
        places = order[index, 0]
        target_docs = docs_of(places, target_lengths[index, 0])
        query_places = lax.dynamic_slice_in_dim(places, place * rows, rows)
        query_docs = lax.dynamic_slice_in_dim(target_docs, place * rows, rows)
        source_docs = docs_of(jnp.arange(source_total, dtype=jnp.int32), source_lengths[index, 0])

        def self_allowed(start, count):
            key_docs = lax.dynamic_slice_in_dim(target_docs, start, count)
            key_places = lax.dynamic_slice_in_dim(places, start, count)
            return (query_docs[:, None] == key_docs[None, :]) & (
                key_places[None, :] <= query_places[:, None]
            )

        def cross_allowed(start, count):
            return (
                query_docs[:, None] == lax.dynamic_slice_in_dim(source_docs, start, count)[None, :]
            )

        first = norm_apply(values, gains[0], biases[0]).astype(jnp.bfloat16)
        query = jnp.dot(first, self_in_full[:, :model], preferred_element_type=jnp.float32).astype(
            jnp.bfloat16
        )
        local_pairs = jnp.dot(
            first, self_in_full[:, model:], preferred_element_type=jnp.float32
        ).astype(jnp.bfloat16)
        self_pairs = lax.all_gather(local_pairs, "ctx", axis=0, tiled=True)
        self_total = log_mass(query, self_pairs, self_allowed, self_width)
        self_mixed = attend_forward(query, self_pairs, self_allowed, self_width, self_total)
        after_self = values + jnp.dot(self_mixed, self_out_full, preferred_element_type=jnp.float32)
        second = norm_apply(after_self, gains[1], biases[1]).astype(jnp.bfloat16)
        cross_queries = jnp.dot(
            second, cross_query_full, preferred_element_type=jnp.float32
        ).astype(jnp.bfloat16)
        cross_local = jnp.dot(source, cross_source_full, preferred_element_type=jnp.float32).astype(
            jnp.bfloat16
        )
        cross_pairs = lax.all_gather(cross_local, "ctx", axis=0, tiled=True)
        cross_total = log_mass(cross_queries, cross_pairs, cross_allowed, cross_width)
        cross_mixed = attend_forward(
            cross_queries, cross_pairs, cross_allowed, cross_width, cross_total
        )
        after_cross = after_self + jnp.dot(
            cross_mixed, cross_out_full, preferred_element_type=jnp.float32
        )
        third = norm_apply(after_cross, gains[2], biases[2]).astype(jnp.bfloat16)
        hidden = jnp.dot(third, feed_in_full, preferred_element_type=jnp.float32)
        active = gelu_exact(hidden).astype(jnp.bfloat16)
        result = (
            after_cross + jnp.dot(active, feed_out_full, preferred_element_type=jnp.float32)
        ).astype(jnp.bfloat16)
        grad_feed_out = jnp.einsum(
            "rf,rd->fd", active, grad_out, preferred_element_type=jnp.float32
        )
        grad_active = jnp.einsum(
            "rd,fd->rf", grad_out, feed_out_full, preferred_element_type=jnp.float32
        ).astype(jnp.bfloat16)
        _, gelu_pull = jax.vjp(gelu_exact, hidden)
        grad_hidden = gelu_pull(grad_active.astype(jnp.float32))[0].astype(jnp.bfloat16)
        grad_feed_in = jnp.einsum(
            "rd,rf->df", third, grad_hidden, preferred_element_type=jnp.float32
        )
        grad_third = jnp.einsum(
            "rf,df->rd", grad_hidden, feed_in_full, preferred_element_type=jnp.float32
        )
        _, norm_pull = jax.vjp(norm_apply, after_cross, gains[2], biases[2])
        norm_part, gain_two, bias_two = norm_pull(grad_third)
        grad_after_cross = grad_out.astype(jnp.float32) + norm_part
        cross_branch = grad_after_cross.astype(jnp.bfloat16)
        grad_cross_output = jnp.einsum(
            "rd,re->de", cross_mixed, cross_branch, preferred_element_type=jnp.float32
        )
        grad_cross_mixed = jnp.einsum(
            "re,de->rd", cross_branch, cross_out_full, preferred_element_type=jnp.float32
        ).astype(jnp.bfloat16)
        cross_delta = attend_delta(
            cross_queries, cross_pairs, cross_allowed, grad_cross_mixed, cross_total, cross_width
        )
        grad_cross_queries = attend_query_grad(
            cross_queries,
            cross_pairs,
            cross_allowed,
            grad_cross_mixed,
            cross_total,
            cross_delta,
            cross_width,
        )
        grad_source = lax.psum_scatter(
            key_terms(
                cross_queries,
                cross_pairs,
                cross_allowed,
                grad_cross_mixed,
                cross_total,
                cross_delta,
                cross_width,
                source_rows * lax.axis_size("ctx"),
            ).astype(jnp.bfloat16),
            "ctx",
            scatter_dimension=0,
            tiled=True,
        )
        grad_cross_source = jnp.einsum(
            "sd,se->de", source, grad_source, preferred_element_type=jnp.float32
        )
        grad_encoded = jnp.einsum(
            "se,de->sd", grad_source, cross_source_full, preferred_element_type=jnp.float32
        ).astype(jnp.bfloat16)
        grad_cross_query = jnp.einsum(
            "rd,re->de", second, grad_cross_queries, preferred_element_type=jnp.float32
        )
        grad_second = jnp.einsum(
            "re,de->rd", grad_cross_queries, cross_query_full, preferred_element_type=jnp.float32
        )
        _, norm_pull = jax.vjp(norm_apply, after_self, gains[1], biases[1])
        norm_part, gain_one, bias_one = norm_pull(grad_second)
        grad_after_self = grad_after_cross + norm_part
        self_branch = grad_after_self.astype(jnp.bfloat16)
        grad_self_output = jnp.einsum(
            "rd,re->de", self_mixed, self_branch, preferred_element_type=jnp.float32
        )
        grad_self_mixed = jnp.einsum(
            "re,de->rd", self_branch, self_out_full, preferred_element_type=jnp.float32
        ).astype(jnp.bfloat16)
        self_delta = attend_delta(
            query, self_pairs, self_allowed, grad_self_mixed, self_total, self_width
        )
        grad_query = attend_query_grad(
            query, self_pairs, self_allowed, grad_self_mixed, self_total, self_delta, self_width
        )
        grad_pairs = lax.psum_scatter(
            key_terms(
                query,
                self_pairs,
                self_allowed,
                grad_self_mixed,
                self_total,
                self_delta,
                self_width,
                rows * lax.axis_size("ctx"),
            ).astype(jnp.bfloat16),
            "ctx",
            scatter_dimension=0,
            tiled=True,
        )
        grad_projected = jnp.concatenate([grad_query, grad_pairs], axis=1)
        grad_self_project = jnp.einsum(
            "rd,re->de", first, grad_projected, preferred_element_type=jnp.float32
        )
        grad_first = jnp.einsum(
            "re,de->rd", grad_projected, self_in_full, preferred_element_type=jnp.float32
        )
        _, norm_pull = jax.vjp(norm_apply, values, gains[0], biases[0])
        norm_part, gain_zero, bias_zero = norm_pull(grad_first)
        grad_values = (grad_after_self + norm_part).astype(jnp.bfloat16)
        grads = (
            grad_self_project,
            grad_self_output,
            grad_cross_query,
            grad_cross_source,
            grad_cross_output,
            grad_feed_in,
            grad_feed_out,
            jnp.stack([gain_zero, gain_one, gain_two]),
            jnp.stack([bias_zero, bias_one, bias_two]),
        )
        result, grad_values, grad_encoded, grads = (result, grad_values, grad_encoded, grads)
        totals = (
            grads
            if index == 0
            else tuple((jnp.add(left, right) for left, right in zip(totals, grads)))
        )
        results.append(result)
        grad_values_all.append(grad_values)
        grad_encoded_all.append(grad_encoded)
    shares = (
        lax.psum_scatter(
            totals[0].astype(jnp.bfloat16), "fsdp", scatter_dimension=0, tiled=True
        ).astype(jnp.float32),
        lax.psum_scatter(
            totals[1].astype(jnp.bfloat16), "fsdp", scatter_dimension=0, tiled=True
        ).astype(jnp.float32),
        lax.psum_scatter(
            totals[2].astype(jnp.bfloat16), "fsdp", scatter_dimension=0, tiled=True
        ).astype(jnp.float32),
        lax.psum_scatter(
            totals[3].astype(jnp.bfloat16), "fsdp", scatter_dimension=0, tiled=True
        ).astype(jnp.float32),
        lax.psum_scatter(
            totals[4].astype(jnp.bfloat16), "fsdp", scatter_dimension=0, tiled=True
        ).astype(jnp.float32),
        lax.psum_scatter(
            totals[5].astype(jnp.bfloat16), "fsdp", scatter_dimension=0, tiled=True
        ).astype(jnp.float32),
        lax.psum_scatter(
            totals[6].astype(jnp.bfloat16), "fsdp", scatter_dimension=0, tiled=True
        ).astype(jnp.float32),
        lax.psum_scatter(
            totals[7].astype(jnp.bfloat16), "fsdp", scatter_dimension=1, tiled=True
        ).astype(jnp.float32),
        lax.psum_scatter(
            totals[8].astype(jnp.bfloat16), "fsdp", scatter_dimension=1, tiled=True
        ).astype(jnp.float32),
    )
    totals = tuple(
        jax.tree.map(lambda part: part.astype(jnp.float32), lax.psum(as_sent(tuple(shares)), "ctx"))
    )
    output = jnp.stack(results)[:, None]
    grad_tokens = jnp.stack(grad_values_all)[:, None]
    grad_source_rows = jnp.stack(grad_encoded_all)[:, None]
    return (
        output,
        grad_tokens,
        grad_source_rows,
        totals[0],
        totals[1],
        totals[2],
        totals[3],
        totals[4],
        totals[5],
        totals[6],
        totals[7],
        totals[8][:2],
        totals[8][2],
    )


BIG = 1e30
SCALE2 = HEAD ** (-0.5) * math.log2(math.e)
NT = (((1,), (1,)), ((), ()))
TN = (((0,), (0,)), ((), ()))
NN = (((1,), (0,)), ((), ()))


def dot(left, right, dims=NN):
    return lax.dot_general(left, right, dims, preferred_element_type=jnp.float32)


def lanes(rows):
    return lax.broadcasted_iota(jnp.int32, (rows, 128), 1)


def parts(x):
    hi = x.astype(jnp.bfloat16)
    rest = x - hi.astype(jnp.float32)
    mid = rest.astype(jnp.bfloat16)
    lo = (rest - mid.astype(jnp.float32)).astype(jnp.bfloat16)
    return (hi, mid, lo)


def spread(x, base):
    hi, mid, lo = parts(x)
    lane = lanes(x.shape[0]) % HEAD
    return jnp.where(lane == 4, hi, jnp.where(lane == 5, mid, jnp.where(lane == 6, lo, base)))


def two_heads(ref, own, other):
    left = lanes(own.shape[0]) < HEAD
    ref[0] = jnp.where(left, own, other)
    ref[1] = jnp.where(left, other, own)


def tail_masked(scores, rows):
    width = scores.shape[1] - rows
    row = lax.broadcasted_iota(jnp.int32, (rows, rows), 0)
    column = lax.broadcasted_iota(jnp.int32, (rows, rows), 1)
    tail = jnp.where(column > row, -BIG, scores[:, width:])
    return tail if width == 0 else jnp.concatenate([scores[:, :width], tail], axis=1)


def attend_kernel(plan, q_ref, k_ref, v_ref, qd_ref, kd_ref, out_ref, extra_ref, keys, values):
    two_heads(keys, k_ref[...], kd_ref[...])
    two_heads(values, v_ref[...], jnp.ones_like(v_ref))

    def scores_of(item):
        q0, q1, k0, k1, diagonal = item
        left = lanes(q1 - q0) < HEAD
        q, qd = (q_ref[q0:q1], qd_ref[q0:q1])
        pair = [dot(jnp.where(left == (h == 0), q, qd), keys[h, k0:k1], NT) for h in range(2)]
        return [tail_masked(s, q1 - q0) for s in pair] if diagonal else pair

    following = scores_of(plan[0])
    for index, (q0, q1, k0, k1, _) in enumerate(plan):
        scores = following
        following = scores_of(plan[index + 1]) if index + 1 < len(plan) else None
        left = lanes(q1 - q0) < HEAD
        mixed, tops = ([], [])
        for h in range(2):
            top = jnp.max(scores[h], axis=1, keepdims=True)
            probs = jnp.exp2((scores[h] - top) * SCALE2).astype(jnp.bfloat16)
            mixed.append(dot(probs, values[h, k0:k1]))
            tops.append(top)
        mass = jnp.where(left, mixed[1], mixed[0])
        numer = jnp.where(left, mixed[0], mixed[1])
        out_ref[q0:q1] = (numer / pltpu.roll(mass, HEAD, 1)).astype(jnp.bfloat16)
        top = jnp.where(left, tops[1], tops[0])
        extra_ref[q0:q1] = spread(-(top + HEAD**0.5 * jnp.log(mass)), qd_ref[q0:q1])


def attend_back_kernel(
    plan,
    q_ref,
    k_ref,
    v_ref,
    extra_ref,
    kd_ref,
    out_ref,
    g_ref,
    *refs,
):
    *outs, keys, values, queries, grads, g_t, q_t, dk_t, dv_t = refs
    if len(outs) == 1:
        dq_ref, dk_ref, dv_ref = (outs[0].at[i] for i in range(3))
    else:
        dq_ref, dk_ref, dv_ref = (outs[0], outs[1].at[0], outs[1].at[1])
    two_heads(keys, k_ref[...], kd_ref[...])
    two_heads(values, v_ref[...], jnp.ones_like(v_ref))
    two_heads(queries, q_ref[...], extra_ref[...])
    square = (128, 128)
    row, column = (lax.broadcasted_iota(jnp.int32, square, axis) < HEAD for axis in (0, 1))
    across = jnp.where(row != column, 1.0, 0.0).astype(jnp.bfloat16)
    g = g_ref[...]
    terms = parts(g.astype(jnp.float32) * out_ref[...].astype(jnp.float32))
    delta = sum(dot(term, across) for term in terms)
    two_heads(grads, g, spread(-delta, jnp.zeros_like(g)))
    g_t[...] = g.T
    q_t[...] = q_ref[...].T
    dk_t[...] = jnp.zeros_like(dk_t)
    dv_t[...] = jnp.zeros_like(dv_t)
    for q0, q1, k0, k1, diagonal in plan:
        left = lanes(q1 - q0) < HEAD
        pair = []
        for h in range(2):
            s = dot(queries[h, q0:q1], keys[h, k0:k1], NT)
            s = tail_masked(s, q1 - q0) if diagonal else s
            pair.append((s, dot(grads[h, q0:q1], values[h, k0:k1], NT)))
        dqs = []
        for h, (s, grad_probs) in enumerate(pair):
            probs = jnp.exp2(s * SCALE2)
            ds = (probs * grad_probs).astype(jnp.bfloat16)
            head = slice(h * HEAD, h * HEAD + HEAD)
            dv_t[head, k0:k1] += dot(g_t[head, q0:q1], probs.astype(jnp.bfloat16))
            dk_t[head, k0:k1] += dot(q_t[head, q0:q1], ds)
            dqs.append(dot(ds, k_ref[k0:k1]))
        dq_ref[q0:q1] = (jnp.where(left, dqs[0], dqs[1]) * HEAD ** (-0.5)).astype(jnp.bfloat16)
    dk_ref[...] = (dk_t[...].T * HEAD ** (-0.5)).astype(jnp.bfloat16)
    dv_ref[...] = dv_t[...].T.astype(jnp.bfloat16)


def pair_of_heads(rows):
    return pl.BlockSpec((rows, 128), lambda i: (0, i))


def all_of(rows):
    return pl.BlockSpec((rows, 128), lambda i: (0, 0))


def small_cost():
    return pl.CostEstimate(flops=1 << 10, bytes_accessed=1 << 10, transcendentals=0)


def attend(plan, q, k, v, qd, kd):
    nq, nk, model = (q.shape[0], k.shape[0], q.shape[1])
    shape = jax.ShapeDtypeStruct((nq, model), jnp.bfloat16)
    return pl.pallas_call(
        functools.partial(attend_kernel, plan),
        grid=(model // 128,),
        in_specs=[pair_of_heads(n) for n in (nq, nk, nk)] + [all_of(nq), all_of(nk)],
        out_specs=[pair_of_heads(nq)] * 2,
        out_shape=[shape] * 2,
        scratch_shapes=[pltpu.VMEM((2, nk, 128), jnp.bfloat16)] * 2,
        compiler_params=pltpu.CompilerParams(vmem_limit_bytes=58 * 2**20),
        cost_estimate=small_cost(),
    )(q, k, v, qd, kd)


def stacked(count, rows):
    return pl.BlockSpec((count, rows, 128), lambda i: (0, 0, i))


def attend_back(plan, q, k, v, extra, kd, out, g, together):
    nq, nk, model = (q.shape[0], k.shape[0], q.shape[1])
    if together:
        specs, shapes = ([stacked(3, nq)], [(3, nq, model)])
    else:
        specs, shapes = ([pair_of_heads(nq), stacked(2, nk)], [(nq, model), (2, nk, model)])
    outs = pl.pallas_call(
        functools.partial(attend_back_kernel, plan),
        grid=(model // 128,),
        in_specs=[pair_of_heads(n) for n in (nq, nk, nk, nq)]
        + [all_of(nk)]
        + [pair_of_heads(nq)] * 2,
        out_specs=specs,
        out_shape=[jax.ShapeDtypeStruct(shape, jnp.bfloat16) for shape in shapes],
        scratch_shapes=[pltpu.VMEM((2, nk, 128), jnp.bfloat16)] * 2
        + [pltpu.VMEM((2, nq, 128), jnp.bfloat16)] * 2
        + [pltpu.VMEM((128, nq), jnp.bfloat16)] * 2
        + [pltpu.VMEM((128, nk), jnp.float32)] * 2,
        compiler_params=pltpu.CompilerParams(vmem_limit_bytes=58 * 2**20),
        cost_estimate=small_cost(),
    )(q, k, v, extra, kd, out, g)
    return outs[0] if together else outs


def self_plan(first, total, tile):
    return [
        (start, start + tile, low, start + tile, True)
        for low, high in ((0, first), (first, total))
        for start in range(low, high, tile)
    ]


def cross_plan(first, total, reach, source, tile):
    return [
        (start, start + tile, 0, reach if start < first else source, False)
        for start in range(0, total, tile)
    ]


def query_marks(docs):
    lane = jnp.arange(128) % HEAD
    return jnp.where(docs[:, None] == lane[None, :], BIG, 0.0).astype(jnp.bfloat16)


def key_marks(docs, count):
    lane = (jnp.arange(128) % HEAD)[None, :]
    other = jnp.where(docs[:, None] == lane, 0.0, -1.0)
    return jnp.where(lane < count, other, jnp.where(lane < 7, 1.0, 0.0)).astype(jnp.bfloat16)


MODEL = 1024
TILE = 512


def wide(values):
    return values.astype(jnp.float32)


def short(values):
    return values.astype(jnp.bfloat16)


def gathered(ref):
    return ref[...].reshape(-1, ref.shape[-1])


def once(shape, index):
    return pl.BlockSpec(shape, index, pipeline_mode=pl.Buffered(1))


def weight_at(slot):
    return once((16, 64, MODEL), lambda *_: (0, slot, 0))


def norm_rows():
    return once((8, MODEL), lambda *_: (0, 0))


def by_rows(count, width=MODEL):
    return pl.BlockSpec((count, width), lambda i, *_: (i, 0))


def found_rows(count):
    return pl.BlockSpec((count, MODEL), lambda i, held, *_: (held[i], 0))


def kept_or_sent(rows):
    return [once((rows, MODEL), lambda *_: (0, 0)) for _ in range(2)]


def store_found(held, width, own_ref, away_ref, value):
    spot = held[pl.program_id(0)]
    rows = pl.ds(pl.multiple_of(lax.rem(spot, 2) * width, width), width)

    @pl.when(spot < 2)
    def _():
        own_ref[rows] = value

    @pl.when(spot >= 2)
    def _():
        away_ref[rows] = value


def sums_out():
    return pl.BlockSpec((8, MODEL), lambda *_: (0, 0))


def struct(shape, kind):
    return jax.ShapeDtypeStruct(shape, kind)


def spread_of(values):
    mean = jnp.mean(values, axis=-1, keepdims=True)
    centred = values - mean
    scale = lax.rsqrt(jnp.mean(centred * centred, axis=-1, keepdims=True) + 1e-05)
    return (centred * scale, scale)


def norm_of(values, norm_ref, k):
    hat, _ = spread_of(values)
    return short(hat * norm_ref[k : k + 1] + norm_ref[3 + k : 4 + k])


def norm_back(values, grad, norm_ref, k, sums_ref):
    hat, scale = spread_of(values)
    each = grad * norm_ref[k : k + 1]
    inner = each - jnp.mean(each, axis=-1, keepdims=True)
    inner = inner - hat * jnp.mean(each * hat, axis=-1, keepdims=True)
    sums_ref[0:1] += jnp.sum(grad * hat, axis=0, keepdims=True)
    sums_ref[1:2] += jnp.sum(grad, axis=0, keepdims=True)
    return scale * inner


def call(kernel, grid, in_specs, out_specs, out_shape, scratch=(), prefetch=0):
    return pl.pallas_call(
        kernel,
        grid_spec=pltpu.PrefetchScalarGridSpec(
            num_scalar_prefetch=prefetch,
            grid=grid,
            in_specs=in_specs,
            out_specs=out_specs,
            scratch_shapes=list(scratch),
        ),
        out_shape=out_shape,
        compiler_params=pltpu.CompilerParams(vmem_limit_bytes=58 * 2**20),
        cost_estimate=small_cost(),
    )


def pack_kernel(*refs):
    attention_ref, feed_ref = refs[-2:]
    self_in, self_out, cross_q, cross_s, cross_out, feed_in, feed_out, norms = refs[:-2]
    rows = self_in.shape[0]
    slot = 0
    for ref in (self_in, self_out, cross_q, cross_s, cross_out):
        for start in range(0, ref.shape[1], MODEL):
            attention_ref[slot * rows : (slot + 1) * rows] = ref[:, start : start + MODEL]
            slot += 1
    attention_ref[slot * rows :] = norms[...]
    piece = feed_out.shape[0] // 2
    for lot in range(2):
        for owner in range(16):
            column = (2 * owner + lot) * piece
            slot, spot = (2 * lot + owner // 8, owner % 8 * piece)
            feed_ref[slot * rows : (slot + 1) * rows, spot : spot + piece] = feed_in[
                :, column : column + piece
            ]
    feed_ref[4 * rows : 8 * rows] = feed_out[...]
    feed_ref[8 * rows :] = jnp.zeros_like(norms)


def pack(weights, norms):
    arrays = tuple(weights) + (norms,)
    out = struct((528, MODEL), jnp.bfloat16)
    return call(
        pack_kernel,
        (1,),
        [once(a.shape, lambda i: (0, 0)) for a in arrays],
        [once(out.shape, lambda i: (0, 0))] * 2,
        [out] * 2,
    )(*arrays)


def enter_kernel(held, tokens_ref, norm_ref, wq, wk, wv, first_ref, q_ref, k_ref, v_ref):
    first = norm_of(wide(tokens_ref[...]), norm_ref, 0)
    first_ref[...] = first
    for weight, out in ((wq, q_ref), (wk, k_ref), (wv, v_ref)):
        out[...] = short(dot(first, gathered(weight)))


def enter(held, tokens, norms, weights, width):
    shape = struct(tokens.shape, jnp.bfloat16)
    return call(
        enter_kernel,
        (tokens.shape[0] // width,),
        [found_rows(width), norm_rows()] + [weight_at(i) for i in range(3)],
        [by_rows(width)] * 4,
        [shape] * 4,
        prefetch=1,
    )(held, tokens, norms, weights, weights, weights)


def source_kernel(source_ref, wk, wv, k_ref, v_ref):
    source = source_ref[...]
    k_ref[...] = short(dot(source, gathered(wk)))
    v_ref[...] = short(dot(source, gathered(wv)))


def source_pairs(source, weights, width):
    return call(
        source_kernel,
        (source.shape[0] // width,),
        [by_rows(width), weight_at(5), weight_at(6)],
        [by_rows(width)] * 2,
        [struct(source.shape, jnp.bfloat16)] * 2,
    )(source, weights, weights)


def between_kernel(held, mixed_ref, tokens_ref, norm_ref, wo, wq, after_ref, second_ref, q_ref):
    after = wide(tokens_ref[...]) + dot(mixed_ref[...], gathered(wo))
    after_ref[...] = after
    second = norm_of(after, norm_ref, 1)
    second_ref[...] = second
    q_ref[...] = short(dot(second, gathered(wq)))


def between(held, mixed, tokens, norms, weights, width):
    return call(
        between_kernel,
        (mixed.shape[0] // width,),
        [by_rows(width), found_rows(width), norm_rows(), weight_at(3), weight_at(4)],
        [by_rows(width)] * 3,
        [struct(mixed.shape, kind) for kind in (jnp.float32, jnp.bfloat16, jnp.bfloat16)],
        prefetch=1,
    )(held, mixed, tokens, norms, weights, weights)


def before_feed_kernel(
    held, mixed_ref, base_ref, own_ref, other_ref, norm_ref, wo, after_ref, third_ref, grad_ref
):
    after = base_ref[...] + dot(mixed_ref[...], gathered(wo))
    after_ref[...] = after
    third_ref[...] = norm_of(after, norm_ref, 2)
    own = held[pl.program_id(0)] < 2

    @pl.when(own)
    def _():
        grad_ref[...] = own_ref[...]

    @pl.when(jnp.logical_not(own))
    def _():
        grad_ref[...] = other_ref[...]


def before_feed(held, mixed, base, own, other, norms, weights, width):
    return call(
        before_feed_kernel,
        (mixed.shape[0] // width,),
        [
            by_rows(width),
            by_rows(width),
            pl.BlockSpec((width, MODEL), lambda i, held: (jnp.minimum(held[i], 1), 0)),
            pl.BlockSpec((width, MODEL), lambda i, held: (jnp.maximum(held[i] - 2, 0), 0)),
            norm_rows(),
            weight_at(7),
        ],
        [by_rows(width)] * 3,
        [struct(mixed.shape, kind) for kind in (jnp.float32, jnp.bfloat16, jnp.bfloat16)],
        prefetch=1,
    )(held, mixed, base, own, other, norms, weights)


def gelu_terms(hidden):
    bell = jnp.exp2(hidden * hidden * (-0.5 * math.log2(math.e)))
    t = 1.0 / (1.0 + (0.3275911 / math.sqrt(2.0)) * jnp.abs(hidden))
    series = 1.061405429
    for term in (-1.453152027, 1.421413741, -0.284496736, 0.254829592):
        series = series * t + term
    tail = 0.5 * series * t * bell
    return (jnp.where(hidden < 0, tail, 1.0 - tail), bell * (1.0 / math.sqrt(2.0 * math.pi)))


def deal(place_ref, turned, keep_ref, send_ref, pieces, own_y=True):
    for own in range(2):

        @pl.when(place_ref[0] == own)
        def _(own=own):
            for core, x, y, index, value in pieces:
                rel_x = jnp.bitwise_xor(place_ref[1], x)
                rel_y = jnp.bitwise_xor(place_ref[2], y) if own_y else y
                spot = (rel_y, rel_x) if turned else (rel_x, rel_y)
                ref = keep_ref if core == own else send_ref
                ref[spot + index] = value


def shard_pieces(product, slot, *rest):
    pieces = []
    for owner in range(product.shape[0] // 64):
        for y in range(2):
            start = owner * 64 + y * 32
            index = (owner // 4, slot) + rest
            value = short(product[start : start + 32])
            pieces.append((owner % 2, owner // 2 % 2, y, index, value))
    return pieces


def feed_kernel(
    place_ref,
    third_ref,
    grad_ref,
    win_ref,
    wout_ref,
    out_ref,
    back_ref,
    keep_a,
    send_a,
    keep_b,
    send_b,
    third_t,
    active_ref,
    hidden_ref,
):
    step = pl.program_id(0)

    @pl.when(step == 0)
    def _():
        third_t[...] = third_ref[...].T
        out_ref[...] = jnp.zeros_like(out_ref)
        back_ref[...] = jnp.zeros_like(back_ref)

    win, wout = (gathered(win_ref), gathered(wout_ref))
    rows = third_ref.shape[0]
    lots = [slice(start, start + TILE) for start in range(0, rows, TILE)]

    def enter(lot):
        return (dot(third_ref[lot], win), dot(grad_ref[lot], wout, NT))

    def leave(lot, hidden, grad):
        mass, bell = gelu_terms(hidden)
        active = short(hidden * mass)
        grad = short((mass + hidden * bell) * wide(short(grad)))
        active_ref[lot] = active
        hidden_ref[lot] = grad
        out_ref[lot] += dot(active, wout)
        back_ref[lot] += dot(grad, win, NT)

    ready = enter(lots[0])
    for index, lot in enumerate(lots):
        following = enter(lots[index + 1]) if index + 1 < len(lots) else None
        leave(lot, *ready)
        ready = following
    grad_out = short(dot(active_ref[...], grad_ref[...], TN))
    grad_in = short(dot(third_t[...], hidden_ref[...]))
    turn = lax.rem(step, 4)
    side = pl.ds(pl.multiple_of(lax.rem(turn, 2) * TILE, TILE), TILE)
    pieces = shard_pieces(grad_in, turn // 2, slice(None), side)
    for owner in range(4):
        for y in range(2):
            for half in range(2):
                start = owner * 128 + y * 64 + 32 * half
                value = grad_out[start : start + 32]
                pieces.append((owner % 2, owner // 2, y, (turn, 2 + half), value))

    @pl.when(step < 4)
    def _():
        deal(place_ref, False, keep_a, send_a, pieces)

    @pl.when(step >= 4)
    def _():
        deal(place_ref, True, keep_b, send_b, pieces)


def feed(place, third, grad, weights):
    rows = third.shape[0]
    full = struct((rows, MODEL), jnp.float32)
    buffer = struct((2, 2, 4, 4, 32, MODEL), jnp.bfloat16)
    out, back, *lots = call(
        feed_kernel,
        (8,),
        [
            once((rows, MODEL), lambda t, place: (0, 0)),
            once((rows, MODEL), lambda t, place: (0, 0)),
            pl.BlockSpec((16, 64, TILE), lambda t, place: (0, t // 2, t % 2)),
            pl.BlockSpec((4, 128, MODEL), lambda t, place: (t % 4, 2 + t // 4, 0)),
        ],
        [once((rows, MODEL), lambda t, place: (0, 0))] * 2
        + [once(buffer.shape, lambda t, place: (0, 0, 0, 0, 0, 0))] * 4,
        [full, full] + [buffer] * 4,
        scratch=[
            pltpu.VMEM((MODEL, rows), jnp.bfloat16),
            pltpu.VMEM((rows, TILE), jnp.bfloat16),
            pltpu.VMEM((rows, TILE), jnp.bfloat16),
        ],
        prefetch=1,
    )(place, third, grad, weights, weights)
    return out, back, lots[:2], lots[2:]


def clear(*refs):
    @pl.when(pl.program_id(0) == 0)
    def _():
        for ref in refs:
            ref[...] = jnp.zeros_like(ref)


def add_product(total_ref, left, right):
    total_ref[...] += dot(left, right, TN)


def at_end(store):
    pl.when(pl.program_id(0) == pl.num_programs(0) - 1)(store)


def buffer_of(slots):
    return struct((2, 2, 4, slots, 32, MODEL), jnp.bfloat16)


def slots_at(slots):
    return once((2, 2, 4, slots, 32, MODEL), lambda *_: (0,) * 6)


def after_feed_kernel(
    held,
    place,
    after_ref,
    out_ref,
    back_ref,
    grad_ref,
    cross_ref,
    norm_ref,
    wo,
    own_ref,
    away_ref,
    total_ref,
    mixed_ref,
    sums_ref,
    keep_ref,
    send_ref,
    weight_ref,
):
    clear(sums_ref, weight_ref)
    after = after_ref[...]
    result = short(after + out_ref[...])
    store_found(held, after.shape[0], own_ref, away_ref, result)
    part = norm_back(after, back_ref[...], norm_ref, 2, sums_ref)
    total = wide(grad_ref[...]) + part
    total_ref[...] = total
    branch = short(total)
    mixed_ref[...] = short(dot(branch, gathered(wo), NT))
    add_product(weight_ref, cross_ref[...], branch)
    at_end(lambda: deal(place, False, keep_ref, send_ref, shard_pieces(weight_ref, 0)))


def after_feed(held, place, after, out, back, grad, mixed, norms, weights, width):
    narrow = struct(after.shape, jnp.bfloat16)
    full = struct(after.shape, jnp.float32)
    return call(
        after_feed_kernel,
        (after.shape[0] // width,),
        [by_rows(width)] * 5 + [norm_rows(), weight_at(7)],
        kept_or_sent(2 * width) + [by_rows(width)] * 2 + [sums_out()] + [slots_at(1)] * 2,
        [struct((2 * width, MODEL), jnp.bfloat16)] * 2
        + [full, narrow, struct((8, MODEL), jnp.float32)]
        + [buffer_of(1)] * 2,
        scratch=[pltpu.VMEM((MODEL, MODEL), jnp.float32)],
        prefetch=2,
    )(held, place, after, out, back, grad, mixed, norms, weights)


def middle_kernel(
    place,
    grad_ref,
    second_ref,
    after_ref,
    base_ref,
    self_ref,
    norm_ref,
    wq,
    wo,
    *refs,
):
    total_ref, mixed_ref, sums_ref, keep_ref, send_ref, weight_q, weight_o = refs
    clear(sums_ref, weight_q, weight_o)
    grad_q = grad_ref[...]
    grad = dot(grad_q, gathered(wq), NT)
    add_product(weight_q, second_ref[...], grad_q)
    total = base_ref[...] + norm_back(after_ref[...], grad, norm_ref, 1, sums_ref)
    total_ref[...] = total
    branch = short(total)
    mixed_ref[...] = short(dot(branch, gathered(wo), NT))
    add_product(weight_o, self_ref[...], branch)

    @at_end
    def _():
        deal(place, False, keep_ref, send_ref, shard_pieces(weight_q, 0))
        deal(place, False, keep_ref, send_ref, shard_pieces(weight_o, 1))


def middle(place, grad, second, after, base, mixed, norms, weights, width):
    narrow = struct(after.shape, jnp.bfloat16)
    return call(
        middle_kernel,
        (after.shape[0] // width,),
        [by_rows(width)] * 5 + [norm_rows(), weight_at(4), weight_at(3)],
        [by_rows(width)] * 2 + [sums_out()] + [slots_at(2)] * 2,
        [struct(after.shape, jnp.float32), narrow, struct((8, MODEL), jnp.float32)]
        + [buffer_of(2)] * 2,
        scratch=[pltpu.VMEM((MODEL, MODEL), jnp.float32)] * 2,
        prefetch=1,
    )(place, grad, second, after, base, mixed, norms, weights, weights)


def project_grad_kernel(place, left_ref, right_ref, keep_ref, send_ref, left_t):
    @pl.when(pl.program_id(1) == 0)
    def _():
        left_t[...] = left_ref[...].T

    product = dot(left_t[...], right_ref[0])
    deal(place, False, keep_ref, send_ref, shard_pieces(product, 0), own_y=False)


def project_grad(place, left, right):
    rows = left.shape[0]
    block = (2, 2, TILE // 256, 1, 32, MODEL)
    return call(
        project_grad_kernel,
        (MODEL // TILE, 3),
        [
            pl.BlockSpec((rows, TILE), lambda t, n, place: (0, t)),
            pl.BlockSpec((1, rows, MODEL), lambda t, n, place: (n, 0, 0)),
        ],
        [pl.BlockSpec(block, lambda t, n, place: (0, 0, t, n, 0, 0))] * 2,
        [buffer_of(3)] * 2,
        scratch=[pltpu.VMEM((TILE, rows), jnp.bfloat16)],
        prefetch=1,
    )(place, left, right)


def finish_kernel(
    held, grads_ref, tokens_ref, base_ref, norm_ref, wq, wk, wv, own_ref, away_ref, sums_ref
):
    clear(sums_ref)
    grad = sum(dot(grads_ref[i], gathered(w), NT) for i, w in enumerate((wq, wk, wv)))
    part = norm_back(wide(tokens_ref[...]), grad, norm_ref, 0, sums_ref)
    result = short(base_ref[...] + part)
    store_found(held, result.shape[0], own_ref, away_ref, result)


def finish(held, grads, tokens, base, norms, weights, width):
    return call(
        finish_kernel,
        (base.shape[0] // width,),
        [
            pl.BlockSpec((3, width, MODEL), lambda i, *_: (0, i, 0)),
            found_rows(width),
            by_rows(width),
            norm_rows(),
        ]
        + [weight_at(i) for i in range(3)],
        kept_or_sent(2 * width) + [sums_out()],
        [struct((2 * width, MODEL), jnp.bfloat16)] * 2 + [struct((8, MODEL), jnp.float32)],
        prefetch=1,
    )(held, grads, tokens, base, norms, weights, weights, weights)


def source_back_kernel(
    place, grads_ref, source_ref, wk, wv, own_ref, away_ref, keep_ref, send_ref, weight_ref
):
    clear(weight_ref)
    source = source_ref[...].T
    for i in range(2):
        weight_ref[i] += dot(source, grads_ref[i])
    grad = dot(grads_ref[0], gathered(wk), NT) + dot(grads_ref[1], gathered(wv), NT)
    grad = short(grad)

    @pl.when(pl.program_id(0) == place[2])
    def _():
        own_ref[...] = grad

    @pl.when(pl.program_id(0) != place[2])
    def _():
        away_ref[...] = grad

    @at_end
    def _():
        for i in range(2):
            deal(place, False, keep_ref, send_ref, shard_pieces(weight_ref.at[i], i))


def source_back(place, grads, source, weights, width):
    rows = grads.shape[1]
    return call(
        source_back_kernel,
        (rows // width,),
        [
            pl.BlockSpec((2, width, MODEL), lambda i, *_: (0, i, 0)),
            by_rows(width),
            weight_at(5),
            weight_at(6),
        ],
        kept_or_sent(width) + [slots_at(2)] * 2,
        [struct((width, MODEL), jnp.bfloat16)] * 2 + [buffer_of(2)] * 2,
        scratch=[pltpu.VMEM((2, MODEL, MODEL), jnp.float32)],
        prefetch=1,
    )(place, grads, source, weights, weights)


def pairs(bit):
    return [(i, i ^ bit) for i in range(16)]


def swap(values):
    return lax.ppermute(values, "ctx", [(0, 1), (1, 0)])


def over_x(values):
    return lax.ppermute(values, "fsdp", pairs(2))


def over_core(values):
    return lax.ppermute(values, "fsdp", pairs(1))


def tie(*values):
    return lax.optimization_barrier(values)


def lot_specs(lot, first, second, spread, z_of, depth=1):
    specs = []
    for keep, _ in lot:
        slots, rows = keep.shape[3:5]
        block = (1, spread, depth, slots, rows, MODEL)
        specs += [
            pl.BlockSpec(block, lambda i, place: (first, second, z_of(i, place), 0, 0, 0))
        ] * 2
    return specs


def slots_of(lot):
    return sum(keep.shape[3] for keep, _ in lot)


def in_order(i, place):
    return i


def from_own(i, place):
    return lax.rem(place[3] + i, 4)


def pair_sums(refs, count):
    return [wide(refs[2 * i][...]) + wide(refs[2 * i + 1][...]) for i in range(count)]


def depth_of(lots):
    return 4 if sum(slots_of(lot) for lot in lots) < 4 else 1


def ranges(sizes):
    starts = [sum(sizes[:i]) for i in range(len(sizes))]
    return [(start, start + size) for start, size in zip(starts, sizes)]


def overlaps(sources, pieces):
    for i, (s0, s1) in enumerate(ranges(sources)):
        for j, (p0, p1) in enumerate(ranges(pieces)):
            low, high = (max(s0, p0), min(s1, p1))
            if low < high:
                yield i, j, slice(low - s0, high - s0), slice(low - p0, high - p0)


def sizes_of(lot):
    return [keep.shape[3] for keep, _ in lot]


def first_sums(place, lots, cuts=None):
    cuts = cuts or [[slots_of(lot)] for lot in lots]

    def kernel(place_ref, *refs):
        refs = list(refs)
        outs = refs[-sum(len(cut) for cut in cuts) :]
        for lot, cut in zip(lots, cuts):
            values = pair_sums([refs.pop(0) for _ in range(2 * len(lot))], len(lot))
            pieces, outs = (outs[: len(cut)], outs[len(cut) :])
            for i, j, taken, put in overlaps(sizes_of(lot), cut):
                pieces[j][:, :, put] = short(values[i][0, :, :, taken])

    depth = depth_of(lots)
    shapes = [(2, 4, size, 32, MODEL) for cut in cuts for size in cut]
    outs = call(
        kernel,
        (4 // depth,),
        [spec for lot in lots for spec in lot_specs(lot, 1, 0, 2, in_order, depth)],
        [
            pl.BlockSpec((2, depth) + shape[2:], lambda i, place: (0, i, 0, 0, 0))
            for shape in shapes
        ],
        [struct(shape, jnp.bfloat16) for shape in shapes],
        prefetch=1,
    )(place, *[array for lot in lots for pair in lot for array in pair])
    return [outs[start:end] for start, end in ranges([len(cut) for cut in cuts])]


def second_sums(place, lots, firsts, cuts=None):
    cuts = cuts or [[slots_of(lot)] for lot in lots]

    def kernel(place_ref, *refs):
        refs = list(refs)
        outs = refs[-sum(len(cut) for cut in cuts) :]
        for lot, first, cut in zip(lots, firsts, cuts):
            values = pair_sums([refs.pop(0) for _ in range(2 * len(lot))], len(lot))
            received = [wide(refs.pop(0)[0]) for _ in first]
            received = received[0] if len(first) == 1 else jnp.concatenate(received, axis=1)
            pieces, outs = (outs[: len(cut)], outs[len(cut) :])
            spots = ranges(sizes_of(lot))
            for i, j, taken, put in overlaps(sizes_of(lot), cut):
                there = received[:, spots[i][0] + taken.start : spots[i][0] + taken.stop]
                pieces[j][:, put] = short(values[i][0, 0, :, taken] + there)

    depth = depth_of(lots)
    specs, arrays = ([], [])
    for lot, first in zip(lots, firsts):
        specs += lot_specs(lot, 0, 1, 1, in_order, depth)
        specs += [
            pl.BlockSpec((1, depth) + piece.shape[2:], lambda i, place: (1, i, 0, 0, 0))
            for piece in first
        ]
        arrays += [array for pair in lot for array in pair] + list(first)
    shapes = [(4, size, 32, MODEL) for cut in cuts for size in cut]
    outs = call(
        kernel,
        (4 // depth,),
        specs,
        [pl.BlockSpec((depth,) + shape[1:], lambda i, place: (i, 0, 0, 0)) for shape in shapes],
        [struct(shape, jnp.bfloat16) for shape in shapes],
        prefetch=1,
    )(place, *arrays)
    return [outs[start:end] for start, end in ranges([len(cut) for cut in cuts])]


def third_sums(place, lots, firsts, seconds):
    def kernel(place_ref, *refs):
        refs = list(refs)
        out = refs[-1]
        start = 0
        for lot, first, second in zip(lots, firsts, seconds):
            values = pair_sums([refs.pop(0) for _ in range(2 * len(lot))], len(lot))
            parts_of = (
                [wide(refs.pop(0)[0, 0]) for _ in first],
                [wide(refs.pop(0)[0]) for _ in second],
            )
            received = sum(p[0] if len(p) == 1 else jnp.concatenate(p, axis=0) for p in parts_of)
            for value, (s0, s1) in zip(values, ranges(sizes_of(lot))):
                out[0, start + s0 : start + s1] = short(value[0, 0, 0] + received[s0:s1])
            start += slots_of(lot)

    specs, arrays = ([], [])
    for lot, first, second in zip(lots, firsts, seconds):
        specs += lot_specs(lot, 0, 0, 1, in_order)
        specs += [
            pl.BlockSpec((1, 1) + piece.shape[2:], lambda i, place: (0, i, 0, 0, 0))
            for piece in first
        ]
        specs += [
            pl.BlockSpec((1,) + piece.shape[1:], lambda i, place: (i, 0, 0, 0))
            for piece in second
        ]
        arrays += [array for pair in lot for array in pair] + list(first) + list(second)
    shape = (4, sum(slots_of(lot) for lot in lots), 32, MODEL)
    return call(
        kernel,
        (4,),
        specs,
        [pl.BlockSpec((1,) + shape[1:], lambda i, place: (i, 0, 0, 0))],
        [struct(shape, jnp.bfloat16)],
        prefetch=1,
    )(place, *arrays)[0]


def direct_sums(place, lot, first):
    (keep, core) = lot
    slots = keep.shape[3]

    def kernel(place_ref, keep_ref, core_ref, *refs):
        received = [wide(ref[...]) for ref in refs[:-1]]
        received = received[0] if len(first) == 1 else jnp.concatenate(received, axis=2)
        total = wide(keep_ref[0]) + wide(core_ref[0]) + received
        refs[-1][0] = short(total[:, 0])

    block = (1, 2, 1, slots, 32, MODEL)
    shape = (4, 2, slots, 32, MODEL)
    return call(
        kernel,
        (4,),
        [pl.BlockSpec(block, lambda i, place: (0, 0, i, 0, 0, 0))] * 2
        + [
            pl.BlockSpec((2, 1) + piece.shape[2:], lambda i, place: (0, i, 0, 0, 0))
            for piece in first
        ],
        [pl.BlockSpec((1,) + shape[1:], lambda i, place: (i, 0, 0, 0, 0))],
        [struct(shape, jnp.bfloat16)],
        prefetch=1,
    )(place, keep, core, *first)[0]


def over_z(values):
    groups = [[first + 4 * z for z in range(4)] for first in range(4)]
    return lax.psum_scatter(values, "fsdp", scatter_dimension=0, axis_index_groups=groups)


def both_parts(total, other):
    low = lax.axis_index("ctx") == 0
    return wide(jnp.stack([jnp.where(low, total, other), jnp.where(low, other, total)], axis=1))


def columns(shares, start, stop):
    part = shares[start:stop].reshape(stop - start, -1, MODEL)
    return jnp.concatenate(list(part), axis=1)


def feed_shares(lots):
    inner = [lot[:2].reshape(2, 64, 8, 128).transpose(1, 0, 2, 3).reshape(64, 16, 128) for lot in lots]
    inner = jnp.stack(inner, axis=2).reshape(64, 4 * MODEL)
    outer = [lot[2:].transpose(1, 0, 2, 3).reshape(128, MODEL) for lot in lots]
    return inner, jnp.concatenate(outer)


def whole_packs(mesh):
    return mesh.shape["ctx"] == 2 and mesh.shape["fsdp"] == 16


def whole_pack_body(
    tokens,
    encoded,
    cotangent,
    order,
    target_lengths,
    source_lengths,
    self_project,
    self_output,
    cross_query,
    cross_source,
    cross_output,
    feed_in,
    feed_out,
    norm_gain,
    norm_bias,
):
    rows = tokens.shape[2]
    pack_rows, source_rows = (2 * rows, 2 * encoded.shape[2])
    first_rows = 3 * pack_rows // 4
    width = rows // 2
    mine = lax.axis_index("ctx")
    spot = lax.axis_index("fsdp")
    z = spot // 4
    place = jnp.stack([spot % 2, spot // 2 % 2, mine, z]).astype(jnp.int32)
    part = self_project.shape[0]

    norms = jnp.pad(jnp.concatenate([norm_gain, norm_bias]), ((0, 10), (0, MODEL - part)))
    attention_shard, feed_shard = pack(
        (self_project, self_output, cross_query, cross_source, cross_output, feed_in, feed_out),
        norms,
    )
    weights = lax.all_gather(attention_shard, "fsdp", axis=0)
    norms = wide(weights[:, 8 * part : 8 * part + 8, :part])
    norms = norms.transpose(1, 0, 2).reshape(8, MODEL)

    def both_halves(array):
        own = lax.dynamic_index_in_dim(array, mine, 0, False)[0]
        return own, swap(lax.dynamic_index_in_dim(array, 1 - mine, 0, False)[0])

    places = lax.dynamic_index_in_dim(order, mine, 0, False)[0]
    holds = places[::width] // width
    found = jnp.argsort(holds).astype(jnp.int32)
    held = jnp.where(found // 2 == mine, found % 2, 2 + found % 2)

    def from_both(own, other):
        low = mine == 0
        return jnp.stack([jnp.where(low, own, other), jnp.where(low, other, own)])[:, None]

    halves = jnp.concatenate(both_halves(tokens))
    own, other = both_halves(encoded)
    source = jnp.concatenate([jnp.where(mine == 0, own, other), jnp.where(mine == 0, other, own)])
    lengths = lax.dynamic_index_in_dim(target_lengths, mine, 0, False)[0]
    target_docs = docs_of(jnp.arange(pack_rows, dtype=jnp.int32), lengths)
    lengths = lax.dynamic_index_in_dim(source_lengths, mine, 0, False)[0]
    source_docs = docs_of(jnp.arange(source_rows, dtype=jnp.int32), lengths)
    docs = lengths.shape[0]
    marks = query_marks(target_docs)
    target_marks = key_marks(target_docs, docs)
    source_marks = key_marks(source_docs, docs)
    cotangent_own, cotangent_away = (
        lax.dynamic_index_in_dim(cotangent, which, 0, False)[0] for which in (mine, 1 - mine)
    )
    tied = (feed_shard, halves, source, marks, target_marks, source_marks)
    feed_shard, halves, source, marks, target_marks, source_marks, *cotangents = tie(
        *tied, cotangent_own, cotangent_away
    )
    feed_weights = lax.all_gather(feed_shard, "fsdp", axis=0)

    reach = source_rows // 2

    first, query, keys, values = enter(held, halves, norms, weights, width)
    query, cotangents[1] = tie(query, cotangents[1])
    cotangents[1] = swap(cotangents[1])
    plan = self_plan(first_rows, pack_rows, width)
    self_mixed, self_extra = attend(plan, query, keys, values, marks, target_marks)
    self_mixed, source = tie(self_mixed, source)
    cross_keys, cross_values = source_pairs(source, weights, source_rows // 2)
    after_self, second, cross_queries = between(held, self_mixed, halves, norms, weights, width)
    plan = cross_plan(first_rows, pack_rows, reach, source_rows, width)
    cross_mixed, cross_extra = attend(
        plan, cross_queries, cross_keys, cross_values, marks, source_marks
    )
    after_cross, third, grad_out = before_feed(
        held, cross_mixed, after_self, *cotangents, norms, weights, width
    )

    out, back, lot_a, lot_b = feed(place, third, grad_out, feed_weights)
    lot_a, lot_b = ([(lot[0], over_core(lot[1]))] for lot in (lot_a, lot_b))
    result, result_away, grad_after_cross, grad_cross_mixed, sums_two, *part_out = after_feed(
        held, place, after_cross, out, back, grad_out, cross_mixed, norms, weights, width
    )
    (first_a,), (first_b,) = first_sums(place, [lot_a, lot_b])
    first_ab = (first_a, first_b)
    grad_cross_mixed, part_out[1], *first_ab = tie(grad_cross_mixed, part_out[1], *first_ab)
    first_ab = (over_x(first_ab[0]), swap(first_ab[1]))
    part_out[1] = over_core(part_out[1])
    plan = cross_plan(first_rows, pack_rows, reach, source_rows, width)
    grad_cross_queries, grad_source = attend_back(
        plan,
        cross_queries,
        cross_keys,
        cross_values,
        cross_extra,
        source_marks,
        cross_mixed,
        grad_cross_mixed,
        False,
    )
    grad_source, part_out[1], *first_ab = tie(grad_source, part_out[1], *first_ab)
    encoded_own, encoded_away, *part_source = source_back(
        place, grad_source, source, weights, source_rows // 2
    )
    first_ab = [[first] for first in first_ab]
    second_ab = [second for (second,) in second_sums(place, [lot_a, lot_b], first_ab)]
    grad_cross_queries, encoded_away, *second_ab = tie(
        grad_cross_queries, encoded_away, *second_ab
    )
    second_ab = (swap(second_ab[0]), over_x(second_ab[1]))
    grad_after_self, grad_self_mixed, sums_one, *part_middle = middle(
        place,
        grad_cross_queries,
        second,
        after_self,
        grad_after_cross,
        self_mixed,
        norms,
        weights,
        width,
    )
    grad_self_mixed, part_source[1], part_middle[1], *second_ab = tie(
        grad_self_mixed, part_source[1], part_middle[1], *second_ab
    )
    part_source[1], part_middle[1] = (over_core(part_source[1]), over_core(part_middle[1]))
    third_ab = third_sums(place, [lot_a, lot_b], first_ab, [[second] for second in second_ab])
    lot_c = [part_out, part_source, part_middle]
    ((first_c,),) = first_sums(place, [lot_c])
    grad_self_mixed, first_c, result_away, encoded_away, third_ab = tie(
        grad_self_mixed, first_c, result_away, encoded_away, third_ab
    )
    first_c = over_x(first_c)
    result_away, encoded_away = (swap(result_away), swap(encoded_away))
    total_ab = over_z(third_ab)
    plan = self_plan(first_rows, pack_rows, width)
    grads = attend_back(
        plan,
        query,
        keys,
        values,
        self_extra,
        target_marks,
        self_mixed,
        grad_self_mixed,
        True,
    )
    grads, first_c, result_away, encoded_away, total_ab = tie(
        grads, first_c, result_away, encoded_away, total_ab
    )
    (second_c,) = second_sums(place, [lot_c], [[first_c]], [[3, 2]])
    grads, total_ab, *second_c = tie(grads, total_ab, *second_c)
    second_c[0] = swap(second_c[0])
    lot_d = list(project_grad(place, first, grads))
    lot_d[1], total_ab, *second_c = tie(lot_d[1], total_ab, *second_c)
    second_c[1] = swap(second_c[1])
    lot_d = [(lot_d[0], over_core(lot_d[1]))]
    (first_d,) = first_sums(place, [lot_d], [[2, 1]])
    second_c[1], *first_d = tie(second_c[1], *first_d)
    third_c = third_sums(place, [lot_c], [[first_c]], [second_c])
    grads, third_c, total_ab, *first_d = tie(grads, third_c, total_ab, *first_d)
    total_c, other_ab = (over_z(third_c), swap(total_ab))
    first_d[0] = over_x(first_d[0])
    tokens_own, tokens_away, sums_zero = finish(
        held, grads, halves, grad_after_self, norms, weights, width
    )
    tokens_own, sums_zero, other_ab, *first_d = tie(tokens_own, sums_zero, other_ab, *first_d)
    first_d[1] = over_x(first_d[1])
    tokens_other = swap(tokens_away)
    third_d = direct_sums(place, lot_d[0], first_d)
    sums_zero, other_ab, third_d, result, result_away, encoded_own, encoded_away = tie(
        sums_zero, other_ab, third_d, result, result_away, encoded_own, encoded_away
    )
    total_d = over_z(third_d)
    result = from_both(result, result_away)
    grad_encoded = from_both(encoded_own, encoded_away)
    sums = jnp.concatenate([sums_zero[:2], sums_one[:2], sums_two[:2]])
    for bit in (1, 2, 4, 8):
        sums = sums + lax.ppermute(sums, "fsdp", pairs(bit))
    sums = sums + swap(sums)
    share_ab = both_parts(total_ab, other_ab)
    feed_in_grad, feed_out_grad = feed_shares((share_ab[:4], share_ab[4:]))
    share_c = both_parts(total_c, swap(total_c))
    grad_tokens = from_both(tokens_own, tokens_other)
    tied = (sums, result, grad_encoded, grad_tokens, feed_in_grad, feed_out_grad, share_c, total_d)
    sums, result, grad_encoded, grad_tokens, feed_in_grad, feed_out_grad, share_c, total_d = tie(
        *tied
    )
    share_d = (wide(total_d) + wide(swap(total_d))).transpose(1, 0, 2, 3)

    sums = lax.dynamic_slice_in_dim(sums, spot * part, part, 1)

    return (
        result,
        grad_tokens,
        grad_encoded,
        columns(share_d, 0, 3),
        columns(share_c, 4, 5),
        columns(share_c, 3, 4),
        columns(share_c, 1, 3),
        columns(share_c, 0, 1),
        feed_in_grad,
        feed_out_grad,
        sums[0::2],
        sums[1:4:2],
        sums[5],
    )


def solution(mesh):
    chosen = whole_pack_body if whole_packs(mesh) else body
    return jax.shard_map(
        chosen,
        mesh=mesh,
        in_specs=(
            P(None, "fsdp", "ctx", None),
            P(None, "fsdp", "ctx", None),
            P(None, "fsdp", "ctx", None),
            P(None, "fsdp", None),
            P(None, "fsdp", None),
            P(None, "fsdp", None),
            P("fsdp", None),
            P("fsdp", None),
            P("fsdp", None),
            P("fsdp", None),
            P("fsdp", None),
            P("fsdp", None),
            P("fsdp", None),
            P(None, "fsdp"),
            P(None, "fsdp"),
        ),
        out_specs=(
            P(None, "fsdp", "ctx", None),
            P(None, "fsdp", "ctx", None),
            P(None, "fsdp", "ctx", None),
            P("fsdp", None),
            P("fsdp", None),
            P("fsdp", None),
            P("fsdp", None),
            P("fsdp", None),
            P("fsdp", None),
            P("fsdp", None),
            P(None, "fsdp"),
            P(None, "fsdp"),
            P("fsdp"),
        ),
        check_vma=False,
    )
```

```python
import functools
import math

import jax
import jax.numpy as jnp
from jax import lax
from jax.experimental import pallas as pl
from jax.experimental.pallas import tpu as pltpu
from jax.sharding import PartitionSpec as P

HEAD = 64


MASKED = -1e30


def as_sent(x):

    def short(part):
        return part.astype(jnp.bfloat16) if part.dtype == jnp.float32 else part

    return jax.tree.map(short, x)


def norm_apply(values, gain, bias):
    mean = jnp.mean(values, axis=-1, keepdims=True)
    centred = values - mean
    spread = jnp.mean(centred * centred, axis=-1, keepdims=True)
    return centred * lax.rsqrt(spread + 1e-05) * gain + bias


def gelu_exact(values):
    return jax.nn.gelu(values, approximate=False)


def docs_of(places, lengths):
    ends = jnp.cumsum(lengths)
    return jnp.sum((places[:, None] >= ends[None, :]).astype(jnp.int32), axis=1)


def split_heads(values):
    return values.reshape(values.shape[0], -1, HEAD)


def block_scores(query, pairs, allowed, start, count):
    model = query.shape[1]
    block = lax.dynamic_slice_in_dim(pairs, start, count, 0)
    scores = jnp.einsum(
        "qhd,khd->hqk",
        split_heads(query),
        split_heads(block[:, :model]),
        preferred_element_type=jnp.float32,
    )
    scores = jnp.where(allowed(start, count)[None], scores * HEAD ** (-0.5), MASKED)
    return (scores, block)


def log_mass(query, pairs, allowed, width):
    rows, model = query.shape
    heads = model // HEAD

    def step(index, carry):
        peak, total = carry
        scores, _ = block_scores(query, pairs, allowed, index * width, width)
        new_peak = jnp.maximum(peak, jnp.max(scores, axis=2))
        total = total * jnp.exp(peak - new_peak) + jnp.sum(
            jnp.exp(scores - new_peak[:, :, None]), axis=2
        )
        return (new_peak, total)

    begin = (jnp.full((heads, rows), MASKED, jnp.float32), jnp.zeros((heads, rows), jnp.float32))
    peak, total = lax.fori_loop(0, pairs.shape[0] // width, step, begin)
    return peak + jnp.log(total)


def attend_forward(query, pairs, allowed, width, log_total):
    rows, model = query.shape

    def step(index, mixed):
        scores, block = block_scores(query, pairs, allowed, index * width, width)
        probs = jnp.exp(scores - log_total[:, :, None]).astype(jnp.bfloat16)
        return mixed + jnp.einsum(
            "hqk,khd->qhd", probs, split_heads(block[:, model:]), preferred_element_type=jnp.float32
        )

    mixed = lax.fori_loop(
        0, pairs.shape[0] // width, step, jnp.zeros((rows, model // HEAD, HEAD), jnp.float32)
    )
    return mixed.reshape(rows, model).astype(jnp.bfloat16)


def score_grads(query, pairs, allowed, grad_mixed, log_total, start, count):
    model = query.shape[1]
    scores, block = block_scores(query, pairs, allowed, start, count)
    probs = jnp.exp(scores - log_total[:, :, None])
    grad_probs = jnp.einsum(
        "qhd,khd->hqk",
        split_heads(grad_mixed),
        split_heads(block[:, model:]),
        preferred_element_type=jnp.float32,
    )
    return (probs, grad_probs, block)


def attend_delta(query, pairs, allowed, grad_mixed, log_total, width):
    rows, model = query.shape

    def step(index, delta):
        probs, grad_probs, _ = score_grads(
            query, pairs, allowed, grad_mixed, log_total, index * width, width
        )
        return delta + jnp.sum(probs * grad_probs, axis=2)

    return lax.fori_loop(
        0, pairs.shape[0] // width, step, jnp.zeros((model // HEAD, rows), jnp.float32)
    )


def attend_query_grad(query, pairs, allowed, grad_mixed, log_total, delta, width):
    rows, model = query.shape

    def step(index, grad):
        probs, grad_probs, block = score_grads(
            query, pairs, allowed, grad_mixed, log_total, index * width, width
        )
        grad_scores = (probs * (grad_probs - delta[:, :, None])).astype(jnp.bfloat16)
        return grad + jnp.einsum(
            "hqk,khd->qhd",
            grad_scores,
            split_heads(block[:, :model]),
            preferred_element_type=jnp.float32,
        )

    grad = lax.fori_loop(
        0, pairs.shape[0] // width, step, jnp.zeros((rows, model // HEAD, HEAD), jnp.float32)
    )
    return (grad.reshape(rows, model) * HEAD ** (-0.5)).astype(jnp.bfloat16)


def key_terms(query, pairs, allowed, grad_mixed, log_total, delta, width, count):
    model = query.shape[1]
    step_width = math.gcd(count, width)

    def step(index, terms):
        probs, grad_probs, _ = score_grads(
            query, pairs, allowed, grad_mixed, log_total, index * step_width, step_width
        )
        grad_scores = (probs * (grad_probs - delta[:, :, None])).astype(jnp.bfloat16)
        grad_keys = jnp.einsum(
            "hqk,qhd->khd", grad_scores, split_heads(query), preferred_element_type=jnp.float32
        ) * HEAD ** (-0.5)
        grad_values = jnp.einsum(
            "hqk,qhd->khd",
            probs.astype(jnp.bfloat16),
            split_heads(grad_mixed),
            preferred_element_type=jnp.float32,
        )
        piece = jnp.concatenate(
            [grad_keys.reshape(step_width, model), grad_values.reshape(step_width, model)], axis=1
        )
        return lax.dynamic_update_slice_in_dim(terms, piece, index * step_width, 0)

    return lax.fori_loop(0, count // step_width, step, jnp.zeros((count, 2 * model), jnp.float32))


def body(
    tokens,
    encoded,
    cotangent,
    order,
    target_lengths,
    source_lengths,
    self_project,
    self_output,
    cross_query,
    cross_source,
    cross_output,
    feed_in,
    feed_out,
    norm_gain,
    norm_bias,
):
    micro = tokens.shape[0]
    rows = tokens.shape[2]
    model = tokens.shape[3]
    source_rows = encoded.shape[2]
    place = lax.axis_index("ctx")
    group = lax.axis_size("ctx")
    pack_total = rows * group
    source_total = source_rows * group
    self_width = math.gcd(pack_total, 512)
    cross_width = math.gcd(source_total, 512)
    results = []
    grad_values_all = []
    grad_encoded_all = []
    totals = ()
    for index in range(micro):
        attention_part = (
            lax.all_gather(self_project, "fsdp", axis=0, tiled=True),
            lax.all_gather(self_output, "fsdp", axis=0, tiled=True),
            lax.all_gather(cross_query, "fsdp", axis=0, tiled=True),
            lax.all_gather(cross_source, "fsdp", axis=0, tiled=True),
            lax.all_gather(cross_output, "fsdp", axis=0, tiled=True),
            lax.all_gather(norm_gain, "fsdp", axis=1, tiled=True),
            lax.all_gather(norm_bias, "fsdp", axis=1, tiled=True),
        )
        feed_part = (
            lax.all_gather(feed_in, "fsdp", axis=0, tiled=True),
            lax.all_gather(feed_out, "fsdp", axis=0, tiled=True),
        )
        weights = tuple(attention_part) + tuple(feed_part)
        (
            self_in_full,
            self_out_full,
            cross_query_full,
            cross_source_full,
            cross_out_full,
            gain_full,
            bias_full,
            feed_in_full,
            feed_out_full,
        ) = weights
        gains = gain_full.astype(jnp.float32)
        biases = bias_full.astype(jnp.float32)
        values = tokens[index, 0].astype(jnp.float32)
        source = encoded[index, 0]
        grad_out = cotangent[index, 0]
        places = order[index, 0]
        target_docs = docs_of(places, target_lengths[index, 0])
        query_places = lax.dynamic_slice_in_dim(places, place * rows, rows)
        query_docs = lax.dynamic_slice_in_dim(target_docs, place * rows, rows)
        source_docs = docs_of(jnp.arange(source_total, dtype=jnp.int32), source_lengths[index, 0])

        def self_allowed(start, count):
            key_docs = lax.dynamic_slice_in_dim(target_docs, start, count)
            key_places = lax.dynamic_slice_in_dim(places, start, count)
            return (query_docs[:, None] == key_docs[None, :]) & (
                key_places[None, :] <= query_places[:, None]
            )

        def cross_allowed(start, count):
            return (
                query_docs[:, None] == lax.dynamic_slice_in_dim(source_docs, start, count)[None, :]
            )

        first = norm_apply(values, gains[0], biases[0]).astype(jnp.bfloat16)
        query = jnp.dot(first, self_in_full[:, :model], preferred_element_type=jnp.float32).astype(
            jnp.bfloat16
        )
        local_pairs = jnp.dot(
            first, self_in_full[:, model:], preferred_element_type=jnp.float32
        ).astype(jnp.bfloat16)
        self_pairs = lax.all_gather(local_pairs, "ctx", axis=0, tiled=True)
        self_total = log_mass(query, self_pairs, self_allowed, self_width)
        self_mixed = attend_forward(query, self_pairs, self_allowed, self_width, self_total)
        after_self = values + jnp.dot(self_mixed, self_out_full, preferred_element_type=jnp.float32)
        second = norm_apply(after_self, gains[1], biases[1]).astype(jnp.bfloat16)
        cross_queries = jnp.dot(
            second, cross_query_full, preferred_element_type=jnp.float32
        ).astype(jnp.bfloat16)
        cross_local = jnp.dot(source, cross_source_full, preferred_element_type=jnp.float32).astype(
            jnp.bfloat16
        )
        cross_pairs = lax.all_gather(cross_local, "ctx", axis=0, tiled=True)
        cross_total = log_mass(cross_queries, cross_pairs, cross_allowed, cross_width)
        cross_mixed = attend_forward(
            cross_queries, cross_pairs, cross_allowed, cross_width, cross_total
        )
        after_cross = after_self + jnp.dot(
            cross_mixed, cross_out_full, preferred_element_type=jnp.float32
        )
        third = norm_apply(after_cross, gains[2], biases[2]).astype(jnp.bfloat16)
        hidden = jnp.dot(third, feed_in_full, preferred_element_type=jnp.float32)
        active = gelu_exact(hidden).astype(jnp.bfloat16)
        result = (
            after_cross + jnp.dot(active, feed_out_full, preferred_element_type=jnp.float32)
        ).astype(jnp.bfloat16)
        grad_feed_out = jnp.einsum(
            "rf,rd->fd", active, grad_out, preferred_element_type=jnp.float32
        )
        grad_active = jnp.einsum(
            "rd,fd->rf", grad_out, feed_out_full, preferred_element_type=jnp.float32
        ).astype(jnp.bfloat16)
        _, gelu_pull = jax.vjp(gelu_exact, hidden)
        grad_hidden = gelu_pull(grad_active.astype(jnp.float32))[0].astype(jnp.bfloat16)
        grad_feed_in = jnp.einsum(
            "rd,rf->df", third, grad_hidden, preferred_element_type=jnp.float32
        )
        grad_third = jnp.einsum(
            "rf,df->rd", grad_hidden, feed_in_full, preferred_element_type=jnp.float32
        )
        _, norm_pull = jax.vjp(norm_apply, after_cross, gains[2], biases[2])
        norm_part, gain_two, bias_two = norm_pull(grad_third)
        grad_after_cross = grad_out.astype(jnp.float32) + norm_part
        cross_branch = grad_after_cross.astype(jnp.bfloat16)
        grad_cross_output = jnp.einsum(
            "rd,re->de", cross_mixed, cross_branch, preferred_element_type=jnp.float32
        )
        grad_cross_mixed = jnp.einsum(
            "re,de->rd", cross_branch, cross_out_full, preferred_element_type=jnp.float32
        ).astype(jnp.bfloat16)
        cross_delta = attend_delta(
            cross_queries, cross_pairs, cross_allowed, grad_cross_mixed, cross_total, cross_width
        )
        grad_cross_queries = attend_query_grad(
            cross_queries,
            cross_pairs,
            cross_allowed,
            grad_cross_mixed,
            cross_total,
            cross_delta,
            cross_width,
        )
        grad_source = lax.psum_scatter(
            key_terms(
                cross_queries,
                cross_pairs,
                cross_allowed,
                grad_cross_mixed,
                cross_total,
                cross_delta,
                cross_width,
                source_rows * lax.axis_size("ctx"),
            ).astype(jnp.bfloat16),
            "ctx",
            scatter_dimension=0,
            tiled=True,
        )
        grad_cross_source = jnp.einsum(
            "sd,se->de", source, grad_source, preferred_element_type=jnp.float32
        )
        grad_encoded = jnp.einsum(
            "se,de->sd", grad_source, cross_source_full, preferred_element_type=jnp.float32
        ).astype(jnp.bfloat16)
        grad_cross_query = jnp.einsum(
            "rd,re->de", second, grad_cross_queries, preferred_element_type=jnp.float32
        )
        grad_second = jnp.einsum(
            "re,de->rd", grad_cross_queries, cross_query_full, preferred_element_type=jnp.float32
        )
        _, norm_pull = jax.vjp(norm_apply, after_self, gains[1], biases[1])
        norm_part, gain_one, bias_one = norm_pull(grad_second)
        grad_after_self = grad_after_cross + norm_part
        self_branch = grad_after_self.astype(jnp.bfloat16)
        grad_self_output = jnp.einsum(
            "rd,re->de", self_mixed, self_branch, preferred_element_type=jnp.float32
        )
        grad_self_mixed = jnp.einsum(
            "re,de->rd", self_branch, self_out_full, preferred_element_type=jnp.float32
        ).astype(jnp.bfloat16)
        self_delta = attend_delta(
            query, self_pairs, self_allowed, grad_self_mixed, self_total, self_width
        )
        grad_query = attend_query_grad(
            query, self_pairs, self_allowed, grad_self_mixed, self_total, self_delta, self_width
        )
        grad_pairs = lax.psum_scatter(
            key_terms(
                query,
                self_pairs,
                self_allowed,
                grad_self_mixed,
                self_total,
                self_delta,
                self_width,
                rows * lax.axis_size("ctx"),
            ).astype(jnp.bfloat16),
            "ctx",
            scatter_dimension=0,
            tiled=True,
        )
        grad_projected = jnp.concatenate([grad_query, grad_pairs], axis=1)
        grad_self_project = jnp.einsum(
            "rd,re->de", first, grad_projected, preferred_element_type=jnp.float32
        )
        grad_first = jnp.einsum(
            "re,de->rd", grad_projected, self_in_full, preferred_element_type=jnp.float32
        )
        _, norm_pull = jax.vjp(norm_apply, values, gains[0], biases[0])
        norm_part, gain_zero, bias_zero = norm_pull(grad_first)
        grad_values = (grad_after_self + norm_part).astype(jnp.bfloat16)
        grads = (
            grad_self_project,
            grad_self_output,
            grad_cross_query,
            grad_cross_source,
            grad_cross_output,
            grad_feed_in,
            grad_feed_out,
            jnp.stack([gain_zero, gain_one, gain_two]),
            jnp.stack([bias_zero, bias_one, bias_two]),
        )
        result, grad_values, grad_encoded, grads = (result, grad_values, grad_encoded, grads)
        totals = (
            grads
            if index == 0
            else tuple((jnp.add(left, right) for left, right in zip(totals, grads)))
        )
        results.append(result)
        grad_values_all.append(grad_values)
        grad_encoded_all.append(grad_encoded)
    shares = (
        lax.psum_scatter(
            totals[0].astype(jnp.bfloat16), "fsdp", scatter_dimension=0, tiled=True
        ).astype(jnp.float32),
        lax.psum_scatter(
            totals[1].astype(jnp.bfloat16), "fsdp", scatter_dimension=0, tiled=True
        ).astype(jnp.float32),
        lax.psum_scatter(
            totals[2].astype(jnp.bfloat16), "fsdp", scatter_dimension=0, tiled=True
        ).astype(jnp.float32),
        lax.psum_scatter(
            totals[3].astype(jnp.bfloat16), "fsdp", scatter_dimension=0, tiled=True
        ).astype(jnp.float32),
        lax.psum_scatter(
            totals[4].astype(jnp.bfloat16), "fsdp", scatter_dimension=0, tiled=True
        ).astype(jnp.float32),
        lax.psum_scatter(
            totals[5].astype(jnp.bfloat16), "fsdp", scatter_dimension=0, tiled=True
        ).astype(jnp.float32),
        lax.psum_scatter(
            totals[6].astype(jnp.bfloat16), "fsdp", scatter_dimension=0, tiled=True
        ).astype(jnp.float32),
        lax.psum_scatter(
            totals[7].astype(jnp.bfloat16), "fsdp", scatter_dimension=1, tiled=True
        ).astype(jnp.float32),
        lax.psum_scatter(
            totals[8].astype(jnp.bfloat16), "fsdp", scatter_dimension=1, tiled=True
        ).astype(jnp.float32),
    )
    totals = tuple(
        jax.tree.map(lambda part: part.astype(jnp.float32), lax.psum(as_sent(tuple(shares)), "ctx"))
    )
    output = jnp.stack(results)[:, None]
    grad_tokens = jnp.stack(grad_values_all)[:, None]
    grad_source_rows = jnp.stack(grad_encoded_all)[:, None]
    return (
        output,
        grad_tokens,
        grad_source_rows,
        totals[0],
        totals[1],
        totals[2],
        totals[3],
        totals[4],
        totals[5],
        totals[6],
        totals[7],
        totals[8][:2],
        totals[8][2],
    )


BIG = 1e30
SCALE2 = HEAD ** (-0.5) * math.log2(math.e)
NT = (((1,), (1,)), ((), ()))
TN = (((0,), (0,)), ((), ()))
NN = (((1,), (0,)), ((), ()))


def dot(left, right, dims=NN):
    return lax.dot_general(left, right, dims, preferred_element_type=jnp.float32)


def lanes(rows):
    return lax.broadcasted_iota(jnp.int32, (rows, 128), 1)


def parts(x):
    hi = x.astype(jnp.bfloat16)
    rest = x - hi.astype(jnp.float32)
    mid = rest.astype(jnp.bfloat16)
    lo = (rest - mid.astype(jnp.float32)).astype(jnp.bfloat16)
    return (hi, mid, lo)


def spread(x, base):
    hi, mid, lo = parts(x)
    lane = lanes(x.shape[0]) % HEAD
    return jnp.where(lane == 4, hi, jnp.where(lane == 5, mid, jnp.where(lane == 6, lo, base)))


def two_heads(ref, own, other):
    left = lanes(own.shape[0]) < HEAD
    ref[0] = jnp.where(left, own, other)
    ref[1] = jnp.where(left, other, own)


def tail_masked(scores, rows):
    width = scores.shape[1] - rows
    row = lax.broadcasted_iota(jnp.int32, (rows, rows), 0)
    column = lax.broadcasted_iota(jnp.int32, (rows, rows), 1)
    tail = jnp.where(column > row, -BIG, scores[:, width:])
    return tail if width == 0 else jnp.concatenate([scores[:, :width], tail], axis=1)


def attend_kernel(plan, q_ref, k_ref, v_ref, qd_ref, kd_ref, out_ref, extra_ref, keys, values):
    two_heads(keys, k_ref[...], kd_ref[...])
    two_heads(values, v_ref[...], jnp.ones_like(v_ref))

    def scores_of(item):
        q0, q1, k0, k1, diagonal = item
        left = lanes(q1 - q0) < HEAD
        q, qd = (q_ref[q0:q1], qd_ref[q0:q1])
        pair = [dot(jnp.where(left == (h == 0), q, qd), keys[h, k0:k1], NT) for h in range(2)]
        return [tail_masked(s, q1 - q0) for s in pair] if diagonal else pair

    following = scores_of(plan[0])
    for index, (q0, q1, k0, k1, _) in enumerate(plan):
        scores = following
        following = scores_of(plan[index + 1]) if index + 1 < len(plan) else None
        left = lanes(q1 - q0) < HEAD
        mixed, tops = ([], [])
        for h in range(2):
            top = jnp.max(scores[h], axis=1, keepdims=True)
            probs = jnp.exp2((scores[h] - top) * SCALE2).astype(jnp.bfloat16)
            mixed.append(dot(probs, values[h, k0:k1]))
            tops.append(top)
        mass = jnp.where(left, mixed[1], mixed[0])
        numer = jnp.where(left, mixed[0], mixed[1])
        out_ref[q0:q1] = (numer / pltpu.roll(mass, HEAD, 1)).astype(jnp.bfloat16)
        top = jnp.where(left, tops[1], tops[0])
        extra_ref[q0:q1] = spread(-(top + HEAD**0.5 * jnp.log(mass)), qd_ref[q0:q1])


def attend_back_kernel(
    plan,
    q_ref,
    k_ref,
    v_ref,
    extra_ref,
    kd_ref,
    out_ref,
    g_ref,
    *refs,
):
    *outs, keys, values, queries, grads, g_t, q_t, dk_t, dv_t = refs
    if len(outs) == 1:
        dq_ref, dk_ref, dv_ref = (outs[0].at[i] for i in range(3))
    else:
        dq_ref, dk_ref, dv_ref = (outs[0], outs[1].at[0], outs[1].at[1])
    two_heads(keys, k_ref[...], kd_ref[...])
    two_heads(values, v_ref[...], jnp.ones_like(v_ref))
    two_heads(queries, q_ref[...], extra_ref[...])
    square = (128, 128)
    row, column = (lax.broadcasted_iota(jnp.int32, square, axis) < HEAD for axis in (0, 1))
    across = jnp.where(row != column, 1.0, 0.0).astype(jnp.bfloat16)
    g = g_ref[...]
    terms = parts(g.astype(jnp.float32) * out_ref[...].astype(jnp.float32))
    delta = sum(dot(term, across) for term in terms)
    two_heads(grads, g, spread(-delta, jnp.zeros_like(g)))
    g_t[...] = g.T
    q_t[...] = q_ref[...].T
    dk_t[...] = jnp.zeros_like(dk_t)
    dv_t[...] = jnp.zeros_like(dv_t)
    for q0, q1, k0, k1, diagonal in plan:
        left = lanes(q1 - q0) < HEAD
        pair = []
        for h in range(2):
            s = dot(queries[h, q0:q1], keys[h, k0:k1], NT)
            s = tail_masked(s, q1 - q0) if diagonal else s
            pair.append((s, dot(grads[h, q0:q1], values[h, k0:k1], NT)))
        dqs = []
        for h, (s, grad_probs) in enumerate(pair):
            probs = jnp.exp2(s * SCALE2)
            ds = (probs * grad_probs).astype(jnp.bfloat16)
            head = slice(h * HEAD, h * HEAD + HEAD)
            dv_t[head, k0:k1] += dot(g_t[head, q0:q1], probs.astype(jnp.bfloat16))
            dk_t[head, k0:k1] += dot(q_t[head, q0:q1], ds)
            dqs.append(dot(ds, k_ref[k0:k1]))
        dq_ref[q0:q1] = (jnp.where(left, dqs[0], dqs[1]) * HEAD ** (-0.5)).astype(jnp.bfloat16)
    dk_ref[...] = (dk_t[...].T * HEAD ** (-0.5)).astype(jnp.bfloat16)
    dv_ref[...] = dv_t[...].T.astype(jnp.bfloat16)


def pair_of_heads(rows):
    return pl.BlockSpec((rows, 128), lambda i: (0, i))


def all_of(rows):
    return pl.BlockSpec((rows, 128), lambda i: (0, 0))


def small_cost():
    return pl.CostEstimate(flops=1 << 10, bytes_accessed=1 << 10, transcendentals=0)


def attend(plan, q, k, v, qd, kd):
    nq, nk, model = (q.shape[0], k.shape[0], q.shape[1])
    shape = jax.ShapeDtypeStruct((nq, model), jnp.bfloat16)
    return pl.pallas_call(
        functools.partial(attend_kernel, plan),
        grid=(model // 128,),
        in_specs=[pair_of_heads(n) for n in (nq, nk, nk)] + [all_of(nq), all_of(nk)],
        out_specs=[pair_of_heads(nq)] * 2,
        out_shape=[shape] * 2,
        scratch_shapes=[pltpu.VMEM((2, nk, 128), jnp.bfloat16)] * 2,
        compiler_params=pltpu.CompilerParams(vmem_limit_bytes=58 * 2**20),
        cost_estimate=small_cost(),
    )(q, k, v, qd, kd)


def stacked(count, rows):
    return pl.BlockSpec((count, rows, 128), lambda i: (0, 0, i))


def attend_back(plan, q, k, v, extra, kd, out, g, together):
    nq, nk, model = (q.shape[0], k.shape[0], q.shape[1])
    if together:
        specs, shapes = ([stacked(3, nq)], [(3, nq, model)])
    else:
        specs, shapes = ([pair_of_heads(nq), stacked(2, nk)], [(nq, model), (2, nk, model)])
    outs = pl.pallas_call(
        functools.partial(attend_back_kernel, plan),
        grid=(model // 128,),
        in_specs=[pair_of_heads(n) for n in (nq, nk, nk, nq)]
        + [all_of(nk)]
        + [pair_of_heads(nq)] * 2,
        out_specs=specs,
        out_shape=[jax.ShapeDtypeStruct(shape, jnp.bfloat16) for shape in shapes],
        scratch_shapes=[pltpu.VMEM((2, nk, 128), jnp.bfloat16)] * 2
        + [pltpu.VMEM((2, nq, 128), jnp.bfloat16)] * 2
        + [pltpu.VMEM((128, nq), jnp.bfloat16)] * 2
        + [pltpu.VMEM((128, nk), jnp.float32)] * 2,
        compiler_params=pltpu.CompilerParams(vmem_limit_bytes=58 * 2**20),
        cost_estimate=small_cost(),
    )(q, k, v, extra, kd, out, g)
    return outs[0] if together else outs


def self_plan(first, total, tile):
    return [
        (start, start + tile, low, start + tile, True)
        for low, high in ((0, first), (first, total))
        for start in range(low, high, tile)
    ]


def cross_plan(first, total, reach, source, tile):
    return [
        (start, start + tile, 0, reach if start < first else source, False)
        for start in range(0, total, tile)
    ]


def query_marks(docs):
    lane = jnp.arange(128) % HEAD
    return jnp.where(docs[:, None] == lane[None, :], BIG, 0.0).astype(jnp.bfloat16)


def key_marks(docs, count):
    lane = (jnp.arange(128) % HEAD)[None, :]
    other = jnp.where(docs[:, None] == lane, 0.0, -1.0)
    return jnp.where(lane < count, other, jnp.where(lane < 7, 1.0, 0.0)).astype(jnp.bfloat16)


MODEL = 1024
TILE = 512


def wide(values):
    return values.astype(jnp.float32)


def short(values):
    return values.astype(jnp.bfloat16)


def gathered(ref):
    return ref[...].reshape(-1, ref.shape[-1])


def once(shape, index):
    return pl.BlockSpec(shape, index, pipeline_mode=pl.Buffered(1))


def weight_at(slot):
    return once((16, 64, MODEL), lambda *_: (0, slot, 0))


def norm_rows():
    return once((8, MODEL), lambda *_: (0, 0))


def by_rows(count, width=MODEL):
    return pl.BlockSpec((count, width), lambda i, *_: (i, 0))


def found_rows(count):
    return pl.BlockSpec((count, MODEL), lambda i, held, *_: (held[i], 0))


def kept_or_sent(rows):
    return [once((rows, MODEL), lambda *_: (0, 0)) for _ in range(2)]


def store_found(held, width, own_ref, away_ref, value):
    spot = held[pl.program_id(0)]
    rows = pl.ds(pl.multiple_of(lax.rem(spot, 2) * width, width), width)

    @pl.when(spot < 2)
    def _():
        own_ref[rows] = value

    @pl.when(spot >= 2)
    def _():
        away_ref[rows] = value


def sums_out():
    return pl.BlockSpec((8, MODEL), lambda *_: (0, 0))


def struct(shape, kind):
    return jax.ShapeDtypeStruct(shape, kind)


def spread_of(values):
    mean = jnp.mean(values, axis=-1, keepdims=True)
    centred = values - mean
    scale = lax.rsqrt(jnp.mean(centred * centred, axis=-1, keepdims=True) + 1e-05)
    return (centred * scale, scale)


def norm_of(values, norm_ref, k):
    hat, _ = spread_of(values)
    return short(hat * norm_ref[k : k + 1] + norm_ref[3 + k : 4 + k])


def norm_back(values, grad, norm_ref, k, sums_ref):
    hat, scale = spread_of(values)
    each = grad * norm_ref[k : k + 1]
    inner = each - jnp.mean(each, axis=-1, keepdims=True)
    inner = inner - hat * jnp.mean(each * hat, axis=-1, keepdims=True)
    sums_ref[0:1] += jnp.sum(grad * hat, axis=0, keepdims=True)
    sums_ref[1:2] += jnp.sum(grad, axis=0, keepdims=True)
    return scale * inner


def call(kernel, grid, in_specs, out_specs, out_shape, scratch=(), prefetch=0):
    return pl.pallas_call(
        kernel,
        grid_spec=pltpu.PrefetchScalarGridSpec(
            num_scalar_prefetch=prefetch,
            grid=grid,
            in_specs=in_specs,
            out_specs=out_specs,
            scratch_shapes=list(scratch),
        ),
        out_shape=out_shape,
        compiler_params=pltpu.CompilerParams(vmem_limit_bytes=58 * 2**20),
        cost_estimate=small_cost(),
    )


def pack_kernel(*refs):
    attention_ref, feed_ref = refs[-2:]
    self_in, self_out, cross_q, cross_s, cross_out, feed_in, feed_out, norms = refs[:-2]
    rows = self_in.shape[0]
    slot = 0
    for ref in (self_in, self_out, cross_q, cross_s, cross_out):
        for start in range(0, ref.shape[1], MODEL):
            attention_ref[slot * rows : (slot + 1) * rows] = ref[:, start : start + MODEL]
            slot += 1
    attention_ref[slot * rows :] = norms[...]
    piece = feed_out.shape[0] // 2
    for lot in range(2):
        for owner in range(16):
            column = (2 * owner + lot) * piece
            slot, spot = (2 * lot + owner // 8, owner % 8 * piece)
            feed_ref[slot * rows : (slot + 1) * rows, spot : spot + piece] = feed_in[
                :, column : column + piece
            ]
    feed_ref[4 * rows : 8 * rows] = feed_out[...]
    feed_ref[8 * rows :] = jnp.zeros_like(norms)


def pack(weights, norms):
    arrays = tuple(weights) + (norms,)
    out = struct((528, MODEL), jnp.bfloat16)
    return call(
        pack_kernel,
        (1,),
        [once(a.shape, lambda i: (0, 0)) for a in arrays],
        [once(out.shape, lambda i: (0, 0))] * 2,
        [out] * 2,
    )(*arrays)


def enter_kernel(held, tokens_ref, norm_ref, wq, wk, wv, first_ref, q_ref, k_ref, v_ref):
    first = norm_of(wide(tokens_ref[...]), norm_ref, 0)
    first_ref[...] = first
    for weight, out in ((wq, q_ref), (wk, k_ref), (wv, v_ref)):
        out[...] = short(dot(first, gathered(weight)))


def enter(held, tokens, norms, weights, width):
    shape = struct(tokens.shape, jnp.bfloat16)
    return call(
        enter_kernel,
        (tokens.shape[0] // width,),
        [found_rows(width), norm_rows()] + [weight_at(i) for i in range(3)],
        [by_rows(width)] * 4,
        [shape] * 4,
        prefetch=1,
    )(held, tokens, norms, weights, weights, weights)


def source_kernel(source_ref, wk, wv, k_ref, v_ref):
    source = source_ref[...]
    k_ref[...] = short(dot(source, gathered(wk)))
    v_ref[...] = short(dot(source, gathered(wv)))


def source_pairs(source, weights, width):
    return call(
        source_kernel,
        (source.shape[0] // width,),
        [by_rows(width), weight_at(5), weight_at(6)],
        [by_rows(width)] * 2,
        [struct(source.shape, jnp.bfloat16)] * 2,
    )(source, weights, weights)


def between_kernel(held, mixed_ref, tokens_ref, norm_ref, wo, wq, after_ref, second_ref, q_ref):
    after = wide(tokens_ref[...]) + dot(mixed_ref[...], gathered(wo))
    after_ref[...] = after
    second = norm_of(after, norm_ref, 1)
    second_ref[...] = second
    q_ref[...] = short(dot(second, gathered(wq)))


def between(held, mixed, tokens, norms, weights, width):
    return call(
        between_kernel,
        (mixed.shape[0] // width,),
        [by_rows(width), found_rows(width), norm_rows(), weight_at(3), weight_at(4)],
        [by_rows(width)] * 3,
        [struct(mixed.shape, kind) for kind in (jnp.float32, jnp.bfloat16, jnp.bfloat16)],
        prefetch=1,
    )(held, mixed, tokens, norms, weights, weights)


def before_feed_kernel(
    held, mixed_ref, base_ref, own_ref, other_ref, norm_ref, wo, after_ref, third_ref, grad_ref
):
    after = base_ref[...] + dot(mixed_ref[...], gathered(wo))
    after_ref[...] = after
    third_ref[...] = norm_of(after, norm_ref, 2)
    own = held[pl.program_id(0)] < 2

    @pl.when(own)
    def _():
        grad_ref[...] = own_ref[...]

    @pl.when(jnp.logical_not(own))
    def _():
        grad_ref[...] = other_ref[...]


def before_feed(held, mixed, base, own, other, norms, weights, width):
    return call(
        before_feed_kernel,
        (mixed.shape[0] // width,),
        [
            by_rows(width),
            by_rows(width),
            pl.BlockSpec((width, MODEL), lambda i, held: (jnp.minimum(held[i], 1), 0)),
            pl.BlockSpec((width, MODEL), lambda i, held: (jnp.maximum(held[i] - 2, 0), 0)),
            norm_rows(),
            weight_at(7),
        ],
        [by_rows(width)] * 3,
        [struct(mixed.shape, kind) for kind in (jnp.float32, jnp.bfloat16, jnp.bfloat16)],
        prefetch=1,
    )(held, mixed, base, own, other, norms, weights)


def gelu_terms(hidden):
    bell = jnp.exp2(hidden * hidden * (-0.5 * math.log2(math.e)))
    t = 1.0 / (1.0 + (0.3275911 / math.sqrt(2.0)) * jnp.abs(hidden))
    series = 1.061405429
    for term in (-1.453152027, 1.421413741, -0.284496736, 0.254829592):
        series = series * t + term
    tail = 0.5 * series * t * bell
    return (jnp.where(hidden < 0, tail, 1.0 - tail), bell * (1.0 / math.sqrt(2.0 * math.pi)))


def deal(place_ref, turned, keep_ref, send_ref, pieces, own_y=True):
    for own in range(2):

        @pl.when(place_ref[0] == own)
        def _(own=own):
            for core, x, y, index, value in pieces:
                rel_x = jnp.bitwise_xor(place_ref[1], x)
                rel_y = jnp.bitwise_xor(place_ref[2], y) if own_y else y
                spot = (rel_y, rel_x) if turned else (rel_x, rel_y)
                ref = keep_ref if core == own else send_ref
                ref[spot + index] = value


def shard_pieces(product, slot, *rest):
    pieces = []
    for owner in range(product.shape[0] // 64):
        for y in range(2):
            start = owner * 64 + y * 32
            index = (owner // 4, slot) + rest
            value = short(product[start : start + 32])
            pieces.append((owner % 2, owner // 2 % 2, y, index, value))
    return pieces


def feed_kernel(
    place_ref,
    third_ref,
    grad_ref,
    win_ref,
    wout_ref,
    out_ref,
    back_ref,
    keep_a,
    send_a,
    keep_b,
    send_b,
    third_t,
    active_ref,
    hidden_ref,
):
    step = pl.program_id(0)

    @pl.when(step == 0)
    def _():
        third_t[...] = third_ref[...].T
        out_ref[...] = jnp.zeros_like(out_ref)
        back_ref[...] = jnp.zeros_like(back_ref)

    win, wout = (gathered(win_ref), gathered(wout_ref))
    rows = third_ref.shape[0]
    lots = [slice(start, start + TILE) for start in range(0, rows, TILE)]

    def enter(lot):
        return (dot(third_ref[lot], win), dot(grad_ref[lot], wout, NT))

    def leave(lot, hidden, grad):
        mass, bell = gelu_terms(hidden)
        active = short(hidden * mass)
        grad = short((mass + hidden * bell) * wide(short(grad)))
        active_ref[lot] = active
        hidden_ref[lot] = grad
        out_ref[lot] += dot(active, wout)
        back_ref[lot] += dot(grad, win, NT)

    ready = enter(lots[0])
    for index, lot in enumerate(lots):
        following = enter(lots[index + 1]) if index + 1 < len(lots) else None
        leave(lot, *ready)
        ready = following
    grad_out = short(dot(active_ref[...], grad_ref[...], TN))
    grad_in = short(dot(third_t[...], hidden_ref[...]))
    turn = lax.rem(step, 4)
    side = pl.ds(pl.multiple_of(lax.rem(turn, 2) * TILE, TILE), TILE)
    pieces = shard_pieces(grad_in, turn // 2, slice(None), side)
    for owner in range(4):
        for y in range(2):
            for half in range(2):
                start = owner * 128 + y * 64 + 32 * half
                value = grad_out[start : start + 32]
                pieces.append((owner % 2, owner // 2, y, (turn, 2 + half), value))

    @pl.when(step < 4)
    def _():
        deal(place_ref, False, keep_a, send_a, pieces)

    @pl.when(step >= 4)
    def _():
        deal(place_ref, True, keep_b, send_b, pieces)


def feed(place, third, grad, weights):
    rows = third.shape[0]
    full = struct((rows, MODEL), jnp.float32)
    buffer = struct((2, 2, 4, 4, 32, MODEL), jnp.bfloat16)
    out, back, *lots = call(
        feed_kernel,
        (8,),
        [
            once((rows, MODEL), lambda t, place: (0, 0)),
            once((rows, MODEL), lambda t, place: (0, 0)),
            pl.BlockSpec((16, 64, TILE), lambda t, place: (0, t // 2, t % 2)),
            pl.BlockSpec((4, 128, MODEL), lambda t, place: (t % 4, 2 + t // 4, 0)),
        ],
        [once((rows, MODEL), lambda t, place: (0, 0))] * 2
        + [once(buffer.shape, lambda t, place: (0, 0, 0, 0, 0, 0))] * 4,
        [full, full] + [buffer] * 4,
        scratch=[
            pltpu.VMEM((MODEL, rows), jnp.bfloat16),
            pltpu.VMEM((rows, TILE), jnp.bfloat16),
            pltpu.VMEM((rows, TILE), jnp.bfloat16),
        ],
        prefetch=1,
    )(place, third, grad, weights, weights)
    return out, back, lots[:2], lots[2:]


def clear(*refs):
    @pl.when(pl.program_id(0) == 0)
    def _():
        for ref in refs:
            ref[...] = jnp.zeros_like(ref)


def add_product(total_ref, left, right):
    total_ref[...] += dot(left, right, TN)


def at_end(store):
    pl.when(pl.program_id(0) == pl.num_programs(0) - 1)(store)


def buffer_of(slots):
    return struct((2, 2, 4, slots, 32, MODEL), jnp.bfloat16)


def slots_at(slots):
    return once((2, 2, 4, slots, 32, MODEL), lambda *_: (0,) * 6)


def after_feed_kernel(
    held,
    place,
    after_ref,
    out_ref,
    back_ref,
    grad_ref,
    cross_ref,
    norm_ref,
    wo,
    own_ref,
    away_ref,
    total_ref,
    mixed_ref,
    sums_ref,
    keep_ref,
    send_ref,
    weight_ref,
):
    clear(sums_ref, weight_ref)
    after = after_ref[...]
    result = short(after + out_ref[...])
    store_found(held, after.shape[0], own_ref, away_ref, result)
    part = norm_back(after, back_ref[...], norm_ref, 2, sums_ref)
    total = wide(grad_ref[...]) + part
    total_ref[...] = total
    branch = short(total)
    mixed_ref[...] = short(dot(branch, gathered(wo), NT))
    add_product(weight_ref, cross_ref[...], branch)
    at_end(lambda: deal(place, False, keep_ref, send_ref, shard_pieces(weight_ref, 0)))


def after_feed(held, place, after, out, back, grad, mixed, norms, weights, width):
    narrow = struct(after.shape, jnp.bfloat16)
    full = struct(after.shape, jnp.float32)
    return call(
        after_feed_kernel,
        (after.shape[0] // width,),
        [by_rows(width)] * 5 + [norm_rows(), weight_at(7)],
        kept_or_sent(2 * width) + [by_rows(width)] * 2 + [sums_out()] + [slots_at(1)] * 2,
        [struct((2 * width, MODEL), jnp.bfloat16)] * 2
        + [full, narrow, struct((8, MODEL), jnp.float32)]
        + [buffer_of(1)] * 2,
        scratch=[pltpu.VMEM((MODEL, MODEL), jnp.float32)],
        prefetch=2,
    )(held, place, after, out, back, grad, mixed, norms, weights)


def middle_kernel(
    place,
    grad_ref,
    second_ref,
    after_ref,
    base_ref,
    self_ref,
    norm_ref,
    wq,
    wo,
    *refs,
):
    total_ref, mixed_ref, sums_ref, keep_ref, send_ref, weight_q, weight_o = refs
    clear(sums_ref, weight_q, weight_o)
    grad_q = grad_ref[...]
    grad = dot(grad_q, gathered(wq), NT)
    add_product(weight_q, second_ref[...], grad_q)
    total = base_ref[...] + norm_back(after_ref[...], grad, norm_ref, 1, sums_ref)
    total_ref[...] = total
    branch = short(total)
    mixed_ref[...] = short(dot(branch, gathered(wo), NT))
    add_product(weight_o, self_ref[...], branch)

    @at_end
    def _():
        deal(place, False, keep_ref, send_ref, shard_pieces(weight_q, 0))
        deal(place, False, keep_ref, send_ref, shard_pieces(weight_o, 1))


def middle(place, grad, second, after, base, mixed, norms, weights, width):
    narrow = struct(after.shape, jnp.bfloat16)
    return call(
        middle_kernel,
        (after.shape[0] // width,),
        [by_rows(width)] * 5 + [norm_rows(), weight_at(4), weight_at(3)],
        [by_rows(width)] * 2 + [sums_out()] + [slots_at(2)] * 2,
        [struct(after.shape, jnp.float32), narrow, struct((8, MODEL), jnp.float32)]
        + [buffer_of(2)] * 2,
        scratch=[pltpu.VMEM((MODEL, MODEL), jnp.float32)] * 2,
        prefetch=1,
    )(place, grad, second, after, base, mixed, norms, weights, weights)


def project_grad_kernel(place, left_ref, right_ref, keep_ref, send_ref, left_t):
    @pl.when(pl.program_id(1) == 0)
    def _():
        left_t[...] = left_ref[...].T

    product = dot(left_t[...], right_ref[0])
    deal(place, False, keep_ref, send_ref, shard_pieces(product, 0), own_y=False)


def project_grad(place, left, right):
    rows = left.shape[0]
    block = (2, 2, 4, 1, 32, MODEL)
    return call(
        project_grad_kernel,
        (1, 3),
        [
            pl.BlockSpec((rows, MODEL), lambda t, n, place: (0, t)),
            pl.BlockSpec((1, rows, MODEL), lambda t, n, place: (n, 0, 0)),
        ],
        [pl.BlockSpec(block, lambda t, n, place: (0, 0, t, n, 0, 0))] * 2,
        [buffer_of(3)] * 2,
        scratch=[pltpu.VMEM((MODEL, rows), jnp.bfloat16)],
        prefetch=1,
    )(place, left, right)


def finish_kernel(
    held, grads_ref, tokens_ref, base_ref, norm_ref, wq, wk, wv, own_ref, away_ref, sums_ref
):
    clear(sums_ref)
    grad = sum(dot(grads_ref[i], gathered(w), NT) for i, w in enumerate((wq, wk, wv)))
    part = norm_back(wide(tokens_ref[...]), grad, norm_ref, 0, sums_ref)
    result = short(base_ref[...] + part)
    store_found(held, result.shape[0], own_ref, away_ref, result)


def finish(held, grads, tokens, base, norms, weights, width):
    return call(
        finish_kernel,
        (base.shape[0] // width,),
        [
            pl.BlockSpec((3, width, MODEL), lambda i, *_: (0, i, 0)),
            found_rows(width),
            by_rows(width),
            norm_rows(),
        ]
        + [weight_at(i) for i in range(3)],
        kept_or_sent(2 * width) + [sums_out()],
        [struct((2 * width, MODEL), jnp.bfloat16)] * 2 + [struct((8, MODEL), jnp.float32)],
        prefetch=1,
    )(held, grads, tokens, base, norms, weights, weights, weights)


def source_back_kernel(
    place, grads_ref, source_ref, wk, wv, own_ref, away_ref, keep_ref, send_ref, weight_ref
):
    clear(weight_ref)
    source = source_ref[...].T
    for i in range(2):
        weight_ref[i] += dot(source, grads_ref[i])
    grad = dot(grads_ref[0], gathered(wk), NT) + dot(grads_ref[1], gathered(wv), NT)
    grad = short(grad)

    @pl.when(pl.program_id(0) == place[2])
    def _():
        own_ref[...] = grad

    @pl.when(pl.program_id(0) != place[2])
    def _():
        away_ref[...] = grad

    @at_end
    def _():
        for i in range(2):
            deal(place, False, keep_ref, send_ref, shard_pieces(weight_ref.at[i], i))


def source_back(place, grads, source, weights, width):
    rows = grads.shape[1]
    return call(
        source_back_kernel,
        (rows // width,),
        [
            pl.BlockSpec((2, width, MODEL), lambda i, *_: (0, i, 0)),
            by_rows(width),
            weight_at(5),
            weight_at(6),
        ],
        kept_or_sent(width) + [slots_at(2)] * 2,
        [struct((width, MODEL), jnp.bfloat16)] * 2 + [buffer_of(2)] * 2,
        scratch=[pltpu.VMEM((2, MODEL, MODEL), jnp.float32)],
        prefetch=1,
    )(place, grads, source, weights, weights)


def pairs(bit):
    return [(i, i ^ bit) for i in range(16)]


def swap(values):
    return lax.ppermute(values, "ctx", [(0, 1), (1, 0)])


def over_x(values):
    return lax.ppermute(values, "fsdp", pairs(2))


def over_core(values):
    return lax.ppermute(values, "fsdp", pairs(1))


def tie(*values):
    return lax.optimization_barrier(values)


def lot_specs(lot, first, second, spread, z_of, depth=1):
    specs = []
    for keep, _ in lot:
        slots, rows = keep.shape[3:5]
        block = (1, spread, depth, slots, rows, MODEL)
        specs += [
            pl.BlockSpec(block, lambda i, place: (first, second, z_of(i, place), 0, 0, 0))
        ] * 2
    return specs


def slots_of(lot):
    return sum(keep.shape[3] for keep, _ in lot)


def in_order(i, place):
    return i


def from_own(i, place):
    return lax.rem(place[3] + i, 4)


def pair_sums(refs, count):
    return [wide(refs[2 * i][...]) + wide(refs[2 * i + 1][...]) for i in range(count)]


def depth_of(lots):
    return 4 if sum(slots_of(lot) for lot in lots) < 4 else 1


def ranges(sizes):
    starts = [sum(sizes[:i]) for i in range(len(sizes))]
    return [(start, start + size) for start, size in zip(starts, sizes)]


def overlaps(sources, pieces):
    for i, (s0, s1) in enumerate(ranges(sources)):
        for j, (p0, p1) in enumerate(ranges(pieces)):
            low, high = (max(s0, p0), min(s1, p1))
            if low < high:
                yield i, j, slice(low - s0, high - s0), slice(low - p0, high - p0)


def sizes_of(lot):
    return [keep.shape[3] for keep, _ in lot]


def first_sums(place, lots, cuts=None):
    cuts = cuts or [[slots_of(lot)] for lot in lots]

    def kernel(place_ref, *refs):
        refs = list(refs)
        outs = refs[-sum(len(cut) for cut in cuts) :]
        for lot, cut in zip(lots, cuts):
            values = pair_sums([refs.pop(0) for _ in range(2 * len(lot))], len(lot))
            pieces, outs = (outs[: len(cut)], outs[len(cut) :])
            for i, j, taken, put in overlaps(sizes_of(lot), cut):
                pieces[j][:, :, put] = short(values[i][0, :, :, taken])

    depth = depth_of(lots)
    shapes = [(2, 4, size, 32, MODEL) for cut in cuts for size in cut]
    outs = call(
        kernel,
        (4 // depth,),
        [spec for lot in lots for spec in lot_specs(lot, 1, 0, 2, in_order, depth)],
        [
            pl.BlockSpec((2, depth) + shape[2:], lambda i, place: (0, i, 0, 0, 0))
            for shape in shapes
        ],
        [struct(shape, jnp.bfloat16) for shape in shapes],
        prefetch=1,
    )(place, *[array for lot in lots for pair in lot for array in pair])
    return [outs[start:end] for start, end in ranges([len(cut) for cut in cuts])]


def second_sums(place, lots, firsts, cuts=None):
    cuts = cuts or [[slots_of(lot)] for lot in lots]

    def kernel(place_ref, *refs):
        refs = list(refs)
        outs = refs[-sum(len(cut) for cut in cuts) :]
        for lot, first, cut in zip(lots, firsts, cuts):
            values = pair_sums([refs.pop(0) for _ in range(2 * len(lot))], len(lot))
            received = [wide(refs.pop(0)[0]) for _ in first]
            received = received[0] if len(first) == 1 else jnp.concatenate(received, axis=1)
            pieces, outs = (outs[: len(cut)], outs[len(cut) :])
            spots = ranges(sizes_of(lot))
            for i, j, taken, put in overlaps(sizes_of(lot), cut):
                there = received[:, spots[i][0] + taken.start : spots[i][0] + taken.stop]
                pieces[j][:, put] = short(values[i][0, 0, :, taken] + there)

    depth = depth_of(lots)
    specs, arrays = ([], [])
    for lot, first in zip(lots, firsts):
        specs += lot_specs(lot, 0, 1, 1, in_order, depth)
        specs += [
            pl.BlockSpec((1, depth) + piece.shape[2:], lambda i, place: (1, i, 0, 0, 0))
            for piece in first
        ]
        arrays += [array for pair in lot for array in pair] + list(first)
    shapes = [(4, size, 32, MODEL) for cut in cuts for size in cut]
    outs = call(
        kernel,
        (4 // depth,),
        specs,
        [pl.BlockSpec((depth,) + shape[1:], lambda i, place: (i, 0, 0, 0)) for shape in shapes],
        [struct(shape, jnp.bfloat16) for shape in shapes],
        prefetch=1,
    )(place, *arrays)
    return [outs[start:end] for start, end in ranges([len(cut) for cut in cuts])]


def third_sums(place, lots, firsts, seconds):
    def kernel(place_ref, *refs):
        refs = list(refs)
        out = refs[-1]
        start = 0
        for lot, first, second in zip(lots, firsts, seconds):
            values = pair_sums([refs.pop(0) for _ in range(2 * len(lot))], len(lot))
            parts_of = (
                [wide(refs.pop(0)[0, 0]) for _ in first],
                [wide(refs.pop(0)[0]) for _ in second],
            )
            received = sum(p[0] if len(p) == 1 else jnp.concatenate(p, axis=0) for p in parts_of)
            for value, (s0, s1) in zip(values, ranges(sizes_of(lot))):
                out[0, start + s0 : start + s1] = short(value[0, 0, 0] + received[s0:s1])
            start += slots_of(lot)

    specs, arrays = ([], [])
    for lot, first, second in zip(lots, firsts, seconds):
        specs += lot_specs(lot, 0, 0, 1, in_order)
        specs += [
            pl.BlockSpec((1, 1) + piece.shape[2:], lambda i, place: (0, i, 0, 0, 0))
            for piece in first
        ]
        specs += [
            pl.BlockSpec((1,) + piece.shape[1:], lambda i, place: (i, 0, 0, 0))
            for piece in second
        ]
        arrays += [array for pair in lot for array in pair] + list(first) + list(second)
    shape = (4, sum(slots_of(lot) for lot in lots), 32, MODEL)
    return call(
        kernel,
        (4,),
        specs,
        [pl.BlockSpec((1,) + shape[1:], lambda i, place: (i, 0, 0, 0))],
        [struct(shape, jnp.bfloat16)],
        prefetch=1,
    )(place, *arrays)[0]


def direct_sums(place, lot, first):
    (keep, core) = lot
    slots = keep.shape[3]

    def kernel(place_ref, keep_ref, core_ref, *refs):
        received = [wide(ref[...]) for ref in refs[:-1]]
        received = received[0] if len(first) == 1 else jnp.concatenate(received, axis=2)
        total = wide(keep_ref[0]) + wide(core_ref[0]) + received
        refs[-1][0] = short(total[:, 0])

    block = (1, 2, 1, slots, 32, MODEL)
    shape = (4, 2, slots, 32, MODEL)
    return call(
        kernel,
        (4,),
        [pl.BlockSpec(block, lambda i, place: (0, 0, i, 0, 0, 0))] * 2
        + [
            pl.BlockSpec((2, 1) + piece.shape[2:], lambda i, place: (0, i, 0, 0, 0))
            for piece in first
        ],
        [pl.BlockSpec((1,) + shape[1:], lambda i, place: (i, 0, 0, 0, 0))],
        [struct(shape, jnp.bfloat16)],
        prefetch=1,
    )(place, keep, core, *first)[0]


def over_z(values):
    groups = [[first + 4 * z for z in range(4)] for first in range(4)]
    return lax.psum_scatter(values, "fsdp", scatter_dimension=0, axis_index_groups=groups)


def both_parts(total, other):
    low = lax.axis_index("ctx") == 0
    return wide(jnp.stack([jnp.where(low, total, other), jnp.where(low, other, total)], axis=1))


def columns(shares, start, stop):
    part = shares[start:stop].reshape(stop - start, -1, MODEL)
    return jnp.concatenate(list(part), axis=1)


def feed_shares(lots):
    inner = [lot[:2].reshape(2, 64, 8, 128).transpose(1, 0, 2, 3).reshape(64, 16, 128) for lot in lots]
    inner = jnp.stack(inner, axis=2).reshape(64, 4 * MODEL)
    outer = [lot[2:].transpose(1, 0, 2, 3).reshape(128, MODEL) for lot in lots]
    return inner, jnp.concatenate(outer)


def whole_packs(mesh):
    return mesh.shape["ctx"] == 2 and mesh.shape["fsdp"] == 16


def whole_pack_body(
    tokens,
    encoded,
    cotangent,
    order,
    target_lengths,
    source_lengths,
    self_project,
    self_output,
    cross_query,
    cross_source,
    cross_output,
    feed_in,
    feed_out,
    norm_gain,
    norm_bias,
):
    rows = tokens.shape[2]
    pack_rows, source_rows = (2 * rows, 2 * encoded.shape[2])
    first_rows = 3 * pack_rows // 4
    width = rows // 2
    mine = lax.axis_index("ctx")
    spot = lax.axis_index("fsdp")
    z = spot // 4
    place = jnp.stack([spot % 2, spot // 2 % 2, mine, z]).astype(jnp.int32)
    part = self_project.shape[0]

    norms = jnp.pad(jnp.concatenate([norm_gain, norm_bias]), ((0, 10), (0, MODEL - part)))
    attention_shard, feed_shard = pack(
        (self_project, self_output, cross_query, cross_source, cross_output, feed_in, feed_out),
        norms,
    )
    weights = lax.all_gather(attention_shard, "fsdp", axis=0)
    norms = wide(weights[:, 8 * part : 8 * part + 8, :part])
    norms = norms.transpose(1, 0, 2).reshape(8, MODEL)

    def both_halves(array):
        own = lax.dynamic_index_in_dim(array, mine, 0, False)[0]
        return own, swap(lax.dynamic_index_in_dim(array, 1 - mine, 0, False)[0])

    places = lax.dynamic_index_in_dim(order, mine, 0, False)[0]
    holds = places[::width] // width
    found = jnp.argsort(holds).astype(jnp.int32)
    held = jnp.where(found // 2 == mine, found % 2, 2 + found % 2)

    def from_both(own, other):
        low = mine == 0
        return jnp.stack([jnp.where(low, own, other), jnp.where(low, other, own)])[:, None]

    halves = jnp.concatenate(both_halves(tokens))
    own, other = both_halves(encoded)
    source = jnp.concatenate([jnp.where(mine == 0, own, other), jnp.where(mine == 0, other, own)])
    lengths = lax.dynamic_index_in_dim(target_lengths, mine, 0, False)[0]
    target_docs = docs_of(jnp.arange(pack_rows, dtype=jnp.int32), lengths)
    lengths = lax.dynamic_index_in_dim(source_lengths, mine, 0, False)[0]
    source_docs = docs_of(jnp.arange(source_rows, dtype=jnp.int32), lengths)
    docs = lengths.shape[0]
    marks = query_marks(target_docs)
    target_marks = key_marks(target_docs, docs)
    source_marks = key_marks(source_docs, docs)
    cotangent_own, cotangent_away = (
        lax.dynamic_index_in_dim(cotangent, which, 0, False)[0] for which in (mine, 1 - mine)
    )
    tied = (feed_shard, halves, source, marks, target_marks, source_marks)
    feed_shard, halves, source, marks, target_marks, source_marks, *cotangents = tie(
        *tied, cotangent_own, cotangent_away
    )
    feed_weights = lax.all_gather(feed_shard, "fsdp", axis=0)

    reach = source_rows // 2

    first, query, keys, values = enter(held, halves, norms, weights, width)
    query, cotangents[1] = tie(query, cotangents[1])
    cotangents[1] = swap(cotangents[1])
    plan = self_plan(first_rows, pack_rows, width)
    self_mixed, self_extra = attend(plan, query, keys, values, marks, target_marks)
    self_mixed, source = tie(self_mixed, source)
    cross_keys, cross_values = source_pairs(source, weights, source_rows // 2)
    after_self, second, cross_queries = between(held, self_mixed, halves, norms, weights, width)
    plan = cross_plan(first_rows, pack_rows, reach, source_rows, width)
    cross_mixed, cross_extra = attend(
        plan, cross_queries, cross_keys, cross_values, marks, source_marks
    )
    after_cross, third, grad_out = before_feed(
        held, cross_mixed, after_self, *cotangents, norms, weights, width
    )

    out, back, lot_a, lot_b = feed(place, third, grad_out, feed_weights)
    lot_a, lot_b = ([(lot[0], over_core(lot[1]))] for lot in (lot_a, lot_b))
    result, result_away, grad_after_cross, grad_cross_mixed, sums_two, *part_out = after_feed(
        held, place, after_cross, out, back, grad_out, cross_mixed, norms, weights, width
    )
    (first_a,), (first_b,) = first_sums(place, [lot_a, lot_b])
    first_ab = (first_a, first_b)
    grad_cross_mixed, part_out[1], *first_ab = tie(grad_cross_mixed, part_out[1], *first_ab)
    first_ab = (over_x(first_ab[0]), swap(first_ab[1]))
    part_out[1] = over_core(part_out[1])
    plan = cross_plan(first_rows, pack_rows, reach, source_rows, width)
    grad_cross_queries, grad_source = attend_back(
        plan,
        cross_queries,
        cross_keys,
        cross_values,
        cross_extra,
        source_marks,
        cross_mixed,
        grad_cross_mixed,
        False,
    )
    grad_source, part_out[1], *first_ab = tie(grad_source, part_out[1], *first_ab)
    encoded_own, encoded_away, *part_source = source_back(
        place, grad_source, source, weights, source_rows // 2
    )
    first_ab = [[first] for first in first_ab]
    second_ab = [second for (second,) in second_sums(place, [lot_a, lot_b], first_ab)]
    grad_cross_queries, encoded_away, *second_ab = tie(
        grad_cross_queries, encoded_away, *second_ab
    )
    second_ab = (swap(second_ab[0]), over_x(second_ab[1]))
    grad_after_self, grad_self_mixed, sums_one, *part_middle = middle(
        place,
        grad_cross_queries,
        second,
        after_self,
        grad_after_cross,
        self_mixed,
        norms,
        weights,
        width,
    )
    grad_self_mixed, part_source[1], part_middle[1], *second_ab = tie(
        grad_self_mixed, part_source[1], part_middle[1], *second_ab
    )
    part_source[1], part_middle[1] = (over_core(part_source[1]), over_core(part_middle[1]))
    third_ab = third_sums(place, [lot_a, lot_b], first_ab, [[second] for second in second_ab])
    lot_c = [part_out, part_source, part_middle]
    ((first_c,),) = first_sums(place, [lot_c])
    grad_self_mixed, first_c, result_away, encoded_away, third_ab = tie(
        grad_self_mixed, first_c, result_away, encoded_away, third_ab
    )
    first_c = over_x(first_c)
    result_away, encoded_away = (swap(result_away), swap(encoded_away))
    total_ab = over_z(third_ab)
    plan = self_plan(first_rows, pack_rows, width)
    grads = attend_back(
        plan,
        query,
        keys,
        values,
        self_extra,
        target_marks,
        self_mixed,
        grad_self_mixed,
        True,
    )
    grads, first_c, result_away, encoded_away, total_ab = tie(
        grads, first_c, result_away, encoded_away, total_ab
    )
    (second_c,) = second_sums(place, [lot_c], [[first_c]], [[3, 2]])
    grads, total_ab, *second_c = tie(grads, total_ab, *second_c)
    second_c[0] = swap(second_c[0])
    lot_d = list(project_grad(place, first, grads))
    lot_d[1], total_ab, *second_c = tie(lot_d[1], total_ab, *second_c)
    second_c[1] = swap(second_c[1])
    lot_d = [(lot_d[0], over_core(lot_d[1]))]
    ((first_d,),) = first_sums(place, [lot_d])
    second_c[1], first_d = tie(second_c[1], first_d)
    third_c = third_sums(place, [lot_c], [[first_c]], [second_c])
    grads, third_c, total_ab, first_d = tie(grads, third_c, total_ab, first_d)
    total_c, other_ab = (over_z(third_c), swap(total_ab))
    first_d = over_x(first_d)
    tokens_own, tokens_away, sums_zero = finish(
        held, grads, halves, grad_after_self, norms, weights, width
    )
    tokens_own, sums_zero, other_ab, first_d = tie(tokens_own, sums_zero, other_ab, first_d)
    tokens_other = swap(tokens_away)
    third_d = direct_sums(place, lot_d[0], [first_d])
    sums_zero, other_ab, third_d, result, result_away, encoded_own, encoded_away = tie(
        sums_zero, other_ab, third_d, result, result_away, encoded_own, encoded_away
    )
    total_d = over_z(third_d)
    result = from_both(result, result_away)
    grad_encoded = from_both(encoded_own, encoded_away)
    sums = jnp.concatenate([sums_zero[:2], sums_one[:2], sums_two[:2]])
    for bit in (1, 2, 4, 8):
        sums = sums + lax.ppermute(sums, "fsdp", pairs(bit))
    sums = sums + swap(sums)
    share_ab = both_parts(total_ab, other_ab)
    feed_in_grad, feed_out_grad = feed_shares((share_ab[:4], share_ab[4:]))
    share_c = both_parts(total_c, swap(total_c))
    grad_tokens = from_both(tokens_own, tokens_other)
    tied = (sums, result, grad_encoded, grad_tokens, feed_in_grad, feed_out_grad, share_c, total_d)
    sums, result, grad_encoded, grad_tokens, feed_in_grad, feed_out_grad, share_c, total_d = tie(
        *tied
    )
    share_d = (wide(total_d) + wide(swap(total_d))).transpose(1, 0, 2, 3)

    sums = lax.dynamic_slice_in_dim(sums, spot * part, part, 1)

    return (
        result,
        grad_tokens,
        grad_encoded,
        columns(share_d, 0, 3),
        columns(share_c, 4, 5),
        columns(share_c, 3, 4),
        columns(share_c, 1, 3),
        columns(share_c, 0, 1),
        feed_in_grad,
        feed_out_grad,
        sums[0::2],
        sums[1:4:2],
        sums[5],
    )


def solution(mesh):
    chosen = whole_pack_body if whole_packs(mesh) else body
    return jax.shard_map(
        chosen,
        mesh=mesh,
        in_specs=(
            P(None, "fsdp", "ctx", None),
            P(None, "fsdp", "ctx", None),
            P(None, "fsdp", "ctx", None),
            P(None, "fsdp", None),
            P(None, "fsdp", None),
            P(None, "fsdp", None),
            P("fsdp", None),
            P("fsdp", None),
            P("fsdp", None),
            P("fsdp", None),
            P("fsdp", None),
            P("fsdp", None),
            P("fsdp", None),
            P(None, "fsdp"),
            P(None, "fsdp"),
        ),
        out_specs=(
            P(None, "fsdp", "ctx", None),
            P(None, "fsdp", "ctx", None),
            P(None, "fsdp", "ctx", None),
            P("fsdp", None),
            P("fsdp", None),
            P("fsdp", None),
            P("fsdp", None),
            P("fsdp", None),
            P("fsdp", None),
            P("fsdp", None),
            P(None, "fsdp"),
            P(None, "fsdp"),
            P("fsdp"),
        ),
        check_vma=False,
    )
```

```python
import functools
import math

import jax
import jax.numpy as jnp
from jax import lax
from jax.experimental import pallas as pl
from jax.experimental.pallas import tpu as pltpu
from jax.sharding import PartitionSpec as P

HEAD = 64


MASKED = -1e30


def as_sent(x):

    def short(part):
        return part.astype(jnp.bfloat16) if part.dtype == jnp.float32 else part

    return jax.tree.map(short, x)


def norm_apply(values, gain, bias):
    mean = jnp.mean(values, axis=-1, keepdims=True)
    centred = values - mean
    spread = jnp.mean(centred * centred, axis=-1, keepdims=True)
    return centred * lax.rsqrt(spread + 1e-05) * gain + bias


def gelu_exact(values):
    return jax.nn.gelu(values, approximate=False)


def docs_of(places, lengths):
    ends = jnp.cumsum(lengths)
    return jnp.sum((places[:, None] >= ends[None, :]).astype(jnp.int32), axis=1)


def split_heads(values):
    return values.reshape(values.shape[0], -1, HEAD)


def block_scores(query, pairs, allowed, start, count):
    model = query.shape[1]
    block = lax.dynamic_slice_in_dim(pairs, start, count, 0)
    scores = jnp.einsum(
        "qhd,khd->hqk",
        split_heads(query),
        split_heads(block[:, :model]),
        preferred_element_type=jnp.float32,
    )
    scores = jnp.where(allowed(start, count)[None], scores * HEAD ** (-0.5), MASKED)
    return (scores, block)


def log_mass(query, pairs, allowed, width):
    rows, model = query.shape
    heads = model // HEAD

    def step(index, carry):
        peak, total = carry
        scores, _ = block_scores(query, pairs, allowed, index * width, width)
        new_peak = jnp.maximum(peak, jnp.max(scores, axis=2))
        total = total * jnp.exp(peak - new_peak) + jnp.sum(
            jnp.exp(scores - new_peak[:, :, None]), axis=2
        )
        return (new_peak, total)

    begin = (jnp.full((heads, rows), MASKED, jnp.float32), jnp.zeros((heads, rows), jnp.float32))
    peak, total = lax.fori_loop(0, pairs.shape[0] // width, step, begin)
    return peak + jnp.log(total)


def attend_forward(query, pairs, allowed, width, log_total):
    rows, model = query.shape

    def step(index, mixed):
        scores, block = block_scores(query, pairs, allowed, index * width, width)
        probs = jnp.exp(scores - log_total[:, :, None]).astype(jnp.bfloat16)
        return mixed + jnp.einsum(
            "hqk,khd->qhd", probs, split_heads(block[:, model:]), preferred_element_type=jnp.float32
        )

    mixed = lax.fori_loop(
        0, pairs.shape[0] // width, step, jnp.zeros((rows, model // HEAD, HEAD), jnp.float32)
    )
    return mixed.reshape(rows, model).astype(jnp.bfloat16)


def score_grads(query, pairs, allowed, grad_mixed, log_total, start, count):
    model = query.shape[1]
    scores, block = block_scores(query, pairs, allowed, start, count)
    probs = jnp.exp(scores - log_total[:, :, None])
    grad_probs = jnp.einsum(
        "qhd,khd->hqk",
        split_heads(grad_mixed),
        split_heads(block[:, model:]),
        preferred_element_type=jnp.float32,
    )
    return (probs, grad_probs, block)


def attend_delta(query, pairs, allowed, grad_mixed, log_total, width):
    rows, model = query.shape

    def step(index, delta):
        probs, grad_probs, _ = score_grads(
            query, pairs, allowed, grad_mixed, log_total, index * width, width
        )
        return delta + jnp.sum(probs * grad_probs, axis=2)

    return lax.fori_loop(
        0, pairs.shape[0] // width, step, jnp.zeros((model // HEAD, rows), jnp.float32)
    )


def attend_query_grad(query, pairs, allowed, grad_mixed, log_total, delta, width):
    rows, model = query.shape

    def step(index, grad):
        probs, grad_probs, block = score_grads(
            query, pairs, allowed, grad_mixed, log_total, index * width, width
        )
        grad_scores = (probs * (grad_probs - delta[:, :, None])).astype(jnp.bfloat16)
        return grad + jnp.einsum(
            "hqk,khd->qhd",
            grad_scores,
            split_heads(block[:, :model]),
            preferred_element_type=jnp.float32,
        )

    grad = lax.fori_loop(
        0, pairs.shape[0] // width, step, jnp.zeros((rows, model // HEAD, HEAD), jnp.float32)
    )
    return (grad.reshape(rows, model) * HEAD ** (-0.5)).astype(jnp.bfloat16)


def key_terms(query, pairs, allowed, grad_mixed, log_total, delta, width, count):
    model = query.shape[1]
    step_width = math.gcd(count, width)

    def step(index, terms):
        probs, grad_probs, _ = score_grads(
            query, pairs, allowed, grad_mixed, log_total, index * step_width, step_width
        )
        grad_scores = (probs * (grad_probs - delta[:, :, None])).astype(jnp.bfloat16)
        grad_keys = jnp.einsum(
            "hqk,qhd->khd", grad_scores, split_heads(query), preferred_element_type=jnp.float32
        ) * HEAD ** (-0.5)
        grad_values = jnp.einsum(
            "hqk,qhd->khd",
            probs.astype(jnp.bfloat16),
            split_heads(grad_mixed),
            preferred_element_type=jnp.float32,
        )
        piece = jnp.concatenate(
            [grad_keys.reshape(step_width, model), grad_values.reshape(step_width, model)], axis=1
        )
        return lax.dynamic_update_slice_in_dim(terms, piece, index * step_width, 0)

    return lax.fori_loop(0, count // step_width, step, jnp.zeros((count, 2 * model), jnp.float32))


def body(
    tokens,
    encoded,
    cotangent,
    order,
    target_lengths,
    source_lengths,
    self_project,
    self_output,
    cross_query,
    cross_source,
    cross_output,
    feed_in,
    feed_out,
    norm_gain,
    norm_bias,
):
    micro = tokens.shape[0]
    rows = tokens.shape[2]
    model = tokens.shape[3]
    source_rows = encoded.shape[2]
    place = lax.axis_index("ctx")
    group = lax.axis_size("ctx")
    pack_total = rows * group
    source_total = source_rows * group
    self_width = math.gcd(pack_total, 512)
    cross_width = math.gcd(source_total, 512)
    results = []
    grad_values_all = []
    grad_encoded_all = []
    totals = ()
    for index in range(micro):
        attention_part = (
            lax.all_gather(self_project, "fsdp", axis=0, tiled=True),
            lax.all_gather(self_output, "fsdp", axis=0, tiled=True),
            lax.all_gather(cross_query, "fsdp", axis=0, tiled=True),
            lax.all_gather(cross_source, "fsdp", axis=0, tiled=True),
            lax.all_gather(cross_output, "fsdp", axis=0, tiled=True),
            lax.all_gather(norm_gain, "fsdp", axis=1, tiled=True),
            lax.all_gather(norm_bias, "fsdp", axis=1, tiled=True),
        )
        feed_part = (
            lax.all_gather(feed_in, "fsdp", axis=0, tiled=True),
            lax.all_gather(feed_out, "fsdp", axis=0, tiled=True),
        )
        weights = tuple(attention_part) + tuple(feed_part)
        (
            self_in_full,
            self_out_full,
            cross_query_full,
            cross_source_full,
            cross_out_full,
            gain_full,
            bias_full,
            feed_in_full,
            feed_out_full,
        ) = weights
        gains = gain_full.astype(jnp.float32)
        biases = bias_full.astype(jnp.float32)
        values = tokens[index, 0].astype(jnp.float32)
        source = encoded[index, 0]
        grad_out = cotangent[index, 0]
        places = order[index, 0]
        target_docs = docs_of(places, target_lengths[index, 0])
        query_places = lax.dynamic_slice_in_dim(places, place * rows, rows)
        query_docs = lax.dynamic_slice_in_dim(target_docs, place * rows, rows)
        source_docs = docs_of(jnp.arange(source_total, dtype=jnp.int32), source_lengths[index, 0])

        def self_allowed(start, count):
            key_docs = lax.dynamic_slice_in_dim(target_docs, start, count)
            key_places = lax.dynamic_slice_in_dim(places, start, count)
            return (query_docs[:, None] == key_docs[None, :]) & (
                key_places[None, :] <= query_places[:, None]
            )

        def cross_allowed(start, count):
            return (
                query_docs[:, None] == lax.dynamic_slice_in_dim(source_docs, start, count)[None, :]
            )

        first = norm_apply(values, gains[0], biases[0]).astype(jnp.bfloat16)
        query = jnp.dot(first, self_in_full[:, :model], preferred_element_type=jnp.float32).astype(
            jnp.bfloat16
        )
        local_pairs = jnp.dot(
            first, self_in_full[:, model:], preferred_element_type=jnp.float32
        ).astype(jnp.bfloat16)
        self_pairs = lax.all_gather(local_pairs, "ctx", axis=0, tiled=True)
        self_total = log_mass(query, self_pairs, self_allowed, self_width)
        self_mixed = attend_forward(query, self_pairs, self_allowed, self_width, self_total)
        after_self = values + jnp.dot(self_mixed, self_out_full, preferred_element_type=jnp.float32)
        second = norm_apply(after_self, gains[1], biases[1]).astype(jnp.bfloat16)
        cross_queries = jnp.dot(
            second, cross_query_full, preferred_element_type=jnp.float32
        ).astype(jnp.bfloat16)
        cross_local = jnp.dot(source, cross_source_full, preferred_element_type=jnp.float32).astype(
            jnp.bfloat16
        )
        cross_pairs = lax.all_gather(cross_local, "ctx", axis=0, tiled=True)
        cross_total = log_mass(cross_queries, cross_pairs, cross_allowed, cross_width)
        cross_mixed = attend_forward(
            cross_queries, cross_pairs, cross_allowed, cross_width, cross_total
        )
        after_cross = after_self + jnp.dot(
            cross_mixed, cross_out_full, preferred_element_type=jnp.float32
        )
        third = norm_apply(after_cross, gains[2], biases[2]).astype(jnp.bfloat16)
        hidden = jnp.dot(third, feed_in_full, preferred_element_type=jnp.float32)
        active = gelu_exact(hidden).astype(jnp.bfloat16)
        result = (
            after_cross + jnp.dot(active, feed_out_full, preferred_element_type=jnp.float32)
        ).astype(jnp.bfloat16)
        grad_feed_out = jnp.einsum(
            "rf,rd->fd", active, grad_out, preferred_element_type=jnp.float32
        )
        grad_active = jnp.einsum(
            "rd,fd->rf", grad_out, feed_out_full, preferred_element_type=jnp.float32
        ).astype(jnp.bfloat16)
        _, gelu_pull = jax.vjp(gelu_exact, hidden)
        grad_hidden = gelu_pull(grad_active.astype(jnp.float32))[0].astype(jnp.bfloat16)
        grad_feed_in = jnp.einsum(
            "rd,rf->df", third, grad_hidden, preferred_element_type=jnp.float32
        )
        grad_third = jnp.einsum(
            "rf,df->rd", grad_hidden, feed_in_full, preferred_element_type=jnp.float32
        )
        _, norm_pull = jax.vjp(norm_apply, after_cross, gains[2], biases[2])
        norm_part, gain_two, bias_two = norm_pull(grad_third)
        grad_after_cross = grad_out.astype(jnp.float32) + norm_part
        cross_branch = grad_after_cross.astype(jnp.bfloat16)
        grad_cross_output = jnp.einsum(
            "rd,re->de", cross_mixed, cross_branch, preferred_element_type=jnp.float32
        )
        grad_cross_mixed = jnp.einsum(
            "re,de->rd", cross_branch, cross_out_full, preferred_element_type=jnp.float32
        ).astype(jnp.bfloat16)
        cross_delta = attend_delta(
            cross_queries, cross_pairs, cross_allowed, grad_cross_mixed, cross_total, cross_width
        )
        grad_cross_queries = attend_query_grad(
            cross_queries,
            cross_pairs,
            cross_allowed,
            grad_cross_mixed,
            cross_total,
            cross_delta,
            cross_width,
        )
        grad_source = lax.psum_scatter(
            key_terms(
                cross_queries,
                cross_pairs,
                cross_allowed,
                grad_cross_mixed,
                cross_total,
                cross_delta,
                cross_width,
                source_rows * lax.axis_size("ctx"),
            ).astype(jnp.bfloat16),
            "ctx",
            scatter_dimension=0,
            tiled=True,
        )
        grad_cross_source = jnp.einsum(
            "sd,se->de", source, grad_source, preferred_element_type=jnp.float32
        )
        grad_encoded = jnp.einsum(
            "se,de->sd", grad_source, cross_source_full, preferred_element_type=jnp.float32
        ).astype(jnp.bfloat16)
        grad_cross_query = jnp.einsum(
            "rd,re->de", second, grad_cross_queries, preferred_element_type=jnp.float32
        )
        grad_second = jnp.einsum(
            "re,de->rd", grad_cross_queries, cross_query_full, preferred_element_type=jnp.float32
        )
        _, norm_pull = jax.vjp(norm_apply, after_self, gains[1], biases[1])
        norm_part, gain_one, bias_one = norm_pull(grad_second)
        grad_after_self = grad_after_cross + norm_part
        self_branch = grad_after_self.astype(jnp.bfloat16)
        grad_self_output = jnp.einsum(
            "rd,re->de", self_mixed, self_branch, preferred_element_type=jnp.float32
        )
        grad_self_mixed = jnp.einsum(
            "re,de->rd", self_branch, self_out_full, preferred_element_type=jnp.float32
        ).astype(jnp.bfloat16)
        self_delta = attend_delta(
            query, self_pairs, self_allowed, grad_self_mixed, self_total, self_width
        )
        grad_query = attend_query_grad(
            query, self_pairs, self_allowed, grad_self_mixed, self_total, self_delta, self_width
        )
        grad_pairs = lax.psum_scatter(
            key_terms(
                query,
                self_pairs,
                self_allowed,
                grad_self_mixed,
                self_total,
                self_delta,
                self_width,
                rows * lax.axis_size("ctx"),
            ).astype(jnp.bfloat16),
            "ctx",
            scatter_dimension=0,
            tiled=True,
        )
        grad_projected = jnp.concatenate([grad_query, grad_pairs], axis=1)
        grad_self_project = jnp.einsum(
            "rd,re->de", first, grad_projected, preferred_element_type=jnp.float32
        )
        grad_first = jnp.einsum(
            "re,de->rd", grad_projected, self_in_full, preferred_element_type=jnp.float32
        )
        _, norm_pull = jax.vjp(norm_apply, values, gains[0], biases[0])
        norm_part, gain_zero, bias_zero = norm_pull(grad_first)
        grad_values = (grad_after_self + norm_part).astype(jnp.bfloat16)
        grads = (
            grad_self_project,
            grad_self_output,
            grad_cross_query,
            grad_cross_source,
            grad_cross_output,
            grad_feed_in,
            grad_feed_out,
            jnp.stack([gain_zero, gain_one, gain_two]),
            jnp.stack([bias_zero, bias_one, bias_two]),
        )
        result, grad_values, grad_encoded, grads = (result, grad_values, grad_encoded, grads)
        totals = (
            grads
            if index == 0
            else tuple((jnp.add(left, right) for left, right in zip(totals, grads)))
        )
        results.append(result)
        grad_values_all.append(grad_values)
        grad_encoded_all.append(grad_encoded)
    shares = (
        lax.psum_scatter(
            totals[0].astype(jnp.bfloat16), "fsdp", scatter_dimension=0, tiled=True
        ).astype(jnp.float32),
        lax.psum_scatter(
            totals[1].astype(jnp.bfloat16), "fsdp", scatter_dimension=0, tiled=True
        ).astype(jnp.float32),
        lax.psum_scatter(
            totals[2].astype(jnp.bfloat16), "fsdp", scatter_dimension=0, tiled=True
        ).astype(jnp.float32),
        lax.psum_scatter(
            totals[3].astype(jnp.bfloat16), "fsdp", scatter_dimension=0, tiled=True
        ).astype(jnp.float32),
        lax.psum_scatter(
            totals[4].astype(jnp.bfloat16), "fsdp", scatter_dimension=0, tiled=True
        ).astype(jnp.float32),
        lax.psum_scatter(
            totals[5].astype(jnp.bfloat16), "fsdp", scatter_dimension=0, tiled=True
        ).astype(jnp.float32),
        lax.psum_scatter(
            totals[6].astype(jnp.bfloat16), "fsdp", scatter_dimension=0, tiled=True
        ).astype(jnp.float32),
        lax.psum_scatter(
            totals[7].astype(jnp.bfloat16), "fsdp", scatter_dimension=1, tiled=True
        ).astype(jnp.float32),
        lax.psum_scatter(
            totals[8].astype(jnp.bfloat16), "fsdp", scatter_dimension=1, tiled=True
        ).astype(jnp.float32),
    )
    totals = tuple(
        jax.tree.map(lambda part: part.astype(jnp.float32), lax.psum(as_sent(tuple(shares)), "ctx"))
    )
    output = jnp.stack(results)[:, None]
    grad_tokens = jnp.stack(grad_values_all)[:, None]
    grad_source_rows = jnp.stack(grad_encoded_all)[:, None]
    return (
        output,
        grad_tokens,
        grad_source_rows,
        totals[0],
        totals[1],
        totals[2],
        totals[3],
        totals[4],
        totals[5],
        totals[6],
        totals[7],
        totals[8][:2],
        totals[8][2],
    )


BIG = 1e30
SCALE2 = HEAD ** (-0.5) * math.log2(math.e)
NT = (((1,), (1,)), ((), ()))
TN = (((0,), (0,)), ((), ()))
NN = (((1,), (0,)), ((), ()))


def dot(left, right, dims=NN):
    return lax.dot_general(left, right, dims, preferred_element_type=jnp.float32)


def lanes(rows):
    return lax.broadcasted_iota(jnp.int32, (rows, 128), 1)


def parts(x):
    hi = x.astype(jnp.bfloat16)
    rest = x - hi.astype(jnp.float32)
    mid = rest.astype(jnp.bfloat16)
    lo = (rest - mid.astype(jnp.float32)).astype(jnp.bfloat16)
    return (hi, mid, lo)


def spread(x, base):
    hi, mid, lo = parts(x)
    lane = lanes(x.shape[0]) % HEAD
    return jnp.where(lane == 4, hi, jnp.where(lane == 5, mid, jnp.where(lane == 6, lo, base)))


def two_heads(ref, own, other):
    left = lanes(own.shape[0]) < HEAD
    ref[0] = jnp.where(left, own, other)
    ref[1] = jnp.where(left, other, own)


def tail_masked(scores, rows):
    width = scores.shape[1] - rows
    row = lax.broadcasted_iota(jnp.int32, (rows, rows), 0)
    column = lax.broadcasted_iota(jnp.int32, (rows, rows), 1)
    tail = jnp.where(column > row, -BIG, scores[:, width:])
    return tail if width == 0 else jnp.concatenate([scores[:, :width], tail], axis=1)


def attend_kernel(plan, q_ref, k_ref, v_ref, qd_ref, kd_ref, out_ref, extra_ref, keys, values):
    two_heads(keys, k_ref[...], kd_ref[...])
    two_heads(values, v_ref[...], jnp.ones_like(v_ref))

    def scores_of(item):
        q0, q1, k0, k1, diagonal = item
        left = lanes(q1 - q0) < HEAD
        q, qd = (q_ref[q0:q1], qd_ref[q0:q1])
        pair = [dot(jnp.where(left == (h == 0), q, qd), keys[h, k0:k1], NT) for h in range(2)]
        return [tail_masked(s, q1 - q0) for s in pair] if diagonal else pair

    following = scores_of(plan[0])
    for index, (q0, q1, k0, k1, _) in enumerate(plan):
        scores = following
        following = scores_of(plan[index + 1]) if index + 1 < len(plan) else None
        left = lanes(q1 - q0) < HEAD
        mixed, tops = ([], [])
        for h in range(2):
            top = jnp.max(scores[h], axis=1, keepdims=True)
            probs = jnp.exp2((scores[h] - top) * SCALE2).astype(jnp.bfloat16)
            mixed.append(dot(probs, values[h, k0:k1]))
            tops.append(top)
        mass = jnp.where(left, mixed[1], mixed[0])
        numer = jnp.where(left, mixed[0], mixed[1])
        out_ref[q0:q1] = (numer / pltpu.roll(mass, HEAD, 1)).astype(jnp.bfloat16)
        top = jnp.where(left, tops[1], tops[0])
        extra_ref[q0:q1] = spread(-(top + HEAD**0.5 * jnp.log(mass)), qd_ref[q0:q1])


def attend_back_kernel(
    plan,
    q_ref,
    k_ref,
    v_ref,
    extra_ref,
    kd_ref,
    out_ref,
    g_ref,
    *refs,
):
    *outs, keys, values, queries, grads, g_t, q_t, dk_t, dv_t = refs
    if len(outs) == 1:
        dq_ref, dk_ref, dv_ref = (outs[0].at[i] for i in range(3))
    else:
        dq_ref, dk_ref, dv_ref = (outs[0], outs[1].at[0], outs[1].at[1])
    two_heads(keys, k_ref[...], kd_ref[...])
    two_heads(values, v_ref[...], jnp.ones_like(v_ref))
    two_heads(queries, q_ref[...], extra_ref[...])
    square = (128, 128)
    row, column = (lax.broadcasted_iota(jnp.int32, square, axis) < HEAD for axis in (0, 1))
    across = jnp.where(row != column, 1.0, 0.0).astype(jnp.bfloat16)
    g = g_ref[...]
    terms = parts(g.astype(jnp.float32) * out_ref[...].astype(jnp.float32))
    delta = sum(dot(term, across) for term in terms)
    two_heads(grads, g, spread(-delta, jnp.zeros_like(g)))
    g_t[...] = g.T
    q_t[...] = q_ref[...].T
    dk_t[...] = jnp.zeros_like(dk_t)
    dv_t[...] = jnp.zeros_like(dv_t)
    for q0, q1, k0, k1, diagonal in plan:
        left = lanes(q1 - q0) < HEAD
        pair = []
        for h in range(2):
            s = dot(queries[h, q0:q1], keys[h, k0:k1], NT)
            s = tail_masked(s, q1 - q0) if diagonal else s
            pair.append((s, dot(grads[h, q0:q1], values[h, k0:k1], NT)))
        dqs = []
        for h, (s, grad_probs) in enumerate(pair):
            probs = jnp.exp2(s * SCALE2)
            ds = (probs * grad_probs).astype(jnp.bfloat16)
            head = slice(h * HEAD, h * HEAD + HEAD)
            dv_t[head, k0:k1] += dot(g_t[head, q0:q1], probs.astype(jnp.bfloat16))
            dk_t[head, k0:k1] += dot(q_t[head, q0:q1], ds)
            dqs.append(dot(ds, k_ref[k0:k1]))
        dq_ref[q0:q1] = (jnp.where(left, dqs[0], dqs[1]) * HEAD ** (-0.5)).astype(jnp.bfloat16)
    dk_ref[...] = (dk_t[...].T * HEAD ** (-0.5)).astype(jnp.bfloat16)
    dv_ref[...] = dv_t[...].T.astype(jnp.bfloat16)


def pair_of_heads(rows):
    return pl.BlockSpec((rows, 128), lambda i: (0, i))


def all_of(rows):
    return pl.BlockSpec((rows, 128), lambda i: (0, 0))


def small_cost():
    return pl.CostEstimate(flops=1 << 10, bytes_accessed=1 << 10, transcendentals=0)


def attend(plan, q, k, v, qd, kd):
    nq, nk, model = (q.shape[0], k.shape[0], q.shape[1])
    shape = jax.ShapeDtypeStruct((nq, model), jnp.bfloat16)
    return pl.pallas_call(
        functools.partial(attend_kernel, plan),
        grid=(model // 128,),
        in_specs=[pair_of_heads(n) for n in (nq, nk, nk)] + [all_of(nq), all_of(nk)],
        out_specs=[pair_of_heads(nq)] * 2,
        out_shape=[shape] * 2,
        scratch_shapes=[pltpu.VMEM((2, nk, 128), jnp.bfloat16)] * 2,
        compiler_params=pltpu.CompilerParams(vmem_limit_bytes=58 * 2**20),
        cost_estimate=small_cost(),
    )(q, k, v, qd, kd)


def stacked(count, rows):
    return pl.BlockSpec((count, rows, 128), lambda i: (0, 0, i))


def attend_back(plan, q, k, v, extra, kd, out, g, together):
    nq, nk, model = (q.shape[0], k.shape[0], q.shape[1])
    if together:
        specs, shapes = ([stacked(3, nq)], [(3, nq, model)])
    else:
        specs, shapes = ([pair_of_heads(nq), stacked(2, nk)], [(nq, model), (2, nk, model)])
    outs = pl.pallas_call(
        functools.partial(attend_back_kernel, plan),
        grid=(model // 128,),
        in_specs=[pair_of_heads(n) for n in (nq, nk, nk, nq)]
        + [all_of(nk)]
        + [pair_of_heads(nq)] * 2,
        out_specs=specs,
        out_shape=[jax.ShapeDtypeStruct(shape, jnp.bfloat16) for shape in shapes],
        scratch_shapes=[pltpu.VMEM((2, nk, 128), jnp.bfloat16)] * 2
        + [pltpu.VMEM((2, nq, 128), jnp.bfloat16)] * 2
        + [pltpu.VMEM((128, nq), jnp.bfloat16)] * 2
        + [pltpu.VMEM((128, nk), jnp.float32)] * 2,
        compiler_params=pltpu.CompilerParams(vmem_limit_bytes=58 * 2**20),
        cost_estimate=small_cost(),
    )(q, k, v, extra, kd, out, g)
    return outs[0] if together else outs


def self_plan(first, total, tile):
    return [
        (start, start + tile, low, start + tile, True)
        for low, high in ((0, first), (first, total))
        for start in range(low, high, tile)
    ]


def cross_plan(first, total, reach, source, tile):
    return [
        (start, start + tile, 0, reach if start < first else source, False)
        for start in range(0, total, tile)
    ]


def query_marks(docs):
    lane = jnp.arange(128) % HEAD
    return jnp.where(docs[:, None] == lane[None, :], BIG, 0.0).astype(jnp.bfloat16)


def key_marks(docs, count):
    lane = (jnp.arange(128) % HEAD)[None, :]
    other = jnp.where(docs[:, None] == lane, 0.0, -1.0)
    return jnp.where(lane < count, other, jnp.where(lane < 7, 1.0, 0.0)).astype(jnp.bfloat16)


MODEL = 1024
TILE = 512


def wide(values):
    return values.astype(jnp.float32)


def short(values):
    return values.astype(jnp.bfloat16)


def gathered(ref):
    return ref[...].reshape(-1, ref.shape[-1])


def once(shape, index):
    return pl.BlockSpec(shape, index, pipeline_mode=pl.Buffered(1))


def weight_at(slot):
    return once((16, 64, MODEL), lambda *_: (0, slot, 0))


def norm_rows():
    return once((8, MODEL), lambda *_: (0, 0))


def by_rows(count, width=MODEL):
    return pl.BlockSpec((count, width), lambda i, *_: (i, 0))


def found_rows(count):
    return pl.BlockSpec((count, MODEL), lambda i, held, *_: (held[i], 0))


def kept_or_sent(rows):
    return [once((rows, MODEL), lambda *_: (0, 0)) for _ in range(2)]


def store_found(held, width, own_ref, away_ref, value):
    spot = held[pl.program_id(0)]
    rows = pl.ds(pl.multiple_of(lax.rem(spot, 2) * width, width), width)

    @pl.when(spot < 2)
    def _():
        own_ref[rows] = value

    @pl.when(spot >= 2)
    def _():
        away_ref[rows] = value


def sums_out():
    return pl.BlockSpec((8, MODEL), lambda *_: (0, 0))


def struct(shape, kind):
    return jax.ShapeDtypeStruct(shape, kind)


def spread_of(values):
    mean = jnp.mean(values, axis=-1, keepdims=True)
    centred = values - mean
    scale = lax.rsqrt(jnp.mean(centred * centred, axis=-1, keepdims=True) + 1e-05)
    return (centred * scale, scale)


def norm_of(values, norm_ref, k):
    hat, _ = spread_of(values)
    return short(hat * norm_ref[k : k + 1] + norm_ref[3 + k : 4 + k])


def norm_back(values, grad, norm_ref, k, sums_ref):
    hat, scale = spread_of(values)
    each = grad * norm_ref[k : k + 1]
    inner = each - jnp.mean(each, axis=-1, keepdims=True)
    inner = inner - hat * jnp.mean(each * hat, axis=-1, keepdims=True)
    sums_ref[0:1] += jnp.sum(grad * hat, axis=0, keepdims=True)
    sums_ref[1:2] += jnp.sum(grad, axis=0, keepdims=True)
    return scale * inner


def call(kernel, grid, in_specs, out_specs, out_shape, scratch=(), prefetch=0):
    return pl.pallas_call(
        kernel,
        grid_spec=pltpu.PrefetchScalarGridSpec(
            num_scalar_prefetch=prefetch,
            grid=grid,
            in_specs=in_specs,
            out_specs=out_specs,
            scratch_shapes=list(scratch),
        ),
        out_shape=out_shape,
        compiler_params=pltpu.CompilerParams(vmem_limit_bytes=58 * 2**20),
        cost_estimate=small_cost(),
    )


def pack_kernel(*refs):
    attention_ref, feed_ref = refs[-2:]
    self_in, self_out, cross_q, cross_s, cross_out, feed_in, feed_out, norms = refs[:-2]
    rows = self_in.shape[0]
    slot = 0
    for ref in (self_in, self_out, cross_q, cross_s, cross_out):
        for start in range(0, ref.shape[1], MODEL):
            attention_ref[slot * rows : (slot + 1) * rows] = ref[:, start : start + MODEL]
            slot += 1
    attention_ref[slot * rows :] = norms[...]
    piece = feed_out.shape[0] // 2
    for lot in range(2):
        for owner in range(16):
            column = (2 * owner + lot) * piece
            slot, spot = (2 * lot + owner // 8, owner % 8 * piece)
            feed_ref[slot * rows : (slot + 1) * rows, spot : spot + piece] = feed_in[
                :, column : column + piece
            ]
    feed_ref[4 * rows : 8 * rows] = feed_out[...]
    feed_ref[8 * rows :] = jnp.zeros_like(norms)


def pack(weights, norms):
    arrays = tuple(weights) + (norms,)
    out = struct((528, MODEL), jnp.bfloat16)
    return call(
        pack_kernel,
        (1,),
        [once(a.shape, lambda i: (0, 0)) for a in arrays],
        [once(out.shape, lambda i: (0, 0))] * 2,
        [out] * 2,
    )(*arrays)


def enter_kernel(held, tokens_ref, norm_ref, wq, wk, wv, first_ref, q_ref, k_ref, v_ref):
    first = norm_of(wide(tokens_ref[...]), norm_ref, 0)
    first_ref[...] = first
    for weight, out in ((wq, q_ref), (wk, k_ref), (wv, v_ref)):
        out[...] = short(dot(first, gathered(weight)))


def enter(held, tokens, norms, weights, width):
    shape = struct(tokens.shape, jnp.bfloat16)
    return call(
        enter_kernel,
        (tokens.shape[0] // width,),
        [found_rows(width), norm_rows()] + [weight_at(i) for i in range(3)],
        [by_rows(width)] * 4,
        [shape] * 4,
        prefetch=1,
    )(held, tokens, norms, weights, weights, weights)


def source_kernel(source_ref, wk, wv, k_ref, v_ref):
    source = source_ref[...]
    k_ref[...] = short(dot(source, gathered(wk)))
    v_ref[...] = short(dot(source, gathered(wv)))


def source_pairs(source, weights, width):
    return call(
        source_kernel,
        (source.shape[0] // width,),
        [by_rows(width), weight_at(5), weight_at(6)],
        [by_rows(width)] * 2,
        [struct(source.shape, jnp.bfloat16)] * 2,
    )(source, weights, weights)


def between_kernel(held, mixed_ref, tokens_ref, norm_ref, wo, wq, after_ref, second_ref, q_ref):
    after = wide(tokens_ref[...]) + dot(mixed_ref[...], gathered(wo))
    after_ref[...] = after
    second = norm_of(after, norm_ref, 1)
    second_ref[...] = second
    q_ref[...] = short(dot(second, gathered(wq)))


def between(held, mixed, tokens, norms, weights, width):
    return call(
        between_kernel,
        (mixed.shape[0] // width,),
        [by_rows(width), found_rows(width), norm_rows(), weight_at(3), weight_at(4)],
        [by_rows(width)] * 3,
        [struct(mixed.shape, kind) for kind in (jnp.float32, jnp.bfloat16, jnp.bfloat16)],
        prefetch=1,
    )(held, mixed, tokens, norms, weights, weights)


def before_feed_kernel(
    held, mixed_ref, base_ref, own_ref, other_ref, norm_ref, wo, after_ref, third_ref, grad_ref
):
    after = base_ref[...] + dot(mixed_ref[...], gathered(wo))
    after_ref[...] = after
    third_ref[...] = norm_of(after, norm_ref, 2)
    own = held[pl.program_id(0)] < 2

    @pl.when(own)
    def _():
        grad_ref[...] = own_ref[...]

    @pl.when(jnp.logical_not(own))
    def _():
        grad_ref[...] = other_ref[...]


def before_feed(held, mixed, base, own, other, norms, weights, width):
    return call(
        before_feed_kernel,
        (mixed.shape[0] // width,),
        [
            by_rows(width),
            by_rows(width),
            pl.BlockSpec((width, MODEL), lambda i, held: (jnp.minimum(held[i], 1), 0)),
            pl.BlockSpec((width, MODEL), lambda i, held: (jnp.maximum(held[i] - 2, 0), 0)),
            norm_rows(),
            weight_at(7),
        ],
        [by_rows(width)] * 3,
        [struct(mixed.shape, kind) for kind in (jnp.float32, jnp.bfloat16, jnp.bfloat16)],
        prefetch=1,
    )(held, mixed, base, own, other, norms, weights)


def gelu_terms(hidden):
    bell = jnp.exp2(hidden * hidden * (-0.5 * math.log2(math.e)))
    t = 1.0 / (1.0 + (0.3275911 / math.sqrt(2.0)) * jnp.abs(hidden))
    series = 1.061405429
    for term in (-1.453152027, 1.421413741, -0.284496736, 0.254829592):
        series = series * t + term
    tail = 0.5 * series * t * bell
    return (jnp.where(hidden < 0, tail, 1.0 - tail), bell * (1.0 / math.sqrt(2.0 * math.pi)))


def deal(place_ref, turned, keep_ref, send_ref, pieces, own_y=True):
    for own in range(2):

        @pl.when(place_ref[0] == own)
        def _(own=own):
            for core, x, y, index, value in pieces:
                rel_x = jnp.bitwise_xor(place_ref[1], x)
                rel_y = jnp.bitwise_xor(place_ref[2], y) if own_y else y
                spot = (rel_y, rel_x) if turned else (rel_x, rel_y)
                ref = keep_ref if core == own else send_ref
                ref[spot + index] = value


def shard_pieces(product, slot, *rest):
    pieces = []
    for owner in range(product.shape[0] // 64):
        for y in range(2):
            start = owner * 64 + y * 32
            index = (owner // 4, slot) + rest
            value = short(product[start : start + 32])
            pieces.append((owner % 2, owner // 2 % 2, y, index, value))
    return pieces


def feed_kernel(
    place_ref,
    third_ref,
    grad_ref,
    win_ref,
    wout_ref,
    out_ref,
    back_ref,
    keep_a,
    send_a,
    keep_b,
    send_b,
    third_t,
    active_ref,
    hidden_ref,
):
    step = pl.program_id(0)

    @pl.when(step == 0)
    def _():
        third_t[...] = third_ref[...].T
        out_ref[...] = jnp.zeros_like(out_ref)
        back_ref[...] = jnp.zeros_like(back_ref)

    win, wout = (gathered(win_ref), gathered(wout_ref))
    rows = third_ref.shape[0]
    lots = [slice(start, start + rows // 4) for start in range(0, rows, rows // 4)]

    def enter(lot):
        return (dot(third_ref[lot], win), dot(grad_ref[lot], wout, NT))

    def leave(lot, hidden, grad):
        mass, bell = gelu_terms(hidden)
        active = short(hidden * mass)
        grad = short((mass + hidden * bell) * wide(short(grad)))
        active_ref[lot] = active
        hidden_ref[lot] = grad
        out_ref[lot] += dot(active, wout)
        back_ref[lot] += dot(grad, win, NT)

    ready = enter(lots[0])
    for index, lot in enumerate(lots):
        following = enter(lots[index + 1]) if index + 1 < len(lots) else None
        leave(lot, *ready)
        ready = following
    grad_out = short(dot(active_ref[...], grad_ref[...], TN))
    grad_in = short(dot(third_t[...], hidden_ref[...]))
    turn = lax.rem(step, 4)
    side = pl.ds(pl.multiple_of(lax.rem(turn, 2) * TILE, TILE), TILE)
    pieces = shard_pieces(grad_in, turn // 2, slice(None), side)
    for owner in range(4):
        for y in range(2):
            for half in range(2):
                start = owner * 128 + y * 64 + 32 * half
                value = grad_out[start : start + 32]
                pieces.append((owner % 2, owner // 2, y, (turn, 2 + half), value))

    @pl.when(step < 4)
    def _():
        deal(place_ref, False, keep_a, send_a, pieces)

    @pl.when(step >= 4)
    def _():
        deal(place_ref, True, keep_b, send_b, pieces)


def feed(place, third, grad, weights):
    rows = third.shape[0]
    full = struct((rows, MODEL), jnp.float32)
    buffer = struct((2, 2, 4, 4, 32, MODEL), jnp.bfloat16)
    out, back, *lots = call(
        feed_kernel,
        (8,),
        [
            once((rows, MODEL), lambda t, place: (0, 0)),
            once((rows, MODEL), lambda t, place: (0, 0)),
            pl.BlockSpec((16, 64, TILE), lambda t, place: (0, t // 2, t % 2)),
            pl.BlockSpec((4, 128, MODEL), lambda t, place: (t % 4, 2 + t // 4, 0)),
        ],
        [once((rows, MODEL), lambda t, place: (0, 0))] * 2
        + [once(buffer.shape, lambda t, place: (0, 0, 0, 0, 0, 0))] * 4,
        [full, full] + [buffer] * 4,
        scratch=[
            pltpu.VMEM((MODEL, rows), jnp.bfloat16),
            pltpu.VMEM((rows, TILE), jnp.bfloat16),
            pltpu.VMEM((rows, TILE), jnp.bfloat16),
        ],
        prefetch=1,
    )(place, third, grad, weights, weights)
    return out, back, lots[:2], lots[2:]


def clear(*refs):
    @pl.when(pl.program_id(0) == 0)
    def _():
        for ref in refs:
            ref[...] = jnp.zeros_like(ref)


def add_product(total_ref, left, right):
    total_ref[...] += dot(left, right, TN)


def at_end(store):
    pl.when(pl.program_id(0) == pl.num_programs(0) - 1)(store)


def buffer_of(slots):
    return struct((2, 2, 4, slots, 32, MODEL), jnp.bfloat16)


def slots_at(slots):
    return once((2, 2, 4, slots, 32, MODEL), lambda *_: (0,) * 6)


def after_feed_kernel(
    held,
    place,
    after_ref,
    out_ref,
    back_ref,
    grad_ref,
    cross_ref,
    norm_ref,
    wo,
    own_ref,
    away_ref,
    total_ref,
    mixed_ref,
    sums_ref,
    keep_ref,
    send_ref,
    weight_ref,
):
    clear(sums_ref, weight_ref)
    after = after_ref[...]
    result = short(after + out_ref[...])
    store_found(held, after.shape[0], own_ref, away_ref, result)
    part = norm_back(after, back_ref[...], norm_ref, 2, sums_ref)
    total = wide(grad_ref[...]) + part
    total_ref[...] = total
    branch = short(total)
    mixed_ref[...] = short(dot(branch, gathered(wo), NT))
    add_product(weight_ref, cross_ref[...], branch)
    at_end(lambda: deal(place, False, keep_ref, send_ref, shard_pieces(weight_ref, 0)))


def after_feed(held, place, after, out, back, grad, mixed, norms, weights, width):
    narrow = struct(after.shape, jnp.bfloat16)
    full = struct(after.shape, jnp.float32)
    return call(
        after_feed_kernel,
        (after.shape[0] // width,),
        [by_rows(width)] * 5 + [norm_rows(), weight_at(7)],
        kept_or_sent(2 * width) + [by_rows(width)] * 2 + [sums_out()] + [slots_at(1)] * 2,
        [struct((2 * width, MODEL), jnp.bfloat16)] * 2
        + [full, narrow, struct((8, MODEL), jnp.float32)]
        + [buffer_of(1)] * 2,
        scratch=[pltpu.VMEM((MODEL, MODEL), jnp.float32)],
        prefetch=2,
    )(held, place, after, out, back, grad, mixed, norms, weights)


def middle_kernel(
    place,
    grad_ref,
    second_ref,
    after_ref,
    base_ref,
    self_ref,
    norm_ref,
    wq,
    wo,
    *refs,
):
    total_ref, mixed_ref, sums_ref, keep_ref, send_ref, weight_q, weight_o = refs
    clear(sums_ref, weight_q, weight_o)
    grad_q = grad_ref[...]
    grad = dot(grad_q, gathered(wq), NT)
    add_product(weight_q, second_ref[...], grad_q)
    total = base_ref[...] + norm_back(after_ref[...], grad, norm_ref, 1, sums_ref)
    total_ref[...] = total
    branch = short(total)
    mixed_ref[...] = short(dot(branch, gathered(wo), NT))
    add_product(weight_o, self_ref[...], branch)

    @at_end
    def _():
        deal(place, False, keep_ref, send_ref, shard_pieces(weight_q, 0))
        deal(place, False, keep_ref, send_ref, shard_pieces(weight_o, 1))


def middle(place, grad, second, after, base, mixed, norms, weights, width):
    narrow = struct(after.shape, jnp.bfloat16)
    return call(
        middle_kernel,
        (after.shape[0] // width,),
        [by_rows(width)] * 5 + [norm_rows(), weight_at(4), weight_at(3)],
        [by_rows(width)] * 2 + [sums_out()] + [slots_at(2)] * 2,
        [struct(after.shape, jnp.float32), narrow, struct((8, MODEL), jnp.float32)]
        + [buffer_of(2)] * 2,
        scratch=[pltpu.VMEM((MODEL, MODEL), jnp.float32)] * 2,
        prefetch=1,
    )(place, grad, second, after, base, mixed, norms, weights, weights)


def project_grad_kernel(place, left_ref, right_ref, keep_ref, send_ref, left_t):
    @pl.when(pl.program_id(1) == 0)
    def _():
        left_t[...] = left_ref[...].T

    product = dot(left_t[...], right_ref[0])
    deal(place, False, keep_ref, send_ref, shard_pieces(product, 0), own_y=False)


def project_grad(place, left, right):
    rows = left.shape[0]
    block = (2, 2, 4, 1, 32, MODEL)
    return call(
        project_grad_kernel,
        (1, 3),
        [
            pl.BlockSpec((rows, MODEL), lambda t, n, place: (0, t)),
            pl.BlockSpec((1, rows, MODEL), lambda t, n, place: (n, 0, 0)),
        ],
        [pl.BlockSpec(block, lambda t, n, place: (0, 0, t, n, 0, 0))] * 2,
        [buffer_of(3)] * 2,
        scratch=[pltpu.VMEM((MODEL, rows), jnp.bfloat16)],
        prefetch=1,
    )(place, left, right)


def finish_kernel(
    held, grads_ref, tokens_ref, base_ref, norm_ref, wq, wk, wv, own_ref, away_ref, sums_ref
):
    clear(sums_ref)
    grad = sum(dot(grads_ref[i], gathered(w), NT) for i, w in enumerate((wq, wk, wv)))
    part = norm_back(wide(tokens_ref[...]), grad, norm_ref, 0, sums_ref)
    result = short(base_ref[...] + part)
    store_found(held, result.shape[0], own_ref, away_ref, result)


def finish(held, grads, tokens, base, norms, weights, width):
    return call(
        finish_kernel,
        (base.shape[0] // width,),
        [
            pl.BlockSpec((3, width, MODEL), lambda i, *_: (0, i, 0)),
            found_rows(width),
            by_rows(width),
            norm_rows(),
        ]
        + [weight_at(i) for i in range(3)],
        kept_or_sent(2 * width) + [sums_out()],
        [struct((2 * width, MODEL), jnp.bfloat16)] * 2 + [struct((8, MODEL), jnp.float32)],
        prefetch=1,
    )(held, grads, tokens, base, norms, weights, weights, weights)


def source_back_kernel(
    place, grads_ref, source_ref, wk, wv, own_ref, away_ref, keep_ref, send_ref, weight_ref
):
    clear(weight_ref)
    source = source_ref[...].T
    for i in range(2):
        weight_ref[i] += dot(source, grads_ref[i])
    grad = dot(grads_ref[0], gathered(wk), NT) + dot(grads_ref[1], gathered(wv), NT)
    grad = short(grad)

    @pl.when(pl.program_id(0) == place[2])
    def _():
        own_ref[...] = grad

    @pl.when(pl.program_id(0) != place[2])
    def _():
        away_ref[...] = grad

    @at_end
    def _():
        for i in range(2):
            deal(place, False, keep_ref, send_ref, shard_pieces(weight_ref.at[i], i))


def source_back(place, grads, source, weights, width):
    rows = grads.shape[1]
    return call(
        source_back_kernel,
        (rows // width,),
        [
            pl.BlockSpec((2, width, MODEL), lambda i, *_: (0, i, 0)),
            by_rows(width),
            weight_at(5),
            weight_at(6),
        ],
        kept_or_sent(width) + [slots_at(2)] * 2,
        [struct((width, MODEL), jnp.bfloat16)] * 2 + [buffer_of(2)] * 2,
        scratch=[pltpu.VMEM((2, MODEL, MODEL), jnp.float32)],
        prefetch=1,
    )(place, grads, source, weights, weights)


def pairs(bit):
    return [(i, i ^ bit) for i in range(16)]


def swap(values):
    return lax.ppermute(values, "ctx", [(0, 1), (1, 0)])


def over_x(values):
    return lax.ppermute(values, "fsdp", pairs(2))


def over_core(values):
    return lax.ppermute(values, "fsdp", pairs(1))


def tie(*values):
    return lax.optimization_barrier(values)


def lot_specs(lot, first, second, spread, z_of, depth=1):
    specs = []
    for keep, _ in lot:
        slots, rows = keep.shape[3:5]
        block = (1, spread, depth, slots, rows, MODEL)
        specs += [
            pl.BlockSpec(block, lambda i, place: (first, second, z_of(i, place), 0, 0, 0))
        ] * 2
    return specs


def slots_of(lot):
    return sum(keep.shape[3] for keep, _ in lot)


def in_order(i, place):
    return i


def from_own(i, place):
    return lax.rem(place[3] + i, 4)


def pair_sums(refs, count):
    return [wide(refs[2 * i][...]) + wide(refs[2 * i + 1][...]) for i in range(count)]


def depth_of(lots):
    return 4 if sum(slots_of(lot) for lot in lots) < 4 else 1


def ranges(sizes):
    starts = [sum(sizes[:i]) for i in range(len(sizes))]
    return [(start, start + size) for start, size in zip(starts, sizes)]


def overlaps(sources, pieces):
    for i, (s0, s1) in enumerate(ranges(sources)):
        for j, (p0, p1) in enumerate(ranges(pieces)):
            low, high = (max(s0, p0), min(s1, p1))
            if low < high:
                yield i, j, slice(low - s0, high - s0), slice(low - p0, high - p0)


def sizes_of(lot):
    return [keep.shape[3] for keep, _ in lot]


def first_sums(place, lots, cuts=None):
    cuts = cuts or [[slots_of(lot)] for lot in lots]

    def kernel(place_ref, *refs):
        refs = list(refs)
        outs = refs[-sum(len(cut) for cut in cuts) :]
        for lot, cut in zip(lots, cuts):
            values = pair_sums([refs.pop(0) for _ in range(2 * len(lot))], len(lot))
            pieces, outs = (outs[: len(cut)], outs[len(cut) :])
            for i, j, taken, put in overlaps(sizes_of(lot), cut):
                pieces[j][:, :, put] = short(values[i][0, :, :, taken])

    depth = depth_of(lots)
    shapes = [(2, 4, size, 32, MODEL) for cut in cuts for size in cut]
    outs = call(
        kernel,
        (4 // depth,),
        [spec for lot in lots for spec in lot_specs(lot, 1, 0, 2, in_order, depth)],
        [
            pl.BlockSpec((2, depth) + shape[2:], lambda i, place: (0, i, 0, 0, 0))
            for shape in shapes
        ],
        [struct(shape, jnp.bfloat16) for shape in shapes],
        prefetch=1,
    )(place, *[array for lot in lots for pair in lot for array in pair])
    return [outs[start:end] for start, end in ranges([len(cut) for cut in cuts])]


def second_sums(place, lots, firsts, cuts=None):
    cuts = cuts or [[slots_of(lot)] for lot in lots]

    def kernel(place_ref, *refs):
        refs = list(refs)
        outs = refs[-sum(len(cut) for cut in cuts) :]
        for lot, first, cut in zip(lots, firsts, cuts):
            values = pair_sums([refs.pop(0) for _ in range(2 * len(lot))], len(lot))
            received = [wide(refs.pop(0)[0]) for _ in first]
            received = received[0] if len(first) == 1 else jnp.concatenate(received, axis=1)
            pieces, outs = (outs[: len(cut)], outs[len(cut) :])
            spots = ranges(sizes_of(lot))
            for i, j, taken, put in overlaps(sizes_of(lot), cut):
                there = received[:, spots[i][0] + taken.start : spots[i][0] + taken.stop]
                pieces[j][:, put] = short(values[i][0, 0, :, taken] + there)

    depth = depth_of(lots)
    specs, arrays = ([], [])
    for lot, first in zip(lots, firsts):
        specs += lot_specs(lot, 0, 1, 1, in_order, depth)
        specs += [
            pl.BlockSpec((1, depth) + piece.shape[2:], lambda i, place: (1, i, 0, 0, 0))
            for piece in first
        ]
        arrays += [array for pair in lot for array in pair] + list(first)
    shapes = [(4, size, 32, MODEL) for cut in cuts for size in cut]
    outs = call(
        kernel,
        (4 // depth,),
        specs,
        [pl.BlockSpec((depth,) + shape[1:], lambda i, place: (i, 0, 0, 0)) for shape in shapes],
        [struct(shape, jnp.bfloat16) for shape in shapes],
        prefetch=1,
    )(place, *arrays)
    return [outs[start:end] for start, end in ranges([len(cut) for cut in cuts])]


def third_sums(place, lots, firsts, seconds):
    def kernel(place_ref, *refs):
        refs = list(refs)
        out = refs[-1]
        start = 0
        for lot, first, second in zip(lots, firsts, seconds):
            values = pair_sums([refs.pop(0) for _ in range(2 * len(lot))], len(lot))
            parts_of = (
                [wide(refs.pop(0)[0, 0]) for _ in first],
                [wide(refs.pop(0)[0]) for _ in second],
            )
            received = sum(p[0] if len(p) == 1 else jnp.concatenate(p, axis=0) for p in parts_of)
            for value, (s0, s1) in zip(values, ranges(sizes_of(lot))):
                out[0, start + s0 : start + s1] = short(value[0, 0, 0] + received[s0:s1])
            start += slots_of(lot)

    specs, arrays = ([], [])
    for lot, first, second in zip(lots, firsts, seconds):
        specs += lot_specs(lot, 0, 0, 1, in_order)
        specs += [
            pl.BlockSpec((1, 1) + piece.shape[2:], lambda i, place: (0, i, 0, 0, 0))
            for piece in first
        ]
        specs += [
            pl.BlockSpec((1,) + piece.shape[1:], lambda i, place: (i, 0, 0, 0))
            for piece in second
        ]
        arrays += [array for pair in lot for array in pair] + list(first) + list(second)
    shape = (4, sum(slots_of(lot) for lot in lots), 32, MODEL)
    return call(
        kernel,
        (4,),
        specs,
        [pl.BlockSpec((1,) + shape[1:], lambda i, place: (i, 0, 0, 0))],
        [struct(shape, jnp.bfloat16)],
        prefetch=1,
    )(place, *arrays)[0]


def direct_sums(place, lot, first):
    (keep, core) = lot
    slots = keep.shape[3]

    def kernel(place_ref, keep_ref, core_ref, *refs):
        received = [wide(ref[...]) for ref in refs[:-1]]
        received = received[0] if len(first) == 1 else jnp.concatenate(received, axis=2)
        total = wide(keep_ref[0]) + wide(core_ref[0]) + received
        refs[-1][0] = short(total[:, 0])

    block = (1, 2, 1, slots, 32, MODEL)
    shape = (4, 2, slots, 32, MODEL)
    return call(
        kernel,
        (4,),
        [pl.BlockSpec(block, lambda i, place: (0, 0, i, 0, 0, 0))] * 2
        + [
            pl.BlockSpec((2, 1) + piece.shape[2:], lambda i, place: (0, i, 0, 0, 0))
            for piece in first
        ],
        [pl.BlockSpec((1,) + shape[1:], lambda i, place: (i, 0, 0, 0, 0))],
        [struct(shape, jnp.bfloat16)],
        prefetch=1,
    )(place, keep, core, *first)[0]


def over_z(values):
    groups = [[first + 4 * z for z in range(4)] for first in range(4)]
    return lax.psum_scatter(values, "fsdp", scatter_dimension=0, axis_index_groups=groups)


def both_parts(total, other):
    low = lax.axis_index("ctx") == 0
    return wide(jnp.stack([jnp.where(low, total, other), jnp.where(low, other, total)], axis=1))


def columns(shares, start, stop):
    part = shares[start:stop].reshape(stop - start, -1, MODEL)
    return jnp.concatenate(list(part), axis=1)


def feed_shares(lots):
    inner = [lot[:2].reshape(2, 64, 8, 128).transpose(1, 0, 2, 3).reshape(64, 16, 128) for lot in lots]
    inner = jnp.stack(inner, axis=2).reshape(64, 4 * MODEL)
    outer = [lot[2:].transpose(1, 0, 2, 3).reshape(128, MODEL) for lot in lots]
    return inner, jnp.concatenate(outer)


def whole_packs(mesh):
    return mesh.shape["ctx"] == 2 and mesh.shape["fsdp"] == 16


def whole_pack_body(
    tokens,
    encoded,
    cotangent,
    order,
    target_lengths,
    source_lengths,
    self_project,
    self_output,
    cross_query,
    cross_source,
    cross_output,
    feed_in,
    feed_out,
    norm_gain,
    norm_bias,
):
    rows = tokens.shape[2]
    pack_rows, source_rows = (2 * rows, 2 * encoded.shape[2])
    first_rows = 3 * pack_rows // 4
    width = rows // 2
    mine = lax.axis_index("ctx")
    spot = lax.axis_index("fsdp")
    z = spot // 4
    place = jnp.stack([spot % 2, spot // 2 % 2, mine, z]).astype(jnp.int32)
    part = self_project.shape[0]

    norms = jnp.pad(jnp.concatenate([norm_gain, norm_bias]), ((0, 10), (0, MODEL - part)))
    attention_shard, feed_shard = pack(
        (self_project, self_output, cross_query, cross_source, cross_output, feed_in, feed_out),
        norms,
    )
    weights = lax.all_gather(attention_shard, "fsdp", axis=0)
    norms = wide(weights[:, 8 * part : 8 * part + 8, :part])
    norms = norms.transpose(1, 0, 2).reshape(8, MODEL)

    def both_halves(array):
        own = lax.dynamic_index_in_dim(array, mine, 0, False)[0]
        return own, swap(lax.dynamic_index_in_dim(array, 1 - mine, 0, False)[0])

    places = lax.dynamic_index_in_dim(order, mine, 0, False)[0]
    holds = places[::width] // width
    found = jnp.argsort(holds).astype(jnp.int32)
    held = jnp.where(found // 2 == mine, found % 2, 2 + found % 2)

    def from_both(own, other):
        low = mine == 0
        return jnp.stack([jnp.where(low, own, other), jnp.where(low, other, own)])[:, None]

    halves = jnp.concatenate(both_halves(tokens))
    own, other = both_halves(encoded)
    source = jnp.concatenate([jnp.where(mine == 0, own, other), jnp.where(mine == 0, other, own)])
    lengths = lax.dynamic_index_in_dim(target_lengths, mine, 0, False)[0]
    target_docs = docs_of(jnp.arange(pack_rows, dtype=jnp.int32), lengths)
    lengths = lax.dynamic_index_in_dim(source_lengths, mine, 0, False)[0]
    source_docs = docs_of(jnp.arange(source_rows, dtype=jnp.int32), lengths)
    docs = lengths.shape[0]
    marks = query_marks(target_docs)
    target_marks = key_marks(target_docs, docs)
    source_marks = key_marks(source_docs, docs)
    cotangent_own, cotangent_away = (
        lax.dynamic_index_in_dim(cotangent, which, 0, False)[0] for which in (mine, 1 - mine)
    )
    tied = (feed_shard, halves, source, marks, target_marks, source_marks)
    feed_shard, halves, source, marks, target_marks, source_marks, *cotangents = tie(
        *tied, cotangent_own, cotangent_away
    )
    feed_weights = lax.all_gather(feed_shard, "fsdp", axis=0)

    reach = source_rows // 2

    first, query, keys, values = enter(held, halves, norms, weights, width)
    query, cotangents[1] = tie(query, cotangents[1])
    cotangents[1] = swap(cotangents[1])
    plan = self_plan(first_rows, pack_rows, width)
    self_mixed, self_extra = attend(plan, query, keys, values, marks, target_marks)
    self_mixed, source = tie(self_mixed, source)
    cross_keys, cross_values = source_pairs(source, weights, source_rows // 2)
    after_self, second, cross_queries = between(held, self_mixed, halves, norms, weights, width)
    plan = cross_plan(first_rows, pack_rows, reach, source_rows, width)
    cross_mixed, cross_extra = attend(
        plan, cross_queries, cross_keys, cross_values, marks, source_marks
    )
    after_cross, third, grad_out = before_feed(
        held, cross_mixed, after_self, *cotangents, norms, weights, width
    )

    out, back, lot_a, lot_b = feed(place, third, grad_out, feed_weights)
    lot_a, lot_b = ([(lot[0], over_core(lot[1]))] for lot in (lot_a, lot_b))
    result, result_away, grad_after_cross, grad_cross_mixed, sums_two, *part_out = after_feed(
        held, place, after_cross, out, back, grad_out, cross_mixed, norms, weights, width
    )
    (first_a,), (first_b,) = first_sums(place, [lot_a, lot_b])
    first_ab = (first_a, first_b)
    grad_cross_mixed, part_out[1], *first_ab = tie(grad_cross_mixed, part_out[1], *first_ab)
    first_ab = (over_x(first_ab[0]), swap(first_ab[1]))
    part_out[1] = over_core(part_out[1])
    plan = cross_plan(first_rows, pack_rows, reach, source_rows, width)
    grad_cross_queries, grad_source = attend_back(
        plan,
        cross_queries,
        cross_keys,
        cross_values,
        cross_extra,
        source_marks,
        cross_mixed,
        grad_cross_mixed,
        False,
    )
    grad_source, part_out[1], *first_ab = tie(grad_source, part_out[1], *first_ab)
    encoded_own, encoded_away, *part_source = source_back(
        place, grad_source, source, weights, source_rows // 2
    )
    first_ab = [[first] for first in first_ab]
    second_ab = [second for (second,) in second_sums(place, [lot_a, lot_b], first_ab)]
    grad_cross_queries, encoded_away, *second_ab = tie(
        grad_cross_queries, encoded_away, *second_ab
    )
    second_ab = (swap(second_ab[0]), over_x(second_ab[1]))
    grad_after_self, grad_self_mixed, sums_one, *part_middle = middle(
        place,
        grad_cross_queries,
        second,
        after_self,
        grad_after_cross,
        self_mixed,
        norms,
        weights,
        width,
    )
    grad_self_mixed, part_source[1], part_middle[1], *second_ab = tie(
        grad_self_mixed, part_source[1], part_middle[1], *second_ab
    )
    part_source[1], part_middle[1] = (over_core(part_source[1]), over_core(part_middle[1]))
    third_ab = third_sums(place, [lot_a, lot_b], first_ab, [[second] for second in second_ab])
    lot_c = [part_out, part_source, part_middle]
    ((first_c,),) = first_sums(place, [lot_c])
    grad_self_mixed, first_c, result_away, encoded_away, third_ab = tie(
        grad_self_mixed, first_c, result_away, encoded_away, third_ab
    )
    first_c = over_x(first_c)
    result_away, encoded_away = (swap(result_away), swap(encoded_away))
    total_ab = over_z(third_ab)
    plan = self_plan(first_rows, pack_rows, width)
    grads = attend_back(
        plan,
        query,
        keys,
        values,
        self_extra,
        target_marks,
        self_mixed,
        grad_self_mixed,
        True,
    )
    grads, first_c, result_away, encoded_away, total_ab = tie(
        grads, first_c, result_away, encoded_away, total_ab
    )
    (second_c,) = second_sums(place, [lot_c], [[first_c]], [[3, 2]])
    grads, total_ab, *second_c = tie(grads, total_ab, *second_c)
    second_c[0] = swap(second_c[0])
    lot_d = list(project_grad(place, first, grads))
    lot_d[1], total_ab, *second_c = tie(lot_d[1], total_ab, *second_c)
    second_c[1] = swap(second_c[1])
    lot_d = [(lot_d[0], over_core(lot_d[1]))]
    ((first_d,),) = first_sums(place, [lot_d])
    second_c[1], first_d = tie(second_c[1], first_d)
    third_c = third_sums(place, [lot_c], [[first_c]], [second_c])
    grads, third_c, total_ab, first_d = tie(grads, third_c, total_ab, first_d)
    total_c, other_ab = (over_z(third_c), swap(total_ab))
    first_d = over_x(first_d)
    tokens_own, tokens_away, sums_zero = finish(
        held, grads, halves, grad_after_self, norms, weights, width
    )
    tokens_own, sums_zero, other_ab, first_d = tie(tokens_own, sums_zero, other_ab, first_d)
    tokens_other = swap(tokens_away)
    third_d = direct_sums(place, lot_d[0], [first_d])
    sums_zero, other_ab, third_d, result, result_away, encoded_own, encoded_away = tie(
        sums_zero, other_ab, third_d, result, result_away, encoded_own, encoded_away
    )
    total_d = over_z(third_d)
    result = from_both(result, result_away)
    grad_encoded = from_both(encoded_own, encoded_away)
    sums = jnp.concatenate([sums_zero[:2], sums_one[:2], sums_two[:2]])
    for bit in (1, 2, 4, 8):
        sums = sums + lax.ppermute(sums, "fsdp", pairs(bit))
    sums = sums + swap(sums)
    share_ab = both_parts(total_ab, other_ab)
    feed_in_grad, feed_out_grad = feed_shares((share_ab[:4], share_ab[4:]))
    share_c = both_parts(total_c, swap(total_c))
    grad_tokens = from_both(tokens_own, tokens_other)
    tied = (sums, result, grad_encoded, grad_tokens, feed_in_grad, feed_out_grad, share_c, total_d)
    sums, result, grad_encoded, grad_tokens, feed_in_grad, feed_out_grad, share_c, total_d = tie(
        *tied
    )
    share_d = (wide(total_d) + wide(swap(total_d))).transpose(1, 0, 2, 3)

    sums = lax.dynamic_slice_in_dim(sums, spot * part, part, 1)

    return (
        result,
        grad_tokens,
        grad_encoded,
        columns(share_d, 0, 3),
        columns(share_c, 4, 5),
        columns(share_c, 3, 4),
        columns(share_c, 1, 3),
        columns(share_c, 0, 1),
        feed_in_grad,
        feed_out_grad,
        sums[0::2],
        sums[1:4:2],
        sums[5],
    )


def solution(mesh):
    chosen = whole_pack_body if whole_packs(mesh) else body
    return jax.shard_map(
        chosen,
        mesh=mesh,
        in_specs=(
            P(None, "fsdp", "ctx", None),
            P(None, "fsdp", "ctx", None),
            P(None, "fsdp", "ctx", None),
            P(None, "fsdp", None),
            P(None, "fsdp", None),
            P(None, "fsdp", None),
            P("fsdp", None),
            P("fsdp", None),
            P("fsdp", None),
            P("fsdp", None),
            P("fsdp", None),
            P("fsdp", None),
            P("fsdp", None),
            P(None, "fsdp"),
            P(None, "fsdp"),
        ),
        out_specs=(
            P(None, "fsdp", "ctx", None),
            P(None, "fsdp", "ctx", None),
            P(None, "fsdp", "ctx", None),
            P("fsdp", None),
            P("fsdp", None),
            P("fsdp", None),
            P("fsdp", None),
            P("fsdp", None),
            P("fsdp", None),
            P("fsdp", None),
            P(None, "fsdp"),
            P(None, "fsdp"),
            P("fsdp"),
        ),
        check_vma=False,
    )
```
